32 devices in a mesh: dp: 4 (over y, core), tensor: 8 (over z, x).
Axes of the slice: x: 2, y: 2, z: 4, core: 2. Of those that a mesh axis runs over, the one named last changes fastest.
Arguments:
- tokens: bfloat16 [512, 4096], P(('dp', 'tensor'))
- ln1_gain: float32 [4096], replicated, may hold values from 0.1 to 1.9
- ln1_bias: float32 [4096], replicated, may hold values from -3 to 3
- qkv_weight: bfloat16 [4096, 12288], P(None, 'tensor')
- out_weight: bfloat16 [4096, 4096], P(None, 'tensor'), may hold values from -0.09375 to 0.09375
- layer_scale: float32 [4096], replicated, may hold values from 0.3 to 1.5
- segment_ids: int32 [512], P('dp'), may hold values from 0 to 3, as said below
- positions: int32 [512, 2], P('dp'), may hold values from 0 to 23, as said below
- merge_index: int32 [128, 4], P('dp'), may hold values from 0 to 127, as said below
- merge_weight: bfloat16 [16384, 4096], P('dp', 'tensor'), may hold values from -0.046875 to 0.046875
- owners: int32 [128, 1], P('dp'), may hold values from 0 to 3; in each aligned block of 32 rows (0 to 31, 32 to 63, ...) at most 16 rows name the same one
- ln2_gain: float32 [4096], P('tensor'), may hold values from 0.1 to 1.9
- ln2_bias: float32 [4096], P('tensor'), may hold values from -3 to 3
Outputs:
- hidden: bfloat16 [512, 4096], P(('dp', 'tensor'))
- routed: bfloat16 [256, 4096], P('dp', 'tensor')
The draws below stay inside these ranges and needn't reach their ends.
Inputs may be any that keep to these rules, and one draw needn't show every extreme that they name: `segment_ids`: within a group ids never fall; the last 32 tokens of every group are one image of 16 columns. `positions`: rows and columns of patches inside each image, in row-major order starting at 0 where the image starts; each image's width is 4, 8 or 16 and it covers whole aligned blocks of 32 tokens; in group 0 all tokens before the last 32 form one image of width 4. `merge_index`: merged rows run over the aligned blocks of 32 tokens in order, 8 a block; each names the 2x2 patches (2p, 2q), (2p, 2q + 1), (2p + 1, 2q), (2p + 1, 2q + 1) of one image inside its block, in row-major order of (p, q). `owners`: in each group's 32 merged rows no owner is named more than 16 times.
All inputs are finite; a program needn't handle non-finite values.
Results may differ from the reference program's by a relative error of at most 0.012.
Values may be sent and summed in bfloat16 or wider, within the bound.
No kernel may reach another device: no remote copies, remote signals or barrier semaphores. Data moves between devices by JAX's collectives and lax.ppermute only.
A program may use at most 128 MiB of HBM per device.

```python
import math
import jax
import jax.numpy as jnp
import numpy as np
from jax import lax

D = 4096
HEADS = 32
HD = 128
TOKS = 128
TOKENS = 512
MERGED_G = 32
MERGED = 128
CAP = 16
N_DP = 4


def pack_layout(key):
    base = jax.random.fold_in(key, 7)
    slot_total = TOKENS // 32
    per_group = TOKS // 32
    index_list = jnp.arange(slot_total, dtype=jnp.int32)
    local = index_list % per_group
    group = index_list // per_group
    coin = jax.random.randint(jax.random.fold_in(base, 1), (slot_total,), 0, 2, dtype=jnp.int32)
    boundary = (local == 0) | (local == per_group - 1)
    coin = jnp.where(boundary, 1, coin)
    coin = jnp.where((group == 0) & jnp.logical_not(boundary), 0, coin)
    width_code = jax.random.randint(jax.random.fold_in(base, 2), (slot_total,), 0, 3, dtype=jnp.int32)
    width_code = jnp.where((group == 0) & (local == 0), 0, width_code)
    width_code = jnp.where(local == per_group - 1, 2, width_code)
    begin = lax.cummax(jnp.where(coin == 1, index_list, 0), axis=0)
    widths = jnp.left_shift(jnp.int32(4), jnp.take(width_code, begin))
    return (begin, widths, per_group)


def draw_segment_ids(key, part):
    begin, widths, per_group = pack_layout(key)
    token_slot = jnp.arange(TOKENS, dtype=jnp.int32) // 32
    start_slot = jnp.take(begin, token_slot)
    return (start_slot - token_slot // per_group * per_group).astype(jnp.int32)


def draw_positions(key, part):
    begin, widths, per_group = pack_layout(key)
    token_index = jnp.arange(TOKENS, dtype=jnp.int32)
    token_slot = token_index // 32
    offset = token_index - jnp.take(begin, token_slot) * 32
    width_here = jnp.take(widths, token_slot)
    return jnp.stack([offset // width_here, offset % width_here], axis=1).astype(jnp.int32)


def draw_merge_index(key, part):
    begin, widths, per_group = pack_layout(key)
    merged_index = jnp.arange(MERGED, dtype=jnp.int32)
    slot = merged_index // 8
    inner = merged_index % 8
    width_here = jnp.take(widths, slot)
    half_width = width_here // 2
    pair_row = inner // half_width
    pair_col = inner % half_width
    first = slot % per_group * 32 + 2 * pair_row * width_here + 2 * pair_col
    return jnp.stack([first, first + 1, first + width_here, first + width_here + 1], axis=1).astype(jnp.int32)


def draw_tokens(key, part):
    noise = jax.random.normal(jax.random.fold_in(key, 1), (TOKENS, D), jnp.float32)
    return noise.astype(jnp.bfloat16)


def draw_qkv_weight(key, part):
    columns = HEADS * 3 * HD
    weights = jax.random.normal(jax.random.fold_in(key, 3), (D, columns), jnp.float32) * D ** (-0.5)
    return weights.astype(jnp.bfloat16)


def level_of(stream_key, shape, shards, smallest, largest):
    level = 1.0
    for position, shards_of in shards:
        steps = jax.random.uniform(jax.random.fold_in(jax.random.fold_in(stream_key, 6), position), (shards_of,), jnp.float32, smallest / len(shards), largest / len(shards))
        level = level * jnp.repeat(jnp.exp(steps), shape[position] // shards_of).reshape((-1,) + (1,) * (len(shape) - 1 - position))
    return level


def deal_out(rng, own, number, rows, count, top, limit, skew):
    order = jax.random.permutation(rng, count)
    crowded, usual = shares(count, rows * top, limit, skew, True), shares(count, rows * top, limit, skew, False)
    places = jnp.arange(count)

    def named(tallies, rotation):
        used = int((tallies > 0).sum())
        fixed = max(1, used // 4)
        passed = fixed + (places - fixed + rotation * (used - fixed)) % max(1, count - fixed)
        return jnp.zeros((count,), jnp.int32).at[order[jnp.where(places < fixed, places, passed)]].set(jnp.asarray(tallies, jnp.int32))

    tallies = jnp.where(number % 4 == 0, named(crowded, number // 4), named(usual, number - number // 4 - 1))
    mixed = jax.random.permutation(jax.random.fold_in(own, 3), count)
    source_of, receiver = mixed[0:count // 2 * 2:2], mixed[1:count // 2 * 2:2]
    slack = jnp.minimum(tallies[source_of] - 1, limit - tallies[receiver]) // 2
    slack = jnp.where((source_of == order[0]) | (receiver == order[0]) | (tallies[receiver] == 0), 0, jnp.maximum(slack, 0))
    passed = jax.random.randint(jax.random.fold_in(own, 4), (count // 2,), 0, 1 << 20) % (slack + 1)
    tallies = tallies.at[source_of].add(-passed).at[receiver].add(passed)
    items = jnp.searchsorted(jnp.cumsum(tallies), jnp.arange(rows * top), side="right").astype(jnp.int32)
    grid = items.reshape(top, rows).T
    grid = grid[jax.random.permutation(jax.random.fold_in(own, 1), rows)]
    rotation = jax.random.randint(jax.random.fold_in(own, 2), (rows, 1), 0, top)
    return jnp.take_along_axis(grid, (jnp.arange(top)[None, :] + rotation) % top, axis=1)


def shares(count, total, bound, slope, full):
    weights = [(1 << 20) // math.isqrt(standing ** slope) + 1 for standing in range(1, count + 1)]
    largest = bound if full else min(bound, max(-(-total // count), total * weights[0] // sum(weights)))
    least = 1 if total - largest >= count - 1 else 0
    holding, rest = [largest] + [least] * (count - 1), total - largest - least * (count - 1)
    while rest > 0:
        movable = [i for i in range(1, count) if holding[i] < largest] or [i for i in range(1, count) if holding[i] < bound]
        mass, budget = sum([weights[i] for i in movable]), rest
        for i in movable:
            addition = min(bound - holding[i], max(1, budget * weights[i] // mass), rest)
            holding[i] = holding[i] + addition
            rest = rest - addition
    return np.array(holding)


def bell_draw(rng, extent, scale, most, split=(), held_as=jnp.bfloat16):
    drawn = scale * jax.random.normal(rng, extent, jnp.float32)
    if split:
        drawn = drawn * level_of(rng, extent, split, -0.22, 0.18)
    return jnp.clip(drawn, -most, most).astype(held_as)


def setup_inputs(seed: int = 0) -> dict:
    splits = jax.random.split(jax.random.key(seed), 14)
    tokens = draw_tokens(jax.random.fold_in(splits[13], 71), 0)
    ln1_gain = jnp.clip(1.0 + 0.18 * jax.random.normal(splits[1], (D,), jnp.float32), 0.1, 1.9)
    ln1_bias = bell_draw(splits[2], (D,), 0.5, 3.0, (), jnp.float32)
    qkv_weight = draw_qkv_weight(jax.random.fold_in(splits[13], 71), 0)
    out_weight = bell_draw(splits[4], (HEADS * HD, D), (HEADS * HD) ** -0.5, 0.09375, ((1, 8),))
    layer_scale = jnp.clip(jnp.exp(jax.random.uniform(splits[5], (D,), jnp.float32, math.log(0.3), math.log(1.5))), 0.3, 1.5)
    segment_ids = draw_segment_ids(jax.random.fold_in(splits[13], 71), 0)
    positions = draw_positions(jax.random.fold_in(splits[13], 71), 0)
    merge_index = draw_merge_index(jax.random.fold_in(splits[13], 71), 0)
    merge_weight = bell_draw(splits[9], (4 * D, D), (4 * D) ** -0.5, 0.046875, ((0, 4), (1, 8)))
    owners_keys = jax.random.split(jax.random.fold_in(splits[10], 1), MERGED // MERGED_G)
    owners_turns = jax.random.permutation(jax.random.fold_in(splits[10], 3), MERGED // MERGED_G)
    owners = jax.vmap(lambda own, number: deal_out(jax.random.fold_in(splits[10], 2), own, number, MERGED_G, N_DP, 1, CAP, 2))(owners_keys, owners_turns).reshape((MERGED, 1))
    ln2_gain = jnp.clip(1.0 + 0.18 * jax.random.normal(splits[11], (D,), jnp.float32), 0.1, 1.9)
    ln2_bias = bell_draw(splits[12], (D,), 0.5, 3.0, ((0, 8),), jnp.float32)
    return dict(tokens=tokens, ln1_gain=ln1_gain, ln1_bias=ln1_bias, qkv_weight=qkv_weight, out_weight=out_weight, layer_scale=layer_scale, segment_ids=segment_ids, positions=positions, merge_index=merge_index, merge_weight=merge_weight, owners=owners, ln2_gain=ln2_gain, ln2_bias=ln2_bias)


def layer_norm(values, gain, bias):
    center = values - lax.optimization_barrier(jnp.mean(values, axis=-1, keepdims=True))
    spread = lax.optimization_barrier(jnp.mean(center * center, axis=-1, keepdims=True))
    return center * lax.rsqrt(spread + 1e-06) * gain + bias

def rotate(tensor, rows, columns):
    quarter = tensor.shape[-1] // 4
    index_list = jnp.arange(quarter, dtype=jnp.float32)
    frequency = jnp.exp(index_list * (-math.log(100.0) / quarter))
    pieces = []
    for half_index, coordinate in ((0, rows), (1, columns)):
        section = tensor[..., half_index * 2 * quarter:(half_index + 1) * 2 * quarter]
        angles = coordinate[:, None] * frequency[None, :]
        cosine = jnp.cos(angles)[:, None, :]
        sine = jnp.sin(angles)[:, None, :]
        first_part = section[..., :quarter]
        second_part = section[..., quarter:]
        pieces.append(first_part * cosine - second_part * sine)
        pieces.append(second_part * cosine + first_part * sine)
    return jnp.concatenate(pieces, axis=-1)

def attend(queries, keys_rot, values_in, segments):
    scale_factor = 1.0 / math.sqrt(queries.shape[-1])
    scores = jnp.einsum('shd,thd->hst', queries.astype(jnp.float32), keys_rot.astype(jnp.float32)) * scale_factor
    same = segments[:, None] == segments[None, :]
    scores = jnp.where(same[None], scores, -jnp.inf)
    peak = lax.optimization_barrier(jnp.max(scores, axis=-1, keepdims=True))
    weights = jnp.exp(scores - peak)
    probs = (weights / lax.optimization_barrier(jnp.sum(weights, axis=-1, keepdims=True))).astype(jnp.bfloat16)
    mixed = jnp.einsum('hst,thd->shd', probs.astype(jnp.float32), values_in.astype(jnp.float32))
    return mixed.astype(jnp.bfloat16)

def finish_norm(values, row_total, row_squares, gain, bias):
    mean_row = row_total / D
    var_row = row_squares / D - mean_row * mean_row
    return (values - mean_row[:, None]) * lax.rsqrt(var_row[:, None] + 1e-06) * gain + bias

def reference(tokens, ln1_gain, ln1_bias, qkv_weight, out_weight, layer_scale, segment_ids, positions, merge_index, merge_weight, owners, ln2_gain, ln2_bias):

    def one_group(items):
        group_tokens, segments, places, picks = items
        count = group_tokens.shape[0]
        normed = layer_norm(group_tokens.astype(jnp.float32), ln1_gain, ln1_bias).astype(jnp.bfloat16)
        packed = jnp.dot(normed, qkv_weight, preferred_element_type=jnp.float32).reshape(count, HEADS, 3, HD)
        rows = places[:, 0].astype(jnp.float32)
        columns = places[:, 1].astype(jnp.float32)
        queries = rotate(packed[:, :, 0], rows, columns).astype(jnp.bfloat16)
        keys_rot = rotate(packed[:, :, 1], rows, columns).astype(jnp.bfloat16)
        values_in = packed[:, :, 2].astype(jnp.bfloat16)
        attended = attend(queries, keys_rot, values_in, segments).reshape(count, HEADS * HD)
        projected = jnp.dot(attended, out_weight, preferred_element_type=jnp.float32).astype(jnp.bfloat16)
        hidden = (group_tokens.astype(jnp.float32) + layer_scale * projected.astype(jnp.float32)).astype(jnp.bfloat16)
        merged = jnp.take(hidden, picks.reshape(-1), axis=0).reshape(MERGED_G, 4 * D)
        reduced = jnp.dot(merged, merge_weight, preferred_element_type=jnp.float32).astype(jnp.bfloat16)
        return (hidden, reduced)
    hidden, reduced = lax.map(one_group, (tokens.reshape(N_DP, TOKS, D), segment_ids.reshape(N_DP, TOKS), positions.reshape(N_DP, TOKS, 2), merge_index.reshape(N_DP, MERGED_G, 4)))
    owner_of = owners[:, 0].reshape(N_DP, MERGED_G)

    def slots_of(owner_row):
        one_hot = (owner_row[:, None] == jnp.arange(N_DP, dtype=jnp.int32)[None, :]).astype(jnp.int32)
        before = jnp.cumsum(one_hot, axis=0) - one_hot
        return lax.optimization_barrier(jnp.sum(before * one_hot, axis=1))
    slot_of = jax.vmap(slots_of)(owner_of)
    group_of = jnp.arange(N_DP, dtype=jnp.int32)[:, None]
    target = ((owner_of * N_DP + group_of) * CAP + slot_of).reshape(-1).astype(jnp.int32)
    rows_at = jnp.zeros((N_DP * N_DP * CAP, D), jnp.float32).at[target].set(reduced.reshape(MERGED, D).astype(jnp.float32))
    filled = jnp.zeros((N_DP * N_DP * CAP,), jnp.float32).at[target].set(1.0)
    row_total = lax.optimization_barrier(jnp.sum(rows_at, axis=1))
    row_squares = lax.optimization_barrier(jnp.sum(rows_at * rows_at, axis=1))
    routed = (finish_norm(rows_at, row_total, row_squares, ln2_gain, ln2_bias) * filled[:, None]).astype(jnp.bfloat16)
    return (hidden.reshape(TOKENS, D), routed)
```

```python
import math

import jax
import jax.numpy as jnp
from jax import lax
from jax.sharding import PartitionSpec as P

D = 4096
HD = 128


def layer_norm(values, gain, bias):
    center = values - jnp.mean(values, axis=-1, keepdims=True)
    spread = jnp.mean(center * center, axis=-1, keepdims=True)
    return center * lax.rsqrt(spread + 1e-06) * gain + bias


def rotate(tensor, rows, columns):
    quarter = tensor.shape[-1] // 4
    index_list = jnp.arange(quarter, dtype=jnp.float32)
    frequency = jnp.exp(index_list * (-math.log(100.0) / quarter))
    pieces = []
    for half_index, coordinate in ((0, rows), (1, columns)):
        section = tensor[..., half_index * 2 * quarter : (half_index + 1) * 2 * quarter]
        angles = coordinate[:, None] * frequency[None, :]
        cosine = jnp.cos(angles)[:, None, :]
        sine = jnp.sin(angles)[:, None, :]
        first_part = section[..., :quarter]
        second_part = section[..., quarter:]
        pieces.append(first_part * cosine - second_part * sine)
        pieces.append(second_part * cosine + first_part * sine)
    return jnp.concatenate(pieces, axis=-1)


def attend(queries, keys_rot, values_in, segments):
    scale_factor = 1.0 / math.sqrt(queries.shape[-1])
    scores = (
        jnp.einsum("shd,thd->hst", queries, keys_rot, preferred_element_type=jnp.float32)
        * scale_factor
    )
    same = segments[:, None] == segments[None, :]
    scores = jnp.where(same[None], scores, -jnp.inf)
    peak = jnp.max(scores, axis=-1, keepdims=True)
    weights = jnp.exp(scores - peak)
    probs = (weights / jnp.sum(weights, axis=-1, keepdims=True)).astype(jnp.bfloat16)
    mixed = jnp.einsum("hst,thd->shd", probs, values_in, preferred_element_type=jnp.float32)
    return mixed.astype(jnp.bfloat16)


def finish_norm(values, row_total, row_squares, gain, bias):
    mean_row = row_total / D
    var_row = row_squares / D - mean_row * mean_row
    return (values - mean_row[:, None]) * lax.rsqrt(var_row[:, None] + 1e-06) * gain + bias


def row_stats(values):
    return (jnp.sum(values, axis=1), jnp.sum(values * values, axis=1))


def swap(block, axis, bit):
    count = lax.axis_size(axis)
    return lax.ppermute(block, axis, [(i, i ^ bit) for i in range(count)])


def gather_blocks(block, axis):
    count = lax.axis_size(axis)
    blocks = {0: block}
    bit = count // 2
    while bit:
        blocks.update({index ^ bit: swap(held, axis, bit) for index, held in sorted(blocks.items())})
        bit //= 2
    return [blocks[index] for index in range(count)]


def contract_blocks(blocks, weight, place):
    depth = blocks[0].shape[1]
    total = None
    for index, block in enumerate(blocks):
        rows = lax.dynamic_slice_in_dim(weight, (place ^ index) * depth, depth, axis=0)
        term = jnp.dot(block, rows, preferred_element_type=jnp.float32)
        total = term if total is None else total + term
    return total


def slots_of(owner_of, group_count):
    one_hot = (owner_of[:, None] == jnp.arange(group_count, dtype=jnp.int32)[None, :]).astype(
        jnp.int32
    )
    before = jnp.cumsum(one_hot, axis=0) - one_hot
    return jnp.sum(before * one_hot, axis=1)


def on_device(
    tokens,
    ln1_gain,
    ln1_bias,
    qkv_weight,
    out_weight,
    layer_scale,
    segment_ids,
    positions,
    merge_index,
    merge_weight,
    owners,
    ln2_gain,
    ln2_bias,
):
    tok_count = tokens.shape[0]
    tensor_count = lax.axis_size("tensor")
    group_count = lax.axis_size("dp")
    place = lax.axis_index("tensor")
    seq_count = tok_count * tensor_count
    head_count = qkv_weight.shape[1] // (3 * HD)
    width = out_weight.shape[1]
    merged_count = merge_index.shape[0]
    slots_cap = 2 * merged_count // group_count

    stacked = jnp.stack(gather_blocks(tokens, "tensor"))
    order = jnp.arange(tensor_count, dtype=jnp.int32) ^ place
    all_tokens = jnp.take(stacked, order, axis=0).reshape(seq_count, D)
    normed = layer_norm(all_tokens.astype(jnp.float32), ln1_gain, ln1_bias).astype(jnp.bfloat16)
    packed = jnp.dot(normed, qkv_weight, preferred_element_type=jnp.float32)
    packed = packed.reshape(seq_count, head_count, 3, HD)
    rows = positions[:, 0].astype(jnp.float32)
    columns = positions[:, 1].astype(jnp.float32)
    queries = rotate(packed[:, :, 0], rows, columns).astype(jnp.bfloat16)
    keys_rot = rotate(packed[:, :, 1], rows, columns).astype(jnp.bfloat16)
    values_in = packed[:, :, 2].astype(jnp.bfloat16)
    attended = attend(queries, keys_rot, values_in, segment_ids).reshape(seq_count, head_count * HD)

    projected = contract_blocks(gather_blocks(attended, "tensor"), out_weight, place)
    projected = projected.astype(jnp.bfloat16)
    own_tokens = lax.dynamic_slice_in_dim(all_tokens, place * width, width, axis=1)
    own_scale = lax.dynamic_slice_in_dim(layer_scale, place * width, width, axis=0)
    hidden_columns = (
        own_tokens.astype(jnp.float32) + own_scale * projected.astype(jnp.float32)
    ).astype(jnp.bfloat16)
    hidden = lax.all_to_all(hidden_columns, "tensor", split_axis=0, concat_axis=1, tiled=True)

    if merge_weight.shape[0] == D:
        picked = jnp.take(hidden_columns, merge_index.T.reshape(-1), axis=0)
        arrived_rows = lax.all_to_all(picked, "dp", split_axis=0, concat_axis=0, tiled=True)
        partial = contract_blocks(gather_blocks(arrived_rows, "tensor"), merge_weight, place)
        partial = partial.astype(jnp.bfloat16)
        owner_all = lax.all_gather(owners[:, 0], "dp", axis=0)
        slot_all = jax.vmap(lambda owner_of: slots_of(owner_of, group_count))(owner_all)
        group_all = jnp.arange(group_count, dtype=jnp.int32)[:, None]
        target = ((owner_all * group_count + group_all) * slots_cap + slot_all).reshape(-1)
        slot_total = group_count * group_count * slots_cap
        placing = (
            jnp.arange(slot_total, dtype=jnp.int32)[:, None] == target[None, :]
        ).astype(jnp.bfloat16)
        outgoing = jnp.dot(placing, partial, preferred_element_type=jnp.float32).astype(jnp.bfloat16)
        incoming = lax.all_to_all(
            outgoing.reshape(group_count, group_count * slots_cap, width),
            "dp", split_axis=0, concat_axis=0, tiled=True,
        )
        received = jnp.sum(incoming.astype(jnp.float32), axis=0).astype(jnp.bfloat16)
        marks = jnp.sum(placing.astype(jnp.float32), axis=1).reshape(group_count, -1)
        arrived = lax.dynamic_index_in_dim(marks, lax.axis_index("dp"), axis=0, keepdims=False)
    else:
        all_hidden = lax.all_gather(hidden, "tensor", axis=0, tiled=True)
        merged = jnp.take(all_hidden, merge_index.reshape(-1), axis=0).reshape(merged_count, 4 * D)
        reduced = jnp.dot(
            merged,
            lax.all_gather(merge_weight, "dp", axis=0, tiled=True),
            preferred_element_type=jnp.float32,
        ).astype(jnp.bfloat16)
        target = owners[:, 0] * slots_cap + slots_of(owners[:, 0], group_count)
        placing = (
            jnp.arange(group_count * slots_cap, dtype=jnp.int32)[:, None] == target[None, :]
        ).astype(jnp.bfloat16)
        outgoing = jnp.dot(placing, reduced, preferred_element_type=jnp.float32).astype(jnp.bfloat16)
        marks = jnp.sum(placing.astype(jnp.float32), axis=1).astype(jnp.bfloat16)
        received, arrived = (
            lax.all_to_all(outgoing, "dp", split_axis=0, concat_axis=0, tiled=True),
            lax.all_to_all(marks, "dp", split_axis=0, concat_axis=0, tiled=True),
        )
    received = received.astype(jnp.float32)
    stats = jnp.concatenate(row_stats(received))[None]
    stats = jnp.broadcast_to(stats, (tensor_count, stats.shape[1]))
    stats = jnp.sum(lax.all_to_all(stats, "tensor", split_axis=0, concat_axis=0, tiled=True), axis=0)
    row_total, row_squares = jnp.split(stats, 2)
    routed = (
        finish_norm(received, row_total, row_squares, ln2_gain, ln2_bias)
        * arrived.astype(jnp.float32)[:, None]
    ).astype(jnp.bfloat16)
    return (hidden, routed)


def solution(mesh):
    in_specs = (
        P(("dp", "tensor"), None),
        P(),
        P(),
        P(None, "tensor"),
        P(None, "tensor"),
        P(),
        P("dp"),
        P("dp", None),
        P("dp", None),
        P("dp", "tensor"),
        P("dp", None),
        P("tensor"),
        P("tensor"),
    )
    out_specs = (P(("dp", "tensor"), None), P("dp", "tensor"))
    return jax.shard_map(
        on_device, mesh=mesh, in_specs=in_specs, out_specs=out_specs, check_vma=False
    )
```

```python
import functools
import math

import jax
import jax.numpy as jnp
from jax import lax
from jax.experimental import pallas as pl
from jax.experimental.pallas import tpu as pltpu
from jax.sharding import PartitionSpec as P

D = 4096
HD = 128


def swap(block, axis, bit):
    count = lax.axis_size(axis)
    return lax.ppermute(block, axis, [(i, i ^ bit) for i in range(count)])


def gather_blocks(block, axis):
    count = lax.axis_size(axis)
    blocks = {0: block}
    bit = count // 2
    while bit:
        blocks.update({index ^ bit: swap(held, axis, bit) for index, held in sorted(blocks.items())})
        bit //= 2
    return [blocks[index] for index in range(count)]


def slots_of(owner_of, group_count):
    one_hot = (owner_of[:, None] == jnp.arange(group_count, dtype=jnp.int32)[None, :]).astype(
        jnp.int32
    )
    before = jnp.cumsum(one_hot, axis=0) - one_hot
    return jnp.sum(before * one_hot, axis=1)


VMEM = pl.BlockSpec(memory_space=pltpu.VMEM)
SMEM = pl.BlockSpec(memory_space=pltpu.SMEM)


def rotary_tables(positions):
    quarter = HD // 4
    frequency = jnp.exp(jnp.arange(quarter, dtype=jnp.float32) * (-math.log(100.0) / quarter))
    angles = positions.astype(jnp.float32)[:, :, None] * frequency
    cosine, sine = jnp.cos(angles), jnp.sin(angles)
    cosine = jnp.stack([cosine, cosine], axis=2).reshape(-1, HD)
    sine = jnp.stack([-sine, sine], axis=2).reshape(-1, HD)
    return cosine, sine


def attention_kernel(tensor_count, place_ref, *refs):
    blocks = refs[:tensor_count]
    gain, bias, weight, cosine, sine, seg_col, seg_row, out, normed = refs[tensor_count:]
    place = place_ref[0]
    rows = blocks[0].shape[0]
    for index, block in enumerate(blocks):
        values = block[...].astype(jnp.float32)
        center = values - jnp.mean(values, axis=-1, keepdims=True)
        spread = jnp.mean(center * center, axis=-1, keepdims=True)
        value = center * lax.rsqrt(spread + 1e-06) * gain[...] + bias[...]
        at = pl.multiple_of((place ^ index) * rows, rows)
        normed[pl.ds(at, rows), :] = value.astype(jnp.bfloat16)
    same = seg_col[...] == seg_row[...]
    low = (lax.broadcasted_iota(jnp.int32, cosine.shape, 1) & (HD // 4)) == 0
    for head in range(out.shape[1] // HD):
        first = head * 3 * HD
        packed = jnp.dot(
            normed[...], weight[:, first : first + 3 * HD], preferred_element_type=jnp.float32
        )

        def rotated(part):
            swapped = jnp.where(
                low, pltpu.roll(part, HD - HD // 4, 1), pltpu.roll(part, HD // 4, 1)
            )
            return (part * cosine[...] + swapped * sine[...]).astype(jnp.bfloat16)

        queries, keys = rotated(packed[:, :HD]), rotated(packed[:, HD : 2 * HD])
        values = packed[:, 2 * HD :].astype(jnp.bfloat16)
        scores = lax.dot_general(
            queries, keys, (((1,), (1,)), ((), ())), preferred_element_type=jnp.float32
        ) * (1.0 / math.sqrt(HD))
        scores = jnp.where(same, scores, -jnp.inf)
        weights = jnp.exp(scores - jnp.max(scores, axis=-1, keepdims=True))
        probs = (weights / jnp.sum(weights, axis=-1, keepdims=True)).astype(jnp.bfloat16)
        mixed = jnp.dot(probs, values, preferred_element_type=jnp.float32)
        out[:, head * HD : (head + 1) * HD] = mixed.astype(jnp.bfloat16)


def attention(place, blocks, gain, bias, weight, positions, segments):
    seq = blocks[0].shape[0] * len(blocks)
    cosine, sine = rotary_tables(positions)
    width = weight.shape[1] // 3
    return pl.pallas_call(
        functools.partial(attention_kernel, len(blocks)),
        out_shape=jax.ShapeDtypeStruct((seq, width), jnp.bfloat16),
        in_specs=[SMEM] + [VMEM] * (len(blocks) + 7),
        out_specs=VMEM,
        scratch_shapes=[pltpu.VMEM((seq, D), jnp.bfloat16)],
        compiler_params=pltpu.CompilerParams(vmem_limit_bytes=40 * 2**20),
        cost_estimate=pl.CostEstimate(
            flops=2 * seq * D * width * 3, bytes_accessed=D * width * 6, transcendentals=0
        ),
        name="attention",
    )(place, *blocks, gain[None], bias[None], weight, cosine, sine, segments[:, None], segments[None])


def block_product(place, blocks, weight):
    depth = blocks[0].shape[1]
    total = None
    for index, block in enumerate(blocks):
        at = pl.multiple_of((place ^ index) * depth, depth)
        term = jnp.dot(
            block[...], weight[pl.ds(at, depth), :], preferred_element_type=jnp.float32
        )
        total = term if total is None else total + term
    return total


def hidden_kernel(tensor_count, place_ref, *refs):
    blocks, tokens = refs[:tensor_count], refs[tensor_count : 2 * tensor_count]
    weight, scale, pick, hidden, picked, residual = refs[2 * tensor_count :]
    place = place_ref[0]
    projected = block_product(place, blocks, weight).astype(jnp.bfloat16).astype(jnp.float32)
    width, rows = hidden.shape[1], tokens[0].shape[0]
    lanes = pl.ds(pl.multiple_of(place * width, width), width)
    for index, block in enumerate(tokens):
        at = pl.multiple_of((place ^ index) * rows, rows)
        residual[pl.ds(at, rows), :] = block[:, lanes].astype(jnp.float32)
    result = (residual[...] + scale[:, lanes] * projected).astype(jnp.bfloat16)
    hidden[...] = result
    ids = lax.broadcasted_iota(jnp.int32, picked.shape[:1] + hidden.shape[:1], 1)
    chosen = (pick[...] == ids).astype(jnp.bfloat16)
    picked[...] = jnp.dot(chosen, result, preferred_element_type=jnp.float32).astype(jnp.bfloat16)


def hidden_of(place, blocks, tokens, weight, scale, pick):
    seq, width = blocks[0].shape[0], weight.shape[1]
    return pl.pallas_call(
        functools.partial(hidden_kernel, len(blocks)),
        out_shape=[jax.ShapeDtypeStruct((seq, width), jnp.bfloat16)] * 2,
        in_specs=[SMEM] + [VMEM] * (2 * len(blocks) + 3),
        out_specs=[VMEM] * 2,
        scratch_shapes=[pltpu.VMEM((seq, width), jnp.float32)],
        compiler_params=pltpu.CompilerParams(vmem_limit_bytes=24 * 2**20),
        cost_estimate=pl.CostEstimate(
            flops=2 * seq * D * width, bytes_accessed=D * width * 2, transcendentals=0
        ),
        name="hidden",
    )(place, *blocks, *tokens, weight, scale[None], pick.reshape(-1, 1))


def partial_kernel(tensor_count, place_ref, *refs):
    blocks = refs[:tensor_count]
    weight, target, out = refs[tensor_count:]
    partial = block_product(place_ref[0], blocks, weight).astype(jnp.bfloat16)
    slots = lax.broadcasted_iota(jnp.int32, (out.shape[0], target.shape[1]), 0)
    placing = (slots == target[...]).astype(jnp.bfloat16)
    out[...] = jnp.dot(placing, partial, preferred_element_type=jnp.float32).astype(jnp.bfloat16)


def partial_rows(place, blocks, weight, target, slot_total):
    seq, width = blocks[0].shape[0], weight.shape[1]
    return pl.pallas_call(
        functools.partial(partial_kernel, len(blocks)),
        out_shape=jax.ShapeDtypeStruct((slot_total, width), jnp.bfloat16),
        in_specs=[SMEM] + [VMEM] * (len(blocks) + 2),
        out_specs=VMEM,
        compiler_params=pltpu.CompilerParams(vmem_limit_bytes=24 * 2**20),
        cost_estimate=pl.CostEstimate(
            flops=2 * seq * D * width, bytes_accessed=D * width * 2, transcendentals=0
        ),
        name="partial",
    )(place, *blocks, weight, target[None])


def sum_kernel(incoming, received, stats):
    total = jnp.sum(incoming[...].astype(jnp.float32), axis=0).astype(jnp.bfloat16)
    received[...] = total
    total = total.astype(jnp.float32)
    sums = jnp.sum(total, axis=1, keepdims=True)
    squares = jnp.sum(total * total, axis=1, keepdims=True)
    lane = lax.broadcasted_iota(jnp.int32, stats.shape[1:], 1)
    line = jnp.where(lane == 0, sums, jnp.where(lane == 1, squares, 0.0))
    for index in range(stats.shape[0]):
        stats[index] = line


def summed(incoming, tensor_count):
    _, rows, width = incoming.shape
    return pl.pallas_call(
        sum_kernel,
        out_shape=[
            jax.ShapeDtypeStruct((rows, width), jnp.bfloat16),
            jax.ShapeDtypeStruct((tensor_count, rows, 128), jnp.float32),
        ],
        in_specs=[VMEM],
        out_specs=[VMEM] * 2,
        name="summed",
    )(incoming)


def routed_kernel(received, stats, gain, bias, arrived, out):
    total = jnp.sum(stats[...], axis=0)
    mean_row = total[:, 0:1] * (1.0 / D)
    var_row = total[:, 1:2] * (1.0 / D) - mean_row * mean_row
    value = (received[...].astype(jnp.float32) - mean_row) * lax.rsqrt(var_row + 1e-06)
    value = (value * gain[...] + bias[...]) * arrived[...]
    out[...] = value.astype(jnp.bfloat16)


def routed_rows(received, stats, gain, bias, arrived):
    return pl.pallas_call(
        routed_kernel,
        out_shape=jax.ShapeDtypeStruct(received.shape, jnp.bfloat16),
        in_specs=[VMEM] * 5,
        out_specs=VMEM,
        name="routed",
    )(received, stats, gain[None], bias[None], arrived[:, None])


def on_device(
    tokens,
    ln1_gain,
    ln1_bias,
    qkv_weight,
    out_weight,
    layer_scale,
    segment_ids,
    positions,
    merge_index,
    merge_weight,
    owners,
    ln2_gain,
    ln2_bias,
):
    tensor_count = lax.axis_size("tensor")
    group_count = lax.axis_size("dp")
    place = lax.axis_index("tensor")[None]
    width = out_weight.shape[1]
    merged_count = merge_index.shape[0]
    slots_cap = 2 * merged_count // group_count

    token_blocks = gather_blocks(tokens, "tensor")
    attended = attention(
        place, token_blocks, ln1_gain, ln1_bias, qkv_weight, positions, segment_ids
    )
    hidden_columns, picked = hidden_of(
        place, gather_blocks(attended, "tensor"), token_blocks, out_weight, layer_scale, merge_index.T
    )
    hidden = lax.all_to_all(hidden_columns, "tensor", split_axis=0, concat_axis=1, tiled=True)

    if merge_weight.shape[0] == D:
        arrived_rows = lax.all_to_all(picked, "dp", split_axis=0, concat_axis=0, tiled=True)
        owner_all = jnp.stack(gather_blocks(owners[:, 0], "dp"))
        slot_all = jax.vmap(lambda owner_of: slots_of(owner_of, group_count))(owner_all)
        order = jnp.arange(group_count, dtype=jnp.int32) ^ lax.axis_index("dp")
        owner_all = jnp.take(owner_all, order, axis=0)
        slot_all = jnp.take(slot_all, order, axis=0)
        group_all = jnp.arange(group_count, dtype=jnp.int32)[:, None]
        target = ((owner_all * group_count + group_all) * slots_cap + slot_all).reshape(-1)
        own_slots = group_count * slots_cap
        own_target = target - lax.axis_index("dp") * own_slots
        arrived = jnp.any(
            own_target[None, :] == jnp.arange(own_slots, dtype=jnp.int32)[:, None], axis=1
        ).astype(jnp.float32)
        outgoing = partial_rows(
            place, gather_blocks(arrived_rows, "tensor"), merge_weight, target, group_count * own_slots
        )
        incoming = lax.all_to_all(
            outgoing.reshape(group_count, own_slots, width),
            "dp", split_axis=0, concat_axis=0, tiled=True,
        )
    else:
        all_hidden = lax.all_gather(hidden, "tensor", axis=0, tiled=True)
        merged = jnp.take(all_hidden, merge_index.reshape(-1), axis=0).reshape(merged_count, 4 * D)
        reduced = jnp.dot(
            merged,
            lax.all_gather(merge_weight, "dp", axis=0, tiled=True),
            preferred_element_type=jnp.float32,
        ).astype(jnp.bfloat16)
        target = owners[:, 0] * slots_cap + slots_of(owners[:, 0], group_count)
        placing = (
            jnp.arange(group_count * slots_cap, dtype=jnp.int32)[:, None] == target[None, :]
        ).astype(jnp.bfloat16)
        outgoing = jnp.dot(placing, reduced, preferred_element_type=jnp.float32).astype(jnp.bfloat16)
        marks = jnp.sum(placing.astype(jnp.float32), axis=1).astype(jnp.bfloat16)
        incoming, arrived = (
            lax.all_to_all(outgoing, "dp", split_axis=0, concat_axis=0, tiled=True)[None],
            lax.all_to_all(marks, "dp", split_axis=0, concat_axis=0, tiled=True).astype(jnp.float32),
        )
    received, stats = summed(incoming, tensor_count)
    stats = lax.all_to_all(stats, "tensor", split_axis=0, concat_axis=0, tiled=True)
    routed = routed_rows(received, stats, ln2_gain, ln2_bias, arrived)
    return (hidden, routed)


def solution(mesh):
    in_specs = (
        P(("dp", "tensor"), None),
        P(),
        P(),
        P(None, "tensor"),
        P(None, "tensor"),
        P(),
        P("dp"),
        P("dp", None),
        P("dp", None),
        P("dp", "tensor"),
        P("dp", None),
        P("tensor"),
        P("tensor"),
    )
    out_specs = (P(("dp", "tensor"), None), P("dp", "tensor"))
    return jax.shard_map(
        on_device, mesh=mesh, in_specs=in_specs, out_specs=out_specs, check_vma=False
    )
```

```python
import functools
import math

import jax
import jax.numpy as jnp
from jax import lax
from jax.experimental import pallas as pl
from jax.experimental.pallas import tpu as pltpu
from jax.sharding import PartitionSpec as P

D = 4096
HD = 128


def finish_norm(values, row_total, row_squares, gain, bias):
    mean_row = row_total / D
    var_row = row_squares / D - mean_row * mean_row
    return (values - mean_row[:, None]) * lax.rsqrt(var_row[:, None] + 1e-06) * gain + bias


def row_stats(values):
    return (jnp.sum(values, axis=1), jnp.sum(values * values, axis=1))


def swap(block, axis, bit):
    count = lax.axis_size(axis)
    return lax.ppermute(block, axis, [(i, i ^ bit) for i in range(count)])


def gather_blocks(block, axis):
    count = lax.axis_size(axis)
    blocks = {0: block}
    bit = count // 2
    while bit:
        blocks.update({index ^ bit: swap(held, axis, bit) for index, held in sorted(blocks.items())})
        bit //= 2
    return [blocks[index] for index in range(count)]


def contract_blocks(blocks, weight, place):
    depth = blocks[0].shape[1]
    total = None
    for index, block in enumerate(blocks):
        rows = lax.dynamic_slice_in_dim(weight, (place ^ index) * depth, depth, axis=0)
        term = jnp.dot(block, rows, preferred_element_type=jnp.float32)
        total = term if total is None else total + term
    return total


def slots_of(owner_of, group_count):
    one_hot = (owner_of[:, None] == jnp.arange(group_count, dtype=jnp.int32)[None, :]).astype(
        jnp.int32
    )
    before = jnp.cumsum(one_hot, axis=0) - one_hot
    return jnp.sum(before * one_hot, axis=1)


VMEM = pl.BlockSpec(memory_space=pltpu.VMEM)
HBM = pl.BlockSpec(memory_space=pltpu.HBM)


def column(row, width):
    return jnp.transpose(jnp.broadcast_to(row, (width, row.shape[1])))


def tables_kernel(positions, segments, cosine, sine, same):
    lane = lax.broadcasted_iota(jnp.int32, cosine.shape, 1)
    quarter = HD // 4
    frequency = jnp.exp((lane % quarter).astype(jnp.float32) * (-math.log(100.0) / quarter))
    places = positions[...].astype(jnp.float32)
    rows, columns = column(places[0:1], HD), column(places[1:2], HD)
    angles = jnp.where(lane < 2 * quarter, rows, columns) * frequency
    cosine[...] = jnp.cos(angles)
    sines = jnp.sin(angles)
    sine[...] = jnp.where((lane & quarter) == 0, -sines, sines)
    ids = segments[...].astype(jnp.float32)
    same[...] = (column(ids, ids.shape[1]) == ids).astype(jnp.float32)


def tables(positions, segments):
    seq = segments.shape[0]
    return pl.pallas_call(
        tables_kernel,
        out_shape=[
            jax.ShapeDtypeStruct((seq, HD), jnp.float32),
            jax.ShapeDtypeStruct((seq, HD), jnp.float32),
            jax.ShapeDtypeStruct((seq, seq), jnp.float32),
        ],
        in_specs=[VMEM] * 2,
        out_specs=[VMEM] * 3,
        name="tables",
    )(positions.T, segments[None])


def attention_kernel(tensor_count, *refs):
    arrived = refs[: tensor_count - 1]
    (tokens_in, gain_in, bias_in, weight_in, cosine, sine, same_in, out, residual,
     normed, tokens, gain, bias, weight, small_sems, weight_sems) = refs[tensor_count - 1 :]
    place = lax.axis_index("tensor")
    rows, head_count, width = tokens.shape[0], out.shape[1] // HD, residual.shape[1]
    small = [
        pltpu.make_async_copy(source, held, small_sems.at[index])
        for index, (source, held) in enumerate(
            ((tokens_in, tokens), (gain_in, gain), (bias_in, bias))
        )
    ]
    heads = [
        pltpu.make_async_copy(
            weight_in.at[:, pl.ds(head * 3 * HD, 3 * HD)], weight.at[head], weight_sems.at[head]
        )
        for head in range(head_count)
    ]
    for copy in small + heads:
        copy.start()
    for copy in small:
        copy.wait()
    lanes = pl.ds(pl.multiple_of(place * width, width), width)
    for index, block in enumerate((tokens, *arrived)):
        values = block[...].astype(jnp.float32)
        center = values - jnp.mean(values, axis=-1, keepdims=True)
        spread = jnp.mean(center * center, axis=-1, keepdims=True)
        value = center * lax.rsqrt(spread + 1e-06) * gain[...] + bias[...]
        at = pl.ds(pl.multiple_of((place ^ index) * rows, rows), rows)
        normed[at, :] = value.astype(jnp.bfloat16)
        residual[at, :] = block[:, lanes]
    same = same_in[...] > 0.5
    low = (lax.broadcasted_iota(jnp.int32, cosine.shape, 1) & (HD // 4)) == 0

    def rotated(part):
        swapped = jnp.where(low, pltpu.roll(part, HD - HD // 4, 1), pltpu.roll(part, HD // 4, 1))
        return (part * cosine[...] + swapped * sine[...]).astype(jnp.bfloat16)

    for head in range(head_count):
        heads[head].wait()
        packed = jnp.dot(normed[...], weight[head], preferred_element_type=jnp.float32)
        queries, keys = rotated(packed[:, :HD]), rotated(packed[:, HD : 2 * HD])
        values = packed[:, 2 * HD :].astype(jnp.bfloat16)
        scores = lax.dot_general(
            queries, keys, (((1,), (1,)), ((), ())), preferred_element_type=jnp.float32
        ) * (1.0 / math.sqrt(HD))
        scores = jnp.where(same, scores, -jnp.inf)
        weights = jnp.exp(scores - jnp.max(scores, axis=-1, keepdims=True))
        probs = (weights / jnp.sum(weights, axis=-1, keepdims=True)).astype(jnp.bfloat16)
        mixed = jnp.dot(probs, values, preferred_element_type=jnp.float32)
        out[:, head * HD : (head + 1) * HD] = mixed.astype(jnp.bfloat16)


def attention(blocks, gain, bias, weight, cosine, sine, same, width):
    rows = blocks[0].shape[0]
    seq, columns = rows * len(blocks), weight.shape[1]
    heads = columns // (3 * HD)
    return pl.pallas_call(
        functools.partial(attention_kernel, len(blocks)),
        out_shape=[
            jax.ShapeDtypeStruct((seq, heads * HD), jnp.bfloat16),
            jax.ShapeDtypeStruct((seq, width), jnp.bfloat16),
        ],
        in_specs=[VMEM] * (len(blocks) - 1) + [HBM] * 4 + [VMEM] * 3,
        out_specs=[VMEM] * 2,
        scratch_shapes=[
            pltpu.VMEM((seq, D), jnp.bfloat16),
            pltpu.VMEM((rows, D), jnp.bfloat16),
            pltpu.VMEM((1, D), jnp.float32),
            pltpu.VMEM((1, D), jnp.float32),
            pltpu.VMEM((heads, D, 3 * HD), jnp.bfloat16),
            pltpu.SemaphoreType.DMA((3,)),
            pltpu.SemaphoreType.DMA((heads,)),
        ],
        compiler_params=pltpu.CompilerParams(vmem_limit_bytes=40 * 2**20),
        cost_estimate=pl.CostEstimate(
            flops=2 * seq * D * columns, bytes_accessed=D * columns * 2, transcendentals=0
        ),
        name="attention",
    )(*blocks[1:], blocks[0], gain[None], bias[None], weight, cosine, sine, same)


def start_rows(weight_in, weight, sems, place):
    depth = weight.shape[1]
    copies = [
        pltpu.make_async_copy(
            weight_in.at[pl.ds(pl.multiple_of((place ^ index) * depth, depth), depth), :],
            weight.at[index],
            sems.at[index],
        )
        for index in range(weight.shape[0])
    ]
    for copy in copies:
        copy.start()
    return copies


def block_product(blocks, weight, copies):
    total = None
    for index, block in enumerate(blocks):
        copies[index].wait()
        term = jnp.dot(block[...], weight[index], preferred_element_type=jnp.float32)
        total = term if total is None else total + term
    return total


def hidden_kernel(tensor_count, *refs):
    blocks = refs[:tensor_count]
    weight_in, scale_in, residual, pick, hidden, *picked = refs[tensor_count:-4]
    weight, scale, sems, scale_sem = refs[-4:]
    place, group = lax.axis_index("tensor"), lax.axis_index("dp")
    width = hidden.shape[1]
    scale_copy = pltpu.make_async_copy(
        scale_in.at[:, pl.ds(pl.multiple_of(place * width, width), width)], scale, scale_sem.at[0]
    )
    scale_copy.start()
    copies = start_rows(weight_in, weight, sems, place)
    scale_copy.wait()
    projected = block_product(blocks, weight, copies).astype(jnp.bfloat16).astype(jnp.float32)
    result = (residual[...].astype(jnp.float32) + scale[...] * projected).astype(jnp.bfloat16)
    hidden[...] = result
    ids = lax.broadcasted_iota(jnp.int32, (hidden.shape[0], pick.shape[1]), 0)
    for index, rows in enumerate(picked):
        chosen = (pick[pl.ds(group ^ index, 1), :] == ids).astype(jnp.bfloat16)
        rows[...] = lax.dot_general(
            chosen, result, (((0,), (0,)), ((), ())), preferred_element_type=jnp.float32
        ).astype(jnp.bfloat16)


def hidden_of(blocks, weight, scale, residual, pick):
    seq, width = residual.shape
    depth = blocks[0].shape[1]
    slots, merged = pick.shape
    return pl.pallas_call(
        functools.partial(hidden_kernel, len(blocks)),
        out_shape=[jax.ShapeDtypeStruct((seq, width), jnp.bfloat16)]
        + [jax.ShapeDtypeStruct((merged, width), jnp.bfloat16)] * slots,
        in_specs=[VMEM] * len(blocks) + [HBM] * 2 + [VMEM] * 2,
        out_specs=[VMEM] * (1 + slots),
        scratch_shapes=[
            pltpu.VMEM((len(blocks), depth, width), jnp.bfloat16),
            pltpu.VMEM((1, width), jnp.float32),
            pltpu.SemaphoreType.DMA((len(blocks),)),
            pltpu.SemaphoreType.DMA((1,)),
        ],
        compiler_params=pltpu.CompilerParams(vmem_limit_bytes=24 * 2**20),
        cost_estimate=pl.CostEstimate(
            flops=2 * seq * D * width, bytes_accessed=D * width * 2, transcendentals=0
        ),
        name="hidden",
    )(*blocks, weight, scale[None], residual, pick)


def targets_kernel(group_count, owners, target):
    total = owners.shape[1]
    merged = total // group_count
    lane = lax.broadcasted_iota(jnp.int32, (8, total), 1)
    owner = jnp.broadcast_to(owners[...], (8, total))
    before = lax.broadcasted_iota(jnp.int32, (total, total), 0)
    after = lax.broadcasted_iota(jnp.int32, (total, total), 1)
    earlier = ((before < after) & (before // merged == after // merged)).astype(jnp.bfloat16)
    slot = jnp.zeros((8, total), jnp.float32)
    for index in range(group_count):
        named = (owner == index).astype(jnp.float32)
        count = jnp.dot(named.astype(jnp.bfloat16), earlier, preferred_element_type=jnp.float32)
        slot = slot + named * count
    group = lax.axis_index("dp") ^ (lane // merged)
    cap = 2 * merged // group_count
    result = (owner * group_count + group) * cap + slot.astype(jnp.int32)
    target[...] = result[0:1]


def targets(owners, group_count):
    return pl.pallas_call(
        functools.partial(targets_kernel, group_count),
        out_shape=jax.ShapeDtypeStruct(owners.shape, jnp.int32),
        in_specs=[VMEM],
        out_specs=VMEM,
        name="targets",
    )(owners)


def partial_kernel(tensor_count, *refs):
    blocks = refs[:tensor_count]
    weight_in, target, *outs = refs[tensor_count:-2]
    weight, sems = refs[-2:]
    place, group = lax.axis_index("tensor"), lax.axis_index("dp")
    copies = start_rows(weight_in, weight, sems, place)
    partial = block_product(blocks, weight, copies).astype(jnp.bfloat16)
    cap = outs[0].shape[0]
    slot = lax.broadcasted_iota(jnp.int32, (cap, target.shape[1]), 0)
    for index, out in enumerate(outs):
        placing = (slot + (group ^ index) * cap == target[...]).astype(jnp.bfloat16)
        out[...] = jnp.dot(placing, partial, preferred_element_type=jnp.float32).astype(jnp.bfloat16)


def partial_rows(blocks, weight, target, group_count, own_slots):
    seq, depth = blocks[0].shape
    width = weight.shape[1]
    return pl.pallas_call(
        functools.partial(partial_kernel, len(blocks)),
        out_shape=[jax.ShapeDtypeStruct((own_slots, width), jnp.bfloat16)] * group_count,
        in_specs=[VMEM] * len(blocks) + [HBM, VMEM],
        out_specs=[VMEM] * group_count,
        scratch_shapes=[
            pltpu.VMEM((len(blocks), depth, width), jnp.bfloat16),
            pltpu.SemaphoreType.DMA((len(blocks),)),
        ],
        compiler_params=pltpu.CompilerParams(vmem_limit_bytes=24 * 2**20),
        cost_estimate=pl.CostEstimate(
            flops=2 * seq * D * width, bytes_accessed=D * width * 2, transcendentals=0
        ),
        name="partial",
    )(*blocks, weight, target)


def summed_kernel(*refs):
    *parts, hidden, received, outgoing = refs
    total = parts[0][...].astype(jnp.float32)
    for part in parts[1:]:
        total = total + part[...].astype(jnp.float32)
    received[...] = total.astype(jnp.bfloat16)
    total = total.astype(jnp.bfloat16).astype(jnp.float32)
    sums = jnp.sum(total, axis=1, keepdims=True)
    squares = jnp.sum(total * total, axis=1, keepdims=True)
    both = jnp.concatenate([sums, squares], axis=0)
    lanes = both.shape[0]
    count, rows, _ = outgoing.shape
    width = hidden.shape[1]
    value = jnp.transpose(jnp.broadcast_to(both, (lanes, lanes)))[:rows]
    high = value.astype(jnp.bfloat16).astype(jnp.float32)
    rest = value - high
    middle = rest.astype(jnp.bfloat16).astype(jnp.float32)
    low = rest - middle
    row = lax.broadcasted_iota(jnp.int32, value.shape, 0)
    stats = jnp.where(row == 0, high, jnp.where(row == 1, middle, jnp.where(row == 2, low, 0.0)))
    stats = stats.astype(jnp.bfloat16)
    for index in range(count):
        outgoing[index, :, :width] = hidden[index * rows : (index + 1) * rows, :]
        outgoing[index, :, width:] = stats


def summed(parts, hidden, tensor_count):
    own_slots, width = parts[0].shape
    rows = hidden.shape[0] // tensor_count
    return pl.pallas_call(
        summed_kernel,
        out_shape=[
            jax.ShapeDtypeStruct((own_slots, width), jnp.bfloat16),
            jax.ShapeDtypeStruct((tensor_count, rows, width + 2 * own_slots), jnp.bfloat16),
        ],
        in_specs=[VMEM] * (len(parts) + 1),
        out_specs=[VMEM] * 2,
        name="summed",
    )(*parts, hidden)


def routed_kernel(received, incoming, gain, bias, target, hidden, out):
    own_slots, width = received.shape
    stats = jnp.sum(incoming[:, :, width:].astype(jnp.float32), axis=0)
    line = stats[0:1] + stats[1:2] + stats[2:3]
    totals = column(line, line.shape[1])
    mean_row = totals[:own_slots, 0:1] * (1.0 / D)
    var_row = totals[own_slots:, 0:1] * (1.0 / D) - mean_row * mean_row
    slot = lax.broadcasted_iota(jnp.int32, (own_slots, target.shape[1]), 0)
    slot = slot + lax.axis_index("dp") * own_slots
    filled = jnp.sum((slot == target[...]).astype(jnp.float32), axis=1, keepdims=True)
    value = (received[...].astype(jnp.float32) - mean_row) * lax.rsqrt(var_row + 1e-06)
    value = (value * gain[...] + bias[...]) * filled
    out[...] = value.astype(jnp.bfloat16)
    for index in range(incoming.shape[0]):
        hidden[:, index * width : (index + 1) * width] = incoming[index, :, :width]


def routed_rows(received, incoming, gain, bias, target):
    return pl.pallas_call(
        routed_kernel,
        out_shape=[
            jax.ShapeDtypeStruct((incoming.shape[1], D), jnp.bfloat16),
            jax.ShapeDtypeStruct(received.shape, jnp.bfloat16),
        ],
        in_specs=[VMEM] * 5,
        out_specs=[VMEM] * 2,
        name="routed",
    )(received, incoming, gain[None], bias[None], target)


def exchange(parts):
    far = swap(parts[3], "dp", 2)
    return [parts[0], swap(parts[1], "dp", 1), swap(parts[2], "dp", 2), swap(far, "dp", 1)]


def on_device(
    tokens,
    ln1_gain,
    ln1_bias,
    qkv_weight,
    out_weight,
    layer_scale,
    segment_ids,
    positions,
    merge_index,
    merge_weight,
    owners,
    ln2_gain,
    ln2_bias,
):
    tensor_count = lax.axis_size("tensor")
    group_count = lax.axis_size("dp")
    place = lax.axis_index("tensor")
    width = out_weight.shape[1]
    merged_count = merge_index.shape[0]
    slots_cap = 2 * merged_count // group_count
    own_slots = group_count * slots_cap

    token_blocks = gather_blocks(tokens, "tensor")
    cosine, sine, same = tables(positions, segment_ids)
    attended, residual = attention(
        token_blocks, ln1_gain, ln1_bias, qkv_weight, cosine, sine, same, width
    )
    attended_blocks = gather_blocks(attended, "tensor")

    if group_count == 4 and 2 * own_slots == HD:
        owner_blocks = exchange([owners[:, 0]] * group_count)
        target = targets(jnp.concatenate(owner_blocks)[None], group_count)
        hidden_columns, *picked = hidden_of(
            attended_blocks, out_weight, layer_scale, residual, merge_index.T
        )
        arrived_rows = jnp.concatenate(exchange(picked))
        outgoing = partial_rows(
            gather_blocks(arrived_rows, "tensor"), merge_weight, target, group_count, own_slots
        )
        received, line = summed(exchange(outgoing), hidden_columns, tensor_count)
        line = lax.all_to_all(line, "tensor", split_axis=0, concat_axis=0, tiled=True)
        hidden, routed = routed_rows(received, line, ln2_gain, ln2_bias, target)
        return (hidden, routed)

    projected = contract_blocks(attended_blocks, out_weight, place).astype(jnp.bfloat16)
    own_scale = lax.dynamic_slice_in_dim(layer_scale, place * width, width, axis=0)
    hidden_columns = (
        residual.astype(jnp.float32) + own_scale * projected.astype(jnp.float32)
    ).astype(jnp.bfloat16)
    hidden = lax.all_to_all(hidden_columns, "tensor", split_axis=0, concat_axis=1, tiled=True)
    all_hidden = lax.all_gather(hidden, "tensor", axis=0, tiled=True)
    merged = jnp.take(all_hidden, merge_index.reshape(-1), axis=0).reshape(merged_count, 4 * D)
    reduced = jnp.dot(
        merged,
        lax.all_gather(merge_weight, "dp", axis=0, tiled=True),
        preferred_element_type=jnp.float32,
    ).astype(jnp.bfloat16)
    target = owners[:, 0] * slots_cap + slots_of(owners[:, 0], group_count)
    placing = (
        jnp.arange(own_slots, dtype=jnp.int32)[:, None] == target[None, :]
    ).astype(jnp.bfloat16)
    outgoing = jnp.dot(placing, reduced, preferred_element_type=jnp.float32).astype(jnp.bfloat16)
    marks = jnp.sum(placing.astype(jnp.float32), axis=1).astype(jnp.bfloat16)
    incoming, arrived = (
        lax.all_to_all(outgoing, "dp", split_axis=0, concat_axis=0, tiled=True),
        lax.all_to_all(marks, "dp", split_axis=0, concat_axis=0, tiled=True),
    )
    received = incoming.astype(jnp.float32)
    row_total, row_squares = lax.psum(row_stats(received), "tensor")
    routed = (
        finish_norm(received, row_total, row_squares, ln2_gain, ln2_bias)
        * arrived.astype(jnp.float32)[:, None]
    ).astype(jnp.bfloat16)
    return (hidden, routed)


def solution(mesh):
    in_specs = (
        P(("dp", "tensor"), None),
        P(),
        P(),
        P(None, "tensor"),
        P(None, "tensor"),
        P(),
        P("dp"),
        P("dp", None),
        P("dp", None),
        P("dp", "tensor"),
        P("dp", None),
        P("tensor"),
        P("tensor"),
    )
    out_specs = (P(("dp", "tensor"), None), P("dp", "tensor"))
    return jax.shard_map(
        on_device, mesh=mesh, in_specs=in_specs, out_specs=out_specs, check_vma=False
    )
```

```python
import functools
import math

import jax
import jax.numpy as jnp
from jax import lax
from jax.experimental import pallas as pl
from jax.experimental.pallas import tpu as pltpu
from jax.sharding import PartitionSpec as P

D = 4096
HD = 128


def finish_norm(values, row_total, row_squares, gain, bias):
    mean_row = row_total / D
    var_row = row_squares / D - mean_row * mean_row
    return (values - mean_row[:, None]) * lax.rsqrt(var_row[:, None] + 1e-06) * gain + bias


def row_stats(values):
    return (jnp.sum(values, axis=1), jnp.sum(values * values, axis=1))


def swap(block, axis, bit):
    count = lax.axis_size(axis)
    return lax.ppermute(block, axis, [(i, i ^ bit) for i in range(count)])


def gather_blocks(block, axis, *beside):
    count = lax.axis_size(axis)
    bit = count // 2
    far, near, *beside = lax.optimization_barrier((swap(block, axis, bit), swap(block, axis, 1), *beside))
    blocks = {0: block, bit: far, 1: near}
    for index in range(2, bit):
        blocks[index] = swap(block, axis, index)
    for index in range(1, bit):
        blocks[index ^ bit] = swap(far, axis, index)
    return [blocks[index] for index in range(count)], beside


def contract_blocks(blocks, weight, place):
    depth = blocks[0].shape[1]
    total = None
    for index, block in enumerate(blocks):
        rows = lax.dynamic_slice_in_dim(weight, (place ^ index) * depth, depth, axis=0)
        term = jnp.dot(block, rows, preferred_element_type=jnp.float32)
        total = term if total is None else total + term
    return total


def slots_of(owner_of, group_count):
    one_hot = (owner_of[:, None] == jnp.arange(group_count, dtype=jnp.int32)[None, :]).astype(
        jnp.int32
    )
    before = jnp.cumsum(one_hot, axis=0) - one_hot
    return jnp.sum(before * one_hot, axis=1)


VMEM = pl.BlockSpec(memory_space=pltpu.VMEM)
HBM = pl.BlockSpec(memory_space=pltpu.HBM)
STRIPE = 512


def column(row, width):
    return jnp.transpose(jnp.broadcast_to(row, (width, row.shape[1])))


def start_stripes(source, held, sems):
    copies = [
        pltpu.make_async_copy(
            source.at[pl.ds(index * STRIPE, STRIPE), :],
            held.at[pl.ds(index * STRIPE, STRIPE), :],
            sems.at[index],
        )
        for index in range(held.shape[0] // STRIPE)
    ]
    for copy in copies:
        copy.start()
    return copies


def fetch_kernel(weight_in, weight, sems):
    copies = start_stripes(weight_in, weight, sems)
    for copy in copies:
        copy.wait()


def fetch(weight):
    return pl.pallas_call(
        fetch_kernel,
        out_shape=jax.ShapeDtypeStruct(weight.shape, weight.dtype),
        in_specs=[HBM],
        out_specs=VMEM,
        scratch_shapes=[pltpu.SemaphoreType.DMA((weight.shape[0] // STRIPE,))],
        compiler_params=pltpu.CompilerParams(vmem_limit_bytes=24 * 2**20),
        cost_estimate=pl.CostEstimate(flops=0, bytes_accessed=weight.size * 4, transcendentals=0),
        name="fetch",
    )(weight)


def prepare_kernel(
    positions, segments, gain_in, bias_in, tokens_in, weight_in,
    cosine, sine, same, gain, bias, tokens, weight, sems, weight_sems,
):
    head_width = 3 * HD
    copies = [
        pltpu.make_async_copy(source, held, sems.at[index])
        for index, (source, held) in enumerate(
            ((gain_in, gain), (bias_in, bias), (tokens_in, tokens))
        )
    ]
    for copy in copies:
        copy.start()
    copies += start_stripes(weight_in, weight, weight_sems)
    lane = lax.broadcasted_iota(jnp.int32, cosine.shape, 1)
    quarter = HD // 4
    frequency = jnp.exp((lane % quarter).astype(jnp.float32) * (-math.log(100.0) / quarter))
    places = positions[...].astype(jnp.float32)
    rows, columns = column(places[0:1], HD), column(places[1:2], HD)
    angles = jnp.where(lane < 2 * quarter, rows, columns) * frequency
    cosine[...] = jnp.cos(angles)
    sines = jnp.sin(angles)
    sine[...] = jnp.where((lane & quarter) == 0, -sines, sines)
    ids = segments[...].astype(jnp.float32)
    same[...] = (column(ids, ids.shape[1]) == ids).astype(jnp.float32)
    for copy in copies:
        copy.wait()


def prepare(positions, segments, gain, bias, tokens, weight):
    seq = segments.shape[0]
    held = [gain[None], bias[None], tokens, weight]
    return pl.pallas_call(
        prepare_kernel,
        out_shape=[
            jax.ShapeDtypeStruct((seq, HD), jnp.float32),
            jax.ShapeDtypeStruct((seq, HD), jnp.float32),
            jax.ShapeDtypeStruct((seq, seq), jnp.float32),
        ]
        + [jax.ShapeDtypeStruct(array.shape, array.dtype) for array in held],
        in_specs=[VMEM] * 2 + [HBM] * 4,
        out_specs=[VMEM] * 7,
        scratch_shapes=[
            pltpu.SemaphoreType.DMA((3,)),
            pltpu.SemaphoreType.DMA((weight.shape[0] // STRIPE,)),
        ],
        compiler_params=pltpu.CompilerParams(vmem_limit_bytes=24 * 2**20),
        cost_estimate=pl.CostEstimate(
            flops=0, bytes_accessed=weight.size * 4, transcendentals=0
        ),
        name="prepare",
    )(positions.T, segments[None], *held)


def attention_kernel(tensor_count, *refs):
    blocks = refs[:tensor_count]
    gain, bias, weight, cosine, sine, same_in, out, residual, normed = refs[tensor_count:]
    place = lax.axis_index("tensor")
    rows, head_count, width = blocks[0].shape[0], out.shape[1] // HD, residual.shape[1]
    lanes = pl.ds(pl.multiple_of(place * width, width), width)
    for index, block in enumerate(blocks):
        values = block[...].astype(jnp.float32)
        center = values - jnp.mean(values, axis=-1, keepdims=True)
        spread = jnp.mean(center * center, axis=-1, keepdims=True)
        value = center * lax.rsqrt(spread + 1e-06) * gain[...] + bias[...]
        at = pl.ds(pl.multiple_of((place ^ index) * rows, rows), rows)
        normed[at, :] = value.astype(jnp.bfloat16)
        residual[at, :] = block[:, lanes]
    same = same_in[...] > 0.5
    low = (lax.broadcasted_iota(jnp.int32, cosine.shape, 1) & (HD // 4)) == 0

    def rotated(part):
        swapped = jnp.where(low, pltpu.roll(part, HD - HD // 4, 1), pltpu.roll(part, HD // 4, 1))
        return (part * cosine[...] + swapped * sine[...]).astype(jnp.bfloat16)

    for head in range(head_count):
        first = head * 3 * HD
        packed = jnp.dot(
            normed[...], weight[:, first : first + 3 * HD], preferred_element_type=jnp.float32
        )
        queries, keys = rotated(packed[:, :HD]), rotated(packed[:, HD : 2 * HD])
        values = packed[:, 2 * HD :].astype(jnp.bfloat16)
        scores = lax.dot_general(
            queries, keys, (((1,), (1,)), ((), ())), preferred_element_type=jnp.float32
        ) * (1.0 / math.sqrt(HD))
        scores = jnp.where(same, scores, -jnp.inf)
        weights = jnp.exp(scores - jnp.max(scores, axis=-1, keepdims=True))
        probs = (weights / jnp.sum(weights, axis=-1, keepdims=True)).astype(jnp.bfloat16)
        mixed = jnp.dot(probs, values, preferred_element_type=jnp.float32)
        out[:, head * HD : (head + 1) * HD] = mixed.astype(jnp.bfloat16)


def attention(blocks, gain, bias, weight, cosine, sine, same, width):
    rows = blocks[0].shape[0]
    seq, columns = rows * len(blocks), weight.shape[1]
    heads = columns // (3 * HD)
    return pl.pallas_call(
        functools.partial(attention_kernel, len(blocks)),
        out_shape=[
            jax.ShapeDtypeStruct((seq, heads * HD), jnp.bfloat16),
            jax.ShapeDtypeStruct((seq, width), jnp.bfloat16),
        ],
        in_specs=[VMEM] * (len(blocks) + 6),
        out_specs=[VMEM] * 2,
        scratch_shapes=[pltpu.VMEM((seq, D), jnp.bfloat16)],
        compiler_params=pltpu.CompilerParams(vmem_limit_bytes=24 * 2**20),
        cost_estimate=pl.CostEstimate(
            flops=2 * seq * D * columns, bytes_accessed=D * columns * 2, transcendentals=0
        ),
        name="attention",
    )(*blocks, gain, bias, weight, cosine, sine, same)


def block_product(blocks, weight):
    place = lax.axis_index("tensor")
    depth = blocks[0].shape[1]
    total = None
    for index, block in enumerate(blocks):
        rows = weight[pl.ds(pl.multiple_of((place ^ index) * depth, depth), depth), :]
        term = jnp.dot(block[...], rows, preferred_element_type=jnp.float32)
        total = term if total is None else total + term
    return total


def hidden_kernel(tensor_count, *refs):
    blocks = refs[:tensor_count]
    weight, scale, residual, pick, hidden, *picked = refs[tensor_count:]
    place, group = lax.axis_index("tensor"), lax.axis_index("dp")
    width = hidden.shape[1]
    own_scale = scale[:, pl.ds(pl.multiple_of(place * width, width), width)]
    projected = block_product(blocks, weight).astype(jnp.bfloat16).astype(jnp.float32)
    result = (residual[...].astype(jnp.float32) + own_scale * projected).astype(jnp.bfloat16)
    hidden[...] = result
    ids = lax.broadcasted_iota(jnp.int32, (hidden.shape[0], pick.shape[1]), 0)
    for index, rows in enumerate(picked):
        chosen = (pick[pl.ds(group ^ index, 1), :] == ids).astype(jnp.bfloat16)
        rows[...] = lax.dot_general(
            chosen, result, (((0,), (0,)), ((), ())), preferred_element_type=jnp.float32
        ).astype(jnp.bfloat16)


def hidden_of(blocks, weight, scale, residual, pick):
    seq, width = residual.shape
    slots, merged = pick.shape
    return pl.pallas_call(
        functools.partial(hidden_kernel, len(blocks)),
        out_shape=[jax.ShapeDtypeStruct((seq, width), jnp.bfloat16)]
        + [jax.ShapeDtypeStruct((merged, width), jnp.bfloat16)] * slots,
        in_specs=[VMEM] * (len(blocks) + 4),
        out_specs=[VMEM] * (1 + slots),
        compiler_params=pltpu.CompilerParams(vmem_limit_bytes=24 * 2**20),
        cost_estimate=pl.CostEstimate(
            flops=2 * seq * D * width, bytes_accessed=D * width * 2, transcendentals=0
        ),
        name="hidden",
    )(*blocks, weight, scale[None], residual, pick)


def targets_kernel(group_count, owners, weight_in, target, weight, sems):
    copies = start_stripes(weight_in, weight, sems)
    total = owners.shape[1]
    merged = total // group_count
    lane = lax.broadcasted_iota(jnp.int32, (8, total), 1)
    owner = jnp.broadcast_to(owners[...], (8, total))
    before = lax.broadcasted_iota(jnp.int32, (total, total), 0)
    after = lax.broadcasted_iota(jnp.int32, (total, total), 1)
    earlier = ((before < after) & (before // merged == after // merged)).astype(jnp.bfloat16)
    slot = jnp.zeros((8, total), jnp.float32)
    for index in range(group_count):
        named = (owner == index).astype(jnp.float32)
        count = jnp.dot(named.astype(jnp.bfloat16), earlier, preferred_element_type=jnp.float32)
        slot = slot + named * count
    group = lax.axis_index("dp") ^ (lane // merged)
    cap = 2 * merged // group_count
    result = (owner * group_count + group) * cap + slot.astype(jnp.int32)
    target[...] = result[0:1]
    for copy in copies:
        copy.wait()


def targets(owners, group_count, weight):
    return pl.pallas_call(
        functools.partial(targets_kernel, group_count),
        out_shape=[
            jax.ShapeDtypeStruct(owners.shape, jnp.int32),
            jax.ShapeDtypeStruct(weight.shape, weight.dtype),
        ],
        in_specs=[VMEM, HBM],
        out_specs=[VMEM] * 2,
        scratch_shapes=[pltpu.SemaphoreType.DMA((weight.shape[0] // STRIPE,))],
        compiler_params=pltpu.CompilerParams(vmem_limit_bytes=24 * 2**20),
        cost_estimate=pl.CostEstimate(flops=0, bytes_accessed=weight.size * 4, transcendentals=0),
        name="targets",
    )(owners, weight)


def partial_kernel(tensor_count, *refs):
    blocks = refs[:tensor_count]
    weight, target, *outs = refs[tensor_count:]
    group = lax.axis_index("dp")
    partial = block_product(blocks, weight).astype(jnp.bfloat16)
    cap = outs[0].shape[0]
    slot = lax.broadcasted_iota(jnp.int32, (cap, target.shape[1]), 0)
    for index, out in enumerate(outs):
        placing = (slot + (group ^ index) * cap == target[...]).astype(jnp.bfloat16)
        out[...] = jnp.dot(placing, partial, preferred_element_type=jnp.float32).astype(jnp.bfloat16)


def partial_rows(blocks, weight, target, group_count, own_slots):
    seq, width = blocks[0].shape[0], weight.shape[1]
    return pl.pallas_call(
        functools.partial(partial_kernel, len(blocks)),
        out_shape=[jax.ShapeDtypeStruct((own_slots, width), jnp.bfloat16)] * group_count,
        in_specs=[VMEM] * (len(blocks) + 2),
        out_specs=[VMEM] * group_count,
        compiler_params=pltpu.CompilerParams(vmem_limit_bytes=24 * 2**20),
        cost_estimate=pl.CostEstimate(
            flops=2 * seq * D * width, bytes_accessed=D * width * 2, transcendentals=0
        ),
        name="partial",
    )(*blocks, weight, target)


def summed_kernel(*refs):
    *parts, hidden, received, outgoing = refs
    total = parts[0][...].astype(jnp.float32)
    for part in parts[1:]:
        total = total + part[...].astype(jnp.float32)
    received[...] = total.astype(jnp.bfloat16)
    total = total.astype(jnp.bfloat16).astype(jnp.float32)
    sums = jnp.sum(total, axis=1, keepdims=True)
    squares = jnp.sum(total * total, axis=1, keepdims=True)
    both = jnp.concatenate([sums, squares], axis=0)
    lanes = both.shape[0]
    count, rows, _ = outgoing.shape
    width = hidden.shape[1]
    value = jnp.transpose(jnp.broadcast_to(both, (lanes, lanes)))[:rows]
    high = value.astype(jnp.bfloat16).astype(jnp.float32)
    rest = value - high
    middle = rest.astype(jnp.bfloat16).astype(jnp.float32)
    low = rest - middle
    row = lax.broadcasted_iota(jnp.int32, value.shape, 0)
    stats = jnp.where(row == 0, high, jnp.where(row == 1, middle, jnp.where(row == 2, low, 0.0)))
    stats = stats.astype(jnp.bfloat16)
    for index in range(count):
        outgoing[index, :, :width] = hidden[index * rows : (index + 1) * rows, :]
        outgoing[index, :, width:] = stats


def summed(parts, hidden, tensor_count):
    own_slots, width = parts[0].shape
    rows = hidden.shape[0] // tensor_count
    return pl.pallas_call(
        summed_kernel,
        out_shape=[
            jax.ShapeDtypeStruct((own_slots, width), jnp.bfloat16),
            jax.ShapeDtypeStruct((tensor_count, rows, width + 2 * own_slots), jnp.bfloat16),
        ],
        in_specs=[VMEM] * (len(parts) + 1),
        out_specs=[VMEM] * 2,
        name="summed",
    )(*parts, hidden)


def routed_kernel(received, incoming, gain, bias, target, hidden, out):
    own_slots, width = received.shape
    stats = jnp.sum(incoming[:, :, width:].astype(jnp.float32), axis=0)
    line = stats[0:1] + stats[1:2] + stats[2:3]
    totals = column(line, line.shape[1])
    mean_row = totals[:own_slots, 0:1] * (1.0 / D)
    var_row = totals[own_slots:, 0:1] * (1.0 / D) - mean_row * mean_row
    slot = lax.broadcasted_iota(jnp.int32, (own_slots, target.shape[1]), 0)
    slot = slot + lax.axis_index("dp") * own_slots
    filled = jnp.sum((slot == target[...]).astype(jnp.float32), axis=1, keepdims=True)
    value = (received[...].astype(jnp.float32) - mean_row) * lax.rsqrt(var_row + 1e-06)
    value = (value * gain[...] + bias[...]) * filled
    out[...] = value.astype(jnp.bfloat16)
    for index in range(incoming.shape[0]):
        hidden[:, index * width : (index + 1) * width] = incoming[index, :, :width]


def routed_rows(received, incoming, gain, bias, target):
    return pl.pallas_call(
        routed_kernel,
        out_shape=[
            jax.ShapeDtypeStruct((incoming.shape[1], D), jnp.bfloat16),
            jax.ShapeDtypeStruct(received.shape, jnp.bfloat16),
        ],
        in_specs=[VMEM] * 5,
        out_specs=[VMEM] * 2,
        name="routed",
    )(received, incoming, gain[None], bias[None], target)


def exchange(parts):
    far = swap(parts[3], "dp", 2)
    return [parts[0], swap(parts[1], "dp", 1), swap(parts[2], "dp", 2), swap(far, "dp", 1)]


def on_device(
    tokens,
    ln1_gain,
    ln1_bias,
    qkv_weight,
    out_weight,
    layer_scale,
    segment_ids,
    positions,
    merge_index,
    merge_weight,
    owners,
    ln2_gain,
    ln2_bias,
):
    tensor_count = lax.axis_size("tensor")
    group_count = lax.axis_size("dp")
    place = lax.axis_index("tensor")
    width = out_weight.shape[1]
    merged_count = merge_index.shape[0]
    slots_cap = 2 * merged_count // group_count
    own_slots = group_count * slots_cap

    prepared = prepare(positions, segment_ids, ln1_gain, ln1_bias, tokens, qkv_weight)
    token_blocks, prepared = gather_blocks(tokens, "tensor", *prepared)
    cosine, sine, same, gain, bias, own_tokens, qkv_held = prepared
    attended, residual = attention(
        [own_tokens] + token_blocks[1:], gain, bias, qkv_held, cosine, sine, same, width
    )

    if group_count == 4 and 2 * own_slots == HD:
        owner_all = jnp.concatenate(exchange([owners[:, 0]] * group_count))[None]
        attended_blocks, (target, out_held) = gather_blocks(
            attended, "tensor", *targets(owner_all, group_count, out_weight)
        )
        hidden_columns, *picked = hidden_of(
            attended_blocks, out_held, layer_scale, residual, merge_index.T
        )
        arrived_rows = jnp.concatenate(exchange(picked))
        arrived_blocks, (merge_held,) = gather_blocks(arrived_rows, "tensor", fetch(merge_weight))
        outgoing = partial_rows(arrived_blocks, merge_held, target, group_count, own_slots)
        received, line = summed(exchange(outgoing), hidden_columns, tensor_count)
        line = lax.all_to_all(line, "tensor", split_axis=0, concat_axis=0, tiled=True)
        hidden, routed = routed_rows(received, line, ln2_gain, ln2_bias, target)
        return (hidden, routed)

    attended_blocks, _ = gather_blocks(attended, "tensor")
    projected = contract_blocks(attended_blocks, out_weight, place).astype(jnp.bfloat16)
    own_scale = lax.dynamic_slice_in_dim(layer_scale, place * width, width, axis=0)
    hidden_columns = (
        residual.astype(jnp.float32) + own_scale * projected.astype(jnp.float32)
    ).astype(jnp.bfloat16)
    hidden = lax.all_to_all(hidden_columns, "tensor", split_axis=0, concat_axis=1, tiled=True)
    all_hidden = lax.all_gather(hidden, "tensor", axis=0, tiled=True)
    merged = jnp.take(all_hidden, merge_index.reshape(-1), axis=0).reshape(merged_count, 4 * D)
    reduced = jnp.dot(
        merged,
        lax.all_gather(merge_weight, "dp", axis=0, tiled=True),
        preferred_element_type=jnp.float32,
    ).astype(jnp.bfloat16)
    target = owners[:, 0] * slots_cap + slots_of(owners[:, 0], group_count)
    placing = (
        jnp.arange(own_slots, dtype=jnp.int32)[:, None] == target[None, :]
    ).astype(jnp.bfloat16)
    outgoing = jnp.dot(placing, reduced, preferred_element_type=jnp.float32).astype(jnp.bfloat16)
    marks = jnp.sum(placing.astype(jnp.float32), axis=1).astype(jnp.bfloat16)
    incoming, arrived = (
        lax.all_to_all(outgoing, "dp", split_axis=0, concat_axis=0, tiled=True),
        lax.all_to_all(marks, "dp", split_axis=0, concat_axis=0, tiled=True),
    )
    received = incoming.astype(jnp.float32)
    row_total, row_squares = lax.psum(row_stats(received), "tensor")
    routed = (
        finish_norm(received, row_total, row_squares, ln2_gain, ln2_bias)
        * arrived.astype(jnp.float32)[:, None]
    ).astype(jnp.bfloat16)
    return (hidden, routed)


def solution(mesh):
    in_specs = (
        P(("dp", "tensor"), None),
        P(),
        P(),
        P(None, "tensor"),
        P(None, "tensor"),
        P(),
        P("dp"),
        P("dp", None),
        P("dp", None),
        P("dp", "tensor"),
        P("dp", None),
        P("tensor"),
        P("tensor"),
    )
    out_specs = (P(("dp", "tensor"), None), P("dp", "tensor"))
    return jax.shard_map(
        on_device, mesh=mesh, in_specs=in_specs, out_specs=out_specs, check_vma=False
    )
```

```python
import functools
import math

import jax
import jax.numpy as jnp
from jax import lax
from jax.experimental import pallas as pl
from jax.experimental.pallas import tpu as pltpu
from jax.sharding import PartitionSpec as P

D = 4096
HD = 128


def finish_norm(values, row_total, row_squares, gain, bias):
    mean_row = row_total / D
    var_row = row_squares / D - mean_row * mean_row
    return (values - mean_row[:, None]) * lax.rsqrt(var_row[:, None] + 1e-06) * gain + bias


def row_stats(values):
    return (jnp.sum(values, axis=1), jnp.sum(values * values, axis=1))


def swap(block, axis, bit):
    count = lax.axis_size(axis)
    return lax.ppermute(block, axis, [(i, i ^ bit) for i in range(count)])


def gather_blocks(block, axis, *beside):
    count = lax.axis_size(axis)
    bit = count // 2
    far, near, *beside = lax.optimization_barrier((swap(block, axis, bit), swap(block, axis, 1), *beside))
    blocks = {0: block, bit: far, 1: near}
    for index in range(2, bit):
        blocks[index] = swap(block, axis, index)
    for index in range(1, bit):
        blocks[index ^ bit] = swap(far, axis, index)
    return [blocks[index] for index in range(count)], beside


def contract_blocks(blocks, weight, place):
    depth = blocks[0].shape[1]
    total = None
    for index, block in enumerate(blocks):
        rows = lax.dynamic_slice_in_dim(weight, (place ^ index) * depth, depth, axis=0)
        term = jnp.dot(block, rows, preferred_element_type=jnp.float32)
        total = term if total is None else total + term
    return total


def slots_of(owner_of, group_count):
    one_hot = (owner_of[:, None] == jnp.arange(group_count, dtype=jnp.int32)[None, :]).astype(
        jnp.int32
    )
    before = jnp.cumsum(one_hot, axis=0) - one_hot
    return jnp.sum(before * one_hot, axis=1)


VMEM = pl.BlockSpec(memory_space=pltpu.VMEM)
HBM = pl.BlockSpec(memory_space=pltpu.HBM)
STRIPE = 512
LANES = 128


def column(row, width):
    return jnp.transpose(jnp.broadcast_to(row, (width, row.shape[1])))


def start_stripes(source, held, sems):
    copies = [
        pltpu.make_async_copy(
            source.at[pl.ds(index * STRIPE, STRIPE), :],
            held.at[pl.ds(index * STRIPE, STRIPE), :],
            sems.at[index],
        )
        for index in range(held.shape[0] // STRIPE)
    ]
    for copy in copies:
        copy.start()
    return copies


def fetch_kernel(weight_in, weight, sems):
    copies = start_stripes(weight_in, weight, sems)
    for copy in copies:
        copy.wait()


def fetch(weight):
    return pl.pallas_call(
        fetch_kernel,
        out_shape=jax.ShapeDtypeStruct(weight.shape, weight.dtype),
        in_specs=[HBM],
        out_specs=VMEM,
        scratch_shapes=[pltpu.SemaphoreType.DMA((weight.shape[0] // STRIPE,))],
        compiler_params=pltpu.CompilerParams(vmem_limit_bytes=24 * 2**20),
        cost_estimate=pl.CostEstimate(flops=0, bytes_accessed=weight.size * 4, transcendentals=0),
        name="fetch",
    )(weight)


def prepare_kernel(places, affine, tokens_in, cosine, sine, same, gain, bias, tokens):
    lane = lax.broadcasted_iota(jnp.int32, cosine.shape, 1)
    quarter = HD // 4
    frequency = jnp.exp((lane % quarter).astype(jnp.float32) * (-math.log(100.0) / quarter))
    rows = column(places[0:1, :].astype(jnp.float32), HD)
    columns = column(places[1:2, :].astype(jnp.float32), HD)
    angles = jnp.where(lane < 2 * quarter, rows, columns) * frequency
    cosine[...] = jnp.cos(angles)
    sines = jnp.sin(angles)
    sine[...] = jnp.where((lane & quarter) == 0, -sines, sines)
    ids = places[2:3, :].astype(jnp.float32)
    same[...] = (column(ids, ids.shape[1]) == ids).astype(jnp.float32)
    gain[...] = affine[0:1, :]
    bias[...] = affine[1:2, :]
    tokens[...] = tokens_in[...]


def prepare(positions, segments, gain, bias, tokens):
    seq = segments.shape[0]
    places = jnp.concatenate([positions.T, segments[None]])
    return pl.pallas_call(
        prepare_kernel,
        out_shape=[
            jax.ShapeDtypeStruct((seq, HD), jnp.float32),
            jax.ShapeDtypeStruct((seq, HD), jnp.float32),
            jax.ShapeDtypeStruct((seq, seq), jnp.float32),
            jax.ShapeDtypeStruct((1, D), jnp.float32),
            jax.ShapeDtypeStruct((1, D), jnp.float32),
            jax.ShapeDtypeStruct(tokens.shape, tokens.dtype),
        ],
        in_specs=[VMEM] * 3,
        out_specs=[VMEM] * 6,
        compiler_params=pltpu.CompilerParams(vmem_limit_bytes=24 * 2**20),
        name="prepare",
    )(places, jnp.stack([gain, bias]), tokens)


def attention_kernel(tensor_count, *refs):
    blocks = refs[:tensor_count]
    gain, bias, weight, cosine, sine, same_in, out, residual, normed = refs[tensor_count:]
    place = lax.axis_index("tensor")
    rows, head_count, width = blocks[0].shape[0], out.shape[1] // HD, residual.shape[1]
    lanes = pl.ds(pl.multiple_of(place * width, width), width)
    for index, block in enumerate(blocks):
        values = block[...].astype(jnp.float32)
        center = values - jnp.mean(values, axis=-1, keepdims=True)
        spread = jnp.mean(center * center, axis=-1, keepdims=True)
        value = center * lax.rsqrt(spread + 1e-06) * gain[...] + bias[...]
        at = pl.ds(pl.multiple_of((place ^ index) * rows, rows), rows)
        normed[at, :] = value.astype(jnp.bfloat16)
        residual[at, :] = block[:, lanes]
    same = same_in[...] > 0.5
    low = (lax.broadcasted_iota(jnp.int32, cosine.shape, 1) & (HD // 4)) == 0

    def rotated(part):
        swapped = jnp.where(low, pltpu.roll(part, HD - HD // 4, 1), pltpu.roll(part, HD // 4, 1))
        return (part * cosine[...] + swapped * sine[...]).astype(jnp.bfloat16)

    for head in range(head_count):
        first = head * 3 * HD
        packed = jnp.dot(
            normed[...], weight[:, first : first + 3 * HD], preferred_element_type=jnp.float32
        )
        queries, keys = rotated(packed[:, :HD]), rotated(packed[:, HD : 2 * HD])
        values = packed[:, 2 * HD :].astype(jnp.bfloat16)
        scores = lax.dot_general(
            queries, keys, (((1,), (1,)), ((), ())), preferred_element_type=jnp.float32
        ) * (1.0 / math.sqrt(HD))
        scores = jnp.where(same, scores, -jnp.inf)
        weights = jnp.exp(scores - jnp.max(scores, axis=-1, keepdims=True))
        probs = (weights / jnp.sum(weights, axis=-1, keepdims=True)).astype(jnp.bfloat16)
        mixed = jnp.dot(probs, values, preferred_element_type=jnp.float32)
        out[:, head * HD : (head + 1) * HD] = mixed.astype(jnp.bfloat16)


def attention(blocks, gain, bias, weight, cosine, sine, same, width):
    rows = blocks[0].shape[0]
    seq, columns = rows * len(blocks), weight.shape[1]
    heads = columns // (3 * HD)
    return pl.pallas_call(
        functools.partial(attention_kernel, len(blocks)),
        out_shape=[
            jax.ShapeDtypeStruct((seq, heads * HD), jnp.bfloat16),
            jax.ShapeDtypeStruct((seq, width), jnp.bfloat16),
        ],
        in_specs=[VMEM] * (len(blocks) + 6),
        out_specs=[VMEM] * 2,
        scratch_shapes=[pltpu.VMEM((seq, D), jnp.bfloat16)],
        compiler_params=pltpu.CompilerParams(vmem_limit_bytes=24 * 2**20),
        cost_estimate=pl.CostEstimate(
            flops=2 * seq * D * columns, bytes_accessed=D * columns * 2, transcendentals=0
        ),
        name="attention",
    )(*blocks, gain, bias, weight, cosine, sine, same)


def block_product(blocks, weight):
    place = lax.axis_index("tensor")
    depth = blocks[0].shape[1]
    total = None
    for index, block in enumerate(blocks):
        rows = weight[pl.ds(pl.multiple_of((place ^ index) * depth, depth), depth), :]
        term = jnp.dot(block[...], rows, preferred_element_type=jnp.float32)
        total = term if total is None else total + term
    return total


def hidden_kernel(tensor_count, *refs):
    blocks = refs[:tensor_count]
    weight, scale, residual, pick, target, hidden, *picked = refs[tensor_count:]
    place, group = lax.axis_index("tensor"), lax.axis_index("dp")
    width, merged = hidden.shape[1], pick.shape[1]
    own_scale = scale[:, pl.ds(pl.multiple_of(place * width, width), width)]
    projected = block_product(blocks, weight).astype(jnp.bfloat16).astype(jnp.float32)
    result = (residual[...].astype(jnp.float32) + own_scale * projected).astype(jnp.bfloat16)
    hidden[...] = result
    ids = lax.broadcasted_iota(jnp.int32, (hidden.shape[0], merged), 0)
    lane = lax.broadcasted_iota(jnp.int32, (merged, LANES), 1)
    lines = jnp.broadcast_to(target[...], (merged, LANES))
    for index in range(4):
        chosen = (pick[pl.ds(group ^ index, 1), :] == ids).astype(jnp.bfloat16)
        rows = lax.dot_general(
            chosen, result, (((0,), (0,)), ((), ())), preferred_element_type=jnp.float32
        )
        at = pl.ds(index % 2 * merged, merged)
        picked[index // 2][at, :width] = rows.astype(jnp.bfloat16)
        stands = index % 2 * 2 + index // 2
        line = jnp.where(lane // merged == stands, lines, 0.0)
        picked[index // 2][at, width:] = line.astype(jnp.bfloat16)


def hidden_of(blocks, weight, scale, residual, pick, target):
    seq, width = residual.shape
    slots, merged = pick.shape
    return pl.pallas_call(
        functools.partial(hidden_kernel, len(blocks)),
        out_shape=[jax.ShapeDtypeStruct((seq, width), jnp.bfloat16)]
        + [jax.ShapeDtypeStruct((2 * merged, width + LANES), jnp.bfloat16)] * 2,
        in_specs=[VMEM] * (len(blocks) + 5),
        out_specs=[VMEM] * 3,
        compiler_params=pltpu.CompilerParams(vmem_limit_bytes=24 * 2**20),
        cost_estimate=pl.CostEstimate(
            flops=2 * seq * D * width, bytes_accessed=D * width * 2, transcendentals=0
        ),
        name="hidden",
    )(*blocks, weight, scale[None], residual, pick, target)


def targets_kernel(group_count, owners, weight_in, target, weight, sems):
    copies = start_stripes(weight_in, weight, sems)
    total = owners.shape[1]
    merged = total // group_count
    owner = jnp.broadcast_to(owners[...], (8, total))
    before = lax.broadcasted_iota(jnp.int32, (total, total), 0)
    after = lax.broadcasted_iota(jnp.int32, (total, total), 1)
    earlier = ((before < after) & (before // merged == after // merged)).astype(jnp.bfloat16)
    slot = jnp.zeros((8, total), jnp.float32)
    for index in range(group_count):
        named = (owner == index).astype(jnp.float32)
        count = jnp.dot(named.astype(jnp.bfloat16), earlier, preferred_element_type=jnp.float32)
        slot = slot + named * count
    cap = 2 * merged // group_count
    start = (owner * group_count + lax.axis_index("dp")) * cap
    target[...] = (start.astype(jnp.float32) + slot)[0:1]
    for copy in copies:
        copy.wait()


def targets(owners, group_count, weight):
    total = owners.shape[0] * group_count
    return pl.pallas_call(
        functools.partial(targets_kernel, group_count),
        out_shape=[
            jax.ShapeDtypeStruct((1, total), jnp.float32),
            jax.ShapeDtypeStruct(weight.shape, weight.dtype),
        ],
        in_specs=[VMEM, HBM],
        out_specs=[VMEM] * 2,
        scratch_shapes=[pltpu.SemaphoreType.DMA((weight.shape[0] // STRIPE,))],
        compiler_params=pltpu.CompilerParams(vmem_limit_bytes=24 * 2**20),
        cost_estimate=pl.CostEstimate(flops=0, bytes_accessed=weight.size * 4, transcendentals=0),
        name="targets",
    )(jnp.tile(owners[:, 0], group_count)[None], weight)


def partial_kernel(tensor_count, *refs):
    blocks = refs[:tensor_count]
    weight, lines, filled, *outs = refs[tensor_count:]
    group = lax.axis_index("dp")
    partial = block_product(blocks, weight).astype(jnp.bfloat16)
    cap, merged = outs[0].shape[0], lines.shape[0] // len(outs)
    target = lines[0:1, :].astype(jnp.float32)
    for index in range(1, len(outs)):
        target = target + lines[index * merged : index * merged + 1, :].astype(jnp.float32)
    slot = lax.broadcasted_iota(jnp.int32, (cap, target.shape[1]), 0)
    for index, out in enumerate(outs):
        placing = (slot + (group ^ index) * cap == target.astype(jnp.int32)).astype(jnp.float32)
        if index == 0:
            used = jnp.sum(placing, axis=1, keepdims=True)
            filled[...] = jnp.broadcast_to(used, filled.shape)
        out[...] = jnp.dot(
            placing.astype(jnp.bfloat16), partial, preferred_element_type=jnp.float32
        ).astype(jnp.bfloat16)


def partial_rows(blocks, weight, lines, group_count, own_slots):
    seq, width = blocks[0].shape[0], weight.shape[1]
    return pl.pallas_call(
        functools.partial(partial_kernel, len(blocks)),
        out_shape=[jax.ShapeDtypeStruct((own_slots, LANES), jnp.float32)]
        + [jax.ShapeDtypeStruct((own_slots, width), jnp.bfloat16)] * group_count,
        in_specs=[VMEM] * (len(blocks) + 2),
        out_specs=[VMEM] * (1 + group_count),
        compiler_params=pltpu.CompilerParams(vmem_limit_bytes=24 * 2**20),
        cost_estimate=pl.CostEstimate(
            flops=2 * seq * D * width, bytes_accessed=D * width * 2, transcendentals=0
        ),
        name="partial",
    )(*blocks, weight, lines)


def summed_kernel(*refs):
    *parts, hidden, received, outgoing = refs
    total = parts[0][...].astype(jnp.float32)
    for part in parts[1:]:
        total = total + part[...].astype(jnp.float32)
    received[...] = total.astype(jnp.bfloat16)
    total = total.astype(jnp.bfloat16).astype(jnp.float32)
    sums = jnp.sum(total, axis=1, keepdims=True)
    squares = jnp.sum(total * total, axis=1, keepdims=True)
    both = jnp.concatenate([sums, squares], axis=0)
    lanes = both.shape[0]
    count, rows, _ = outgoing.shape
    width = hidden.shape[1]
    value = jnp.transpose(jnp.broadcast_to(both, (lanes, lanes)))[:rows]
    high = value.astype(jnp.bfloat16).astype(jnp.float32)
    rest = value - high
    middle = rest.astype(jnp.bfloat16).astype(jnp.float32)
    low = rest - middle
    row = lax.broadcasted_iota(jnp.int32, value.shape, 0)
    stats = jnp.where(row == 0, high, jnp.where(row == 1, middle, jnp.where(row == 2, low, 0.0)))
    stats = stats.astype(jnp.bfloat16)
    for index in range(count):
        outgoing[index, :, :width] = hidden[index * rows : (index + 1) * rows, :]
        outgoing[index, :, width:] = stats


def summed(parts, hidden, tensor_count):
    own_slots, width = parts[0].shape
    rows = hidden.shape[0] // tensor_count
    return pl.pallas_call(
        summed_kernel,
        out_shape=[
            jax.ShapeDtypeStruct((own_slots, width), jnp.bfloat16),
            jax.ShapeDtypeStruct((tensor_count, rows, width + 2 * own_slots), jnp.bfloat16),
        ],
        in_specs=[VMEM] * (len(parts) + 1),
        out_specs=[VMEM] * 2,
        compiler_params=pltpu.CompilerParams(vmem_limit_bytes=8 * 2**20),
        name="summed",
    )(*parts, hidden)


def routed_kernel(received, incoming, gain, bias, filled, hidden, out):
    own_slots, width = received.shape
    stats = jnp.sum(incoming[:, :, width:].astype(jnp.float32), axis=0)
    line = stats[0:1] + stats[1:2] + stats[2:3]
    totals = column(line, line.shape[1])
    mean_row = totals[:own_slots, 0:1] * (1.0 / D)
    var_row = totals[own_slots:, 0:1] * (1.0 / D) - mean_row * mean_row
    value = (received[...].astype(jnp.float32) - mean_row) * lax.rsqrt(var_row + 1e-06)
    value = (value * gain[...] + bias[...]) * filled[:, 0:1]
    out[...] = value.astype(jnp.bfloat16)
    for index in range(incoming.shape[0]):
        hidden[:, index * width : (index + 1) * width] = incoming[index, :, :width]


def routed_rows(received, incoming, gain, bias, filled):
    return pl.pallas_call(
        routed_kernel,
        out_shape=[
            jax.ShapeDtypeStruct((incoming.shape[1], D), jnp.bfloat16),
            jax.ShapeDtypeStruct(received.shape, jnp.bfloat16),
        ],
        in_specs=[VMEM] * 5,
        out_specs=[VMEM] * 2,
        compiler_params=pltpu.CompilerParams(vmem_limit_bytes=8 * 2**20),
        name="routed",
    )(received, incoming, gain[None], bias[None], filled)


def exchange(parts):
    return [parts[0]] + [swap(part, "dp", index) for index, part in enumerate(parts) if index]


def gather_picked(picked):
    dp, tensor = lax.axis_size("dp"), lax.axis_size("tensor")
    far = tensor // 2
    rows = picked[0].shape[0]
    width = picked[0].shape[1] - LANES
    own, other = picked[0], picked[1]

    def hop(part, group_bit, place_bit):
        pairs = [
            (g * tensor + t, (g ^ group_bit) * tensor + (t ^ place_bit))
            for g in range(dp)
            for t in range(tensor)
        ]
        return lax.ppermute(part, ("dp", "tensor"), pairs)

    half = rows // 2
    block = jnp.concatenate([own[:half], hop(other[:half], 2, 0), hop(own[half:], 1, 0), hop(other[half:], 3, 0)])
    blocks, _ = gather_blocks(block[:, :width], "tensor")
    return blocks, block[:, width:]


def on_device(
    tokens,
    ln1_gain,
    ln1_bias,
    qkv_weight,
    out_weight,
    layer_scale,
    segment_ids,
    positions,
    merge_index,
    merge_weight,
    owners,
    ln2_gain,
    ln2_bias,
):
    tensor_count = lax.axis_size("tensor")
    group_count = lax.axis_size("dp")
    place = lax.axis_index("tensor")
    width = out_weight.shape[1]
    merged_count = merge_index.shape[0]
    slots_cap = 2 * merged_count // group_count
    own_slots = group_count * slots_cap

    prepared = prepare(positions, segment_ids, ln1_gain, ln1_bias, tokens)
    token_blocks, prepared = gather_blocks(tokens, "tensor", *prepared)
    cosine, sine, same, gain, bias, own_tokens = prepared
    attended, residual = attention(
        [own_tokens] + token_blocks[1:], gain, bias, fetch(qkv_weight), cosine, sine, same, width
    )

    if group_count == 4 and 2 * own_slots == HD:
        attended_blocks, _ = gather_blocks(attended, "tensor")
        target, out_held = targets(owners, group_count, out_weight)
        hidden_columns, *picked = hidden_of(
            attended_blocks, out_held, layer_scale, residual, merge_index.T, target
        )
        arrived_blocks, lines = gather_picked(picked)
        filled, *outgoing = partial_rows(
            arrived_blocks, fetch(merge_weight), lines, group_count, own_slots
        )
        received, line = summed(exchange(outgoing), hidden_columns, tensor_count)
        line = lax.all_to_all(line, "tensor", split_axis=0, concat_axis=0, tiled=True)
        hidden, routed = routed_rows(received, line, ln2_gain, ln2_bias, filled)
        return (hidden, routed)

    attended_blocks, _ = gather_blocks(attended, "tensor")
    projected = contract_blocks(attended_blocks, out_weight, place).astype(jnp.bfloat16)
    own_scale = lax.dynamic_slice_in_dim(layer_scale, place * width, width, axis=0)
    hidden_columns = (
        residual.astype(jnp.float32) + own_scale * projected.astype(jnp.float32)
    ).astype(jnp.bfloat16)
    hidden = lax.all_to_all(hidden_columns, "tensor", split_axis=0, concat_axis=1, tiled=True)
    all_hidden = lax.all_gather(hidden, "tensor", axis=0, tiled=True)
    merged = jnp.take(all_hidden, merge_index.reshape(-1), axis=0).reshape(merged_count, 4 * D)
    reduced = jnp.dot(
        merged,
        lax.all_gather(merge_weight, "dp", axis=0, tiled=True),
        preferred_element_type=jnp.float32,
    ).astype(jnp.bfloat16)
    target = owners[:, 0] * slots_cap + slots_of(owners[:, 0], group_count)
    placing = (
        jnp.arange(own_slots, dtype=jnp.int32)[:, None] == target[None, :]
    ).astype(jnp.bfloat16)
    outgoing = jnp.dot(placing, reduced, preferred_element_type=jnp.float32).astype(jnp.bfloat16)
    marks = jnp.sum(placing.astype(jnp.float32), axis=1).astype(jnp.bfloat16)
    incoming, arrived = (
        lax.all_to_all(outgoing, "dp", split_axis=0, concat_axis=0, tiled=True),
        lax.all_to_all(marks, "dp", split_axis=0, concat_axis=0, tiled=True),
    )
    received = incoming.astype(jnp.float32)
    row_total, row_squares = lax.psum(row_stats(received), "tensor")
    routed = (
        finish_norm(received, row_total, row_squares, ln2_gain, ln2_bias)
        * arrived.astype(jnp.float32)[:, None]
    ).astype(jnp.bfloat16)
    return (hidden, routed)


def solution(mesh):
    in_specs = (
        P(("dp", "tensor"), None),
        P(),
        P(),
        P(None, "tensor"),
        P(None, "tensor"),
        P(),
        P("dp"),
        P("dp", None),
        P("dp", None),
        P("dp", "tensor"),
        P("dp", None),
        P("tensor"),
        P("tensor"),
    )
    out_specs = (P(("dp", "tensor"), None), P("dp", "tensor"))
    return jax.shard_map(
        on_device, mesh=mesh, in_specs=in_specs, out_specs=out_specs, check_vma=False
    )
```

```python
import functools
import math

import jax
import jax.numpy as jnp
from jax import lax
from jax.experimental import pallas as pl
from jax.experimental.pallas import tpu as pltpu
from jax.sharding import PartitionSpec as P

D = 4096
HD = 128


def finish_norm(values, row_total, row_squares, gain, bias):
    mean_row = row_total / D
    var_row = row_squares / D - mean_row * mean_row
    return (values - mean_row[:, None]) * lax.rsqrt(var_row[:, None] + 1e-06) * gain + bias


def row_stats(values):
    return (jnp.sum(values, axis=1), jnp.sum(values * values, axis=1))


def swap(block, axis, bit):
    count = lax.axis_size(axis)
    return lax.ppermute(block, axis, [(i, i ^ bit) for i in range(count)])


def gather_blocks(block, axis, *beside):
    count = lax.axis_size(axis)
    bit = count // 2
    early = bit // 2
    far, near, *beside = lax.optimization_barrier(
        (swap(block, axis, bit), swap(block, axis, early), *beside)
    )
    blocks = {0: block, bit: far, early: near}
    for index in range(1, bit):
        if index != early:
            blocks[index] = swap(block, axis, index)
    for index in range(1, bit):
        blocks[index ^ bit] = swap(far, axis, index)
    return [blocks[index] for index in range(count)], beside


def contract_blocks(blocks, weight, place):
    depth = blocks[0].shape[1]
    total = None
    for index, block in enumerate(blocks):
        rows = lax.dynamic_slice_in_dim(weight, (place ^ index) * depth, depth, axis=0)
        term = jnp.dot(block, rows, preferred_element_type=jnp.float32)
        total = term if total is None else total + term
    return total


def slots_of(owner_of, group_count):
    one_hot = (owner_of[:, None] == jnp.arange(group_count, dtype=jnp.int32)[None, :]).astype(
        jnp.int32
    )
    before = jnp.cumsum(one_hot, axis=0) - one_hot
    return jnp.sum(before * one_hot, axis=1)


VMEM = pl.BlockSpec(memory_space=pltpu.VMEM)
HBM = pl.BlockSpec(memory_space=pltpu.HBM)
STRIPE = 512
LANES = 128


def column(row, width):
    return jnp.transpose(jnp.broadcast_to(row, (width, row.shape[1])))


def start_stripes(source, held, sems):
    copies = [
        pltpu.make_async_copy(
            source.at[pl.ds(index * STRIPE, STRIPE), :],
            held.at[pl.ds(index * STRIPE, STRIPE), :],
            sems.at[index],
        )
        for index in range(held.shape[0] // STRIPE)
    ]
    for copy in copies:
        copy.start()
    return copies


def fetch_kernel(weight_in, weight, sems):
    copies = start_stripes(weight_in, weight, sems)
    for copy in copies:
        copy.wait()


def fetch(weight):
    return pl.pallas_call(
        fetch_kernel,
        out_shape=jax.ShapeDtypeStruct(weight.shape, weight.dtype),
        in_specs=[HBM],
        out_specs=VMEM,
        scratch_shapes=[pltpu.SemaphoreType.DMA((weight.shape[0] // STRIPE,))],
        compiler_params=pltpu.CompilerParams(vmem_limit_bytes=24 * 2**20),
        cost_estimate=pl.CostEstimate(flops=0, bytes_accessed=weight.size * 4, transcendentals=0),
        name="fetch",
    )(weight)


def prepare_kernel(places, affine, tokens_in, cosine, sine, same, gain, bias, tokens):
    lane = lax.broadcasted_iota(jnp.int32, cosine.shape, 1)
    quarter = HD // 4
    frequency = jnp.exp((lane % quarter).astype(jnp.float32) * (-math.log(100.0) / quarter))
    rows = column(places[0:1, :].astype(jnp.float32), HD)
    columns = column(places[1:2, :].astype(jnp.float32), HD)
    angles = jnp.where(lane < 2 * quarter, rows, columns) * frequency
    cosine[...] = jnp.cos(angles)
    sines = jnp.sin(angles)
    sine[...] = jnp.where((lane & quarter) == 0, -sines, sines)
    ids = places[2:3, :].astype(jnp.float32)
    same[...] = (column(ids, ids.shape[1]) == ids).astype(jnp.float32)
    gain[...] = affine[0:1, :]
    bias[...] = affine[1:2, :]
    tokens[...] = tokens_in[...]


def prepare(positions, segments, gain, bias, tokens):
    seq = segments.shape[0]
    places = jnp.concatenate([positions.T, segments[None]])
    return pl.pallas_call(
        prepare_kernel,
        out_shape=[
            jax.ShapeDtypeStruct((seq, HD), jnp.float32),
            jax.ShapeDtypeStruct((seq, HD), jnp.float32),
            jax.ShapeDtypeStruct((seq, seq), jnp.float32),
            jax.ShapeDtypeStruct((1, D), jnp.float32),
            jax.ShapeDtypeStruct((1, D), jnp.float32),
            jax.ShapeDtypeStruct(tokens.shape, tokens.dtype),
        ],
        in_specs=[VMEM] * 3,
        out_specs=[VMEM] * 6,
        compiler_params=pltpu.CompilerParams(vmem_limit_bytes=24 * 2**20),
        name="prepare",
    )(places, jnp.stack([gain, bias]), tokens)


def attention_kernel(tensor_count, *refs):
    blocks = refs[:tensor_count]
    gain, bias, weight, cosine, sine, same_in, out, residual, normed = refs[tensor_count:]
    place = lax.axis_index("tensor")
    rows, head_count, width = blocks[0].shape[0], out.shape[1] // HD, residual.shape[1]
    lanes = pl.ds(pl.multiple_of(place * width, width), width)
    for index, block in enumerate(blocks):
        values = block[...].astype(jnp.float32)
        center = values - jnp.mean(values, axis=-1, keepdims=True)
        spread = jnp.mean(center * center, axis=-1, keepdims=True)
        value = center * lax.rsqrt(spread + 1e-06) * gain[...] + bias[...]
        at = pl.ds(pl.multiple_of((place ^ index) * rows, rows), rows)
        normed[at, :] = value.astype(jnp.bfloat16)
        residual[at, :] = block[:, lanes]
    same = same_in[...] > 0.5
    low = (lax.broadcasted_iota(jnp.int32, cosine.shape, 1) & (HD // 4)) == 0

    def rotated(part):
        swapped = jnp.where(low, pltpu.roll(part, HD - HD // 4, 1), pltpu.roll(part, HD // 4, 1))
        return (part * cosine[...] + swapped * sine[...]).astype(jnp.bfloat16)

    packed = jnp.dot(normed[...], weight[...], preferred_element_type=jnp.float32)
    parts = [packed[:, at : at + HD] for at in range(0, packed.shape[1], HD)]
    queries, keys = [rotated(part) for part in parts[::3]], [rotated(part) for part in parts[1::3]]
    values = [part.astype(jnp.bfloat16) for part in parts[2::3]]
    scores = [
        lax.dot_general(
            query, key, (((1,), (1,)), ((), ())), preferred_element_type=jnp.float32
        )
        * (1.0 / math.sqrt(HD))
        for query, key in zip(queries, keys)
    ]
    scores = [jnp.where(same, score, -jnp.inf) for score in scores]
    weights = [jnp.exp(score - jnp.max(score, axis=-1, keepdims=True)) for score in scores]
    probs = [
        (part / jnp.sum(part, axis=-1, keepdims=True)).astype(jnp.bfloat16)
        for part in weights
    ]
    for head in range(head_count):
        mixed = jnp.dot(probs[head], values[head], preferred_element_type=jnp.float32)
        out[:, head * HD : (head + 1) * HD] = mixed.astype(jnp.bfloat16)


def attention(blocks, gain, bias, weight, cosine, sine, same, width):
    rows = blocks[0].shape[0]
    seq, columns = rows * len(blocks), weight.shape[1]
    heads = columns // (3 * HD)
    return pl.pallas_call(
        functools.partial(attention_kernel, len(blocks)),
        out_shape=[
            jax.ShapeDtypeStruct((seq, heads * HD), jnp.bfloat16),
            jax.ShapeDtypeStruct((seq, width), jnp.bfloat16),
        ],
        in_specs=[VMEM] * (len(blocks) + 6),
        out_specs=[VMEM] * 2,
        scratch_shapes=[pltpu.VMEM((seq, D), jnp.bfloat16)],
        compiler_params=pltpu.CompilerParams(vmem_limit_bytes=24 * 2**20),
        cost_estimate=pl.CostEstimate(
            flops=2 * seq * D * columns, bytes_accessed=D * columns * 2, transcendentals=0
        ),
        name="attention",
    )(*blocks, gain, bias, weight, cosine, sine, same)


def block_product(blocks, weight):
    place = lax.axis_index("tensor")
    depth = blocks[0].shape[1]
    total = None
    for index, block in enumerate(blocks):
        rows = weight[pl.ds(pl.multiple_of((place ^ index) * depth, depth), depth), :]
        term = jnp.dot(block[...], rows, preferred_element_type=jnp.float32)
        total = term if total is None else total + term
    return total


def hidden_kernel(tensor_count, *refs):
    blocks = refs[:tensor_count]
    weight, scale, residual, pick, target, hidden, *picked = refs[tensor_count:]
    place, group = lax.axis_index("tensor"), lax.axis_index("dp")
    width, merged = hidden.shape[1], pick.shape[1]
    own_scale = scale[:, pl.ds(pl.multiple_of(place * width, width), width)]
    projected = block_product(blocks, weight).astype(jnp.bfloat16).astype(jnp.float32)
    result = (residual[...].astype(jnp.float32) + own_scale * projected).astype(jnp.bfloat16)
    hidden[...] = result
    ids = lax.broadcasted_iota(jnp.int32, (hidden.shape[0], merged), 0)
    lane = lax.broadcasted_iota(jnp.int32, (merged, LANES), 1)
    lines = jnp.broadcast_to(target[...], (merged, LANES))
    for index in range(4):
        chosen = (pick[pl.ds(group ^ index, 1), :] == ids).astype(jnp.bfloat16)
        rows = lax.dot_general(
            chosen, result, (((0,), (0,)), ((), ())), preferred_element_type=jnp.float32
        )
        at = pl.ds(index % 2 * merged, merged)
        picked[index // 2][at, :width] = rows.astype(jnp.bfloat16)
        stands = index % 2 * 2 + index // 2
        line = jnp.where(lane // merged == stands, lines, 0.0)
        picked[index // 2][at, width:] = line.astype(jnp.bfloat16)


def hidden_of(blocks, weight, scale, residual, pick, target):
    seq, width = residual.shape
    slots, merged = pick.shape
    return pl.pallas_call(
        functools.partial(hidden_kernel, len(blocks)),
        out_shape=[jax.ShapeDtypeStruct((seq, width), jnp.bfloat16)]
        + [jax.ShapeDtypeStruct((2 * merged, width + LANES), jnp.bfloat16)] * 2,
        in_specs=[VMEM] * (len(blocks) + 5),
        out_specs=[VMEM] * 3,
        compiler_params=pltpu.CompilerParams(vmem_limit_bytes=24 * 2**20),
        cost_estimate=pl.CostEstimate(
            flops=2 * seq * D * width, bytes_accessed=D * width * 2, transcendentals=0
        ),
        name="hidden",
    )(*blocks, weight, scale[None], residual, pick, target)


def targets_kernel(group_count, owners, weight_in, target, weight, sems):
    copies = start_stripes(weight_in, weight, sems)
    total = owners.shape[1]
    merged = total // group_count
    owner = jnp.broadcast_to(owners[...], (8, total))
    before = lax.broadcasted_iota(jnp.int32, (total, total), 0)
    after = lax.broadcasted_iota(jnp.int32, (total, total), 1)
    earlier = ((before < after) & (before // merged == after // merged)).astype(jnp.bfloat16)
    slot = jnp.zeros((8, total), jnp.float32)
    for index in range(group_count):
        named = (owner == index).astype(jnp.float32)
        count = jnp.dot(named.astype(jnp.bfloat16), earlier, preferred_element_type=jnp.float32)
        slot = slot + named * count
    cap = 2 * merged // group_count
    start = (owner * group_count + lax.axis_index("dp")) * cap
    target[...] = (start.astype(jnp.float32) + slot)[0:1]
    for copy in copies:
        copy.wait()


def targets(owners, group_count, weight):
    total = owners.shape[0] * group_count
    return pl.pallas_call(
        functools.partial(targets_kernel, group_count),
        out_shape=[
            jax.ShapeDtypeStruct((1, total), jnp.float32),
            jax.ShapeDtypeStruct(weight.shape, weight.dtype),
        ],
        in_specs=[VMEM, HBM],
        out_specs=[VMEM] * 2,
        scratch_shapes=[pltpu.SemaphoreType.DMA((weight.shape[0] // STRIPE,))],
        compiler_params=pltpu.CompilerParams(vmem_limit_bytes=24 * 2**20),
        cost_estimate=pl.CostEstimate(flops=0, bytes_accessed=weight.size * 4, transcendentals=0),
        name="targets",
    )(jnp.tile(owners[:, 0], group_count)[None], weight)


def partial_kernel(tensor_count, *refs):
    blocks = refs[:tensor_count]
    weight, lines, filled, *outs = refs[tensor_count:]
    group = lax.axis_index("dp")
    partial = block_product(blocks, weight).astype(jnp.bfloat16)
    cap, merged = outs[0].shape[0], lines.shape[0] // len(outs)
    target = lines[0:1, :].astype(jnp.float32)
    for index in range(1, len(outs)):
        target = target + lines[index * merged : index * merged + 1, :].astype(jnp.float32)
    slot = lax.broadcasted_iota(jnp.int32, (cap, target.shape[1]), 0)
    for index, out in enumerate(outs):
        placing = (slot + (group ^ index) * cap == target.astype(jnp.int32)).astype(jnp.float32)
        if index == 0:
            used = jnp.sum(placing, axis=1, keepdims=True)
            filled[...] = jnp.broadcast_to(used, filled.shape)
        out[...] = jnp.dot(
            placing.astype(jnp.bfloat16), partial, preferred_element_type=jnp.float32
        ).astype(jnp.bfloat16)


def partial_rows(blocks, weight, lines, group_count, own_slots):
    seq, width = blocks[0].shape[0], weight.shape[1]
    return pl.pallas_call(
        functools.partial(partial_kernel, len(blocks)),
        out_shape=[jax.ShapeDtypeStruct((own_slots, LANES), jnp.float32)]
        + [jax.ShapeDtypeStruct((own_slots, width), jnp.bfloat16)] * group_count,
        in_specs=[VMEM] * (len(blocks) + 2),
        out_specs=[VMEM] * (1 + group_count),
        compiler_params=pltpu.CompilerParams(vmem_limit_bytes=24 * 2**20),
        cost_estimate=pl.CostEstimate(
            flops=2 * seq * D * width, bytes_accessed=D * width * 2, transcendentals=0
        ),
        name="partial",
    )(*blocks, weight, lines)


def summed_kernel(*refs):
    *parts, hidden, received, outgoing = refs
    total = parts[0][...].astype(jnp.float32)
    for part in parts[1:]:
        total = total + part[...].astype(jnp.float32)
    received[...] = total.astype(jnp.bfloat16)
    total = total.astype(jnp.bfloat16).astype(jnp.float32)
    sums = jnp.sum(total, axis=1, keepdims=True)
    squares = jnp.sum(total * total, axis=1, keepdims=True)
    both = jnp.concatenate([sums, squares], axis=0)
    lanes = both.shape[0]
    count, rows, _ = outgoing.shape
    width = hidden.shape[1]
    value = jnp.transpose(jnp.broadcast_to(both, (lanes, lanes)))[:rows]
    high = value.astype(jnp.bfloat16).astype(jnp.float32)
    rest = value - high
    middle = rest.astype(jnp.bfloat16).astype(jnp.float32)
    low = rest - middle
    row = lax.broadcasted_iota(jnp.int32, value.shape, 0)
    stats = jnp.where(row == 0, high, jnp.where(row == 1, middle, jnp.where(row == 2, low, 0.0)))
    stats = stats.astype(jnp.bfloat16)
    for index in range(count):
        outgoing[index, :, :width] = hidden[index * rows : (index + 1) * rows, :]
        outgoing[index, :, width:] = stats


def summed(parts, hidden, tensor_count):
    own_slots, width = parts[0].shape
    rows = hidden.shape[0] // tensor_count
    return pl.pallas_call(
        summed_kernel,
        out_shape=[
            jax.ShapeDtypeStruct((own_slots, width), jnp.bfloat16),
            jax.ShapeDtypeStruct((tensor_count, rows, width + 2 * own_slots), jnp.bfloat16),
        ],
        in_specs=[VMEM] * (len(parts) + 1),
        out_specs=[VMEM] * 2,
        compiler_params=pltpu.CompilerParams(vmem_limit_bytes=8 * 2**20),
        name="summed",
    )(*parts, hidden)


def routed_kernel(received, incoming, gain, bias, filled, hidden, out):
    own_slots, width = received.shape
    stats = jnp.sum(incoming[:, :, width:].astype(jnp.float32), axis=0)
    line = stats[0:1] + stats[1:2] + stats[2:3]
    totals = column(line, line.shape[1])
    mean_row = totals[:own_slots, 0:1] * (1.0 / D)
    var_row = totals[own_slots:, 0:1] * (1.0 / D) - mean_row * mean_row
    value = (received[...].astype(jnp.float32) - mean_row) * lax.rsqrt(var_row + 1e-06)
    value = (value * gain[...] + bias[...]) * filled[:, 0:1]
    out[...] = value.astype(jnp.bfloat16)
    for index in range(incoming.shape[0]):
        hidden[:, index * width : (index + 1) * width] = incoming[index, :, :width]


def routed_rows(received, incoming, gain, bias, filled):
    return pl.pallas_call(
        routed_kernel,
        out_shape=[
            jax.ShapeDtypeStruct((incoming.shape[1], D), jnp.bfloat16),
            jax.ShapeDtypeStruct(received.shape, jnp.bfloat16),
        ],
        in_specs=[VMEM] * 5,
        out_specs=[VMEM] * 2,
        compiler_params=pltpu.CompilerParams(vmem_limit_bytes=8 * 2**20),
        name="routed",
    )(received, incoming, gain[None], bias[None], filled)


def exchange(parts):
    return [parts[0]] + [swap(part, "dp", index) for index, part in enumerate(parts) if index]


def gather_picked(picked, *beside):
    dp, tensor = lax.axis_size("dp"), lax.axis_size("tensor")
    far = tensor // 2
    rows = picked[0].shape[0]
    width = picked[0].shape[1] - LANES
    own, other = picked[0], picked[1]

    def hop(part, group_bit, place_bit):
        pairs = [
            (g * tensor + t, (g ^ group_bit) * tensor + (t ^ place_bit))
            for g in range(dp)
            for t in range(tensor)
        ]
        return lax.ppermute(part, ("dp", "tensor"), pairs)

    half = rows // 2
    block = jnp.concatenate(
        [own[:half], hop(other[:half], 2, 0), hop(own[half:], 1, 0), hop(other[half:], 3, 0)]
    )
    blocks, beside = gather_blocks(block[:, :width], "tensor", *beside)
    return blocks, block[:, width:], beside


def on_device(
    tokens,
    ln1_gain,
    ln1_bias,
    qkv_weight,
    out_weight,
    layer_scale,
    segment_ids,
    positions,
    merge_index,
    merge_weight,
    owners,
    ln2_gain,
    ln2_bias,
):
    tensor_count = lax.axis_size("tensor")
    group_count = lax.axis_size("dp")
    place = lax.axis_index("tensor")
    width = out_weight.shape[1]
    merged_count = merge_index.shape[0]
    slots_cap = 2 * merged_count // group_count
    own_slots = group_count * slots_cap

    prepared = prepare(positions, segment_ids, ln1_gain, ln1_bias, tokens)
    token_blocks, prepared = gather_blocks(tokens, "tensor", *prepared)
    cosine, sine, same, gain, bias, own_tokens = prepared
    attended, residual = attention(
        [own_tokens] + token_blocks[1:], gain, bias, fetch(qkv_weight), cosine, sine, same, width
    )

    if group_count == 4 and 2 * own_slots == HD:
        attended_blocks, _ = gather_blocks(attended, "tensor")
        target, out_held = targets(owners, group_count, out_weight)
        hidden_columns, *picked = hidden_of(
            attended_blocks, out_held, layer_scale, residual, merge_index.T, target
        )
        arrived_blocks, lines, _ = gather_picked(picked)
        filled, *outgoing = partial_rows(
            arrived_blocks, fetch(merge_weight), lines, group_count, own_slots
        )
        received, line = summed(exchange(outgoing), hidden_columns, tensor_count)
        line = lax.all_to_all(line, "tensor", split_axis=0, concat_axis=0, tiled=True)
        hidden, routed = routed_rows(received, line, ln2_gain, ln2_bias, filled)
        return (hidden, routed)

    attended_blocks, _ = gather_blocks(attended, "tensor")
    projected = contract_blocks(attended_blocks, out_weight, place).astype(jnp.bfloat16)
    own_scale = lax.dynamic_slice_in_dim(layer_scale, place * width, width, axis=0)
    hidden_columns = (
        residual.astype(jnp.float32) + own_scale * projected.astype(jnp.float32)
    ).astype(jnp.bfloat16)
    hidden = lax.all_to_all(hidden_columns, "tensor", split_axis=0, concat_axis=1, tiled=True)
    all_hidden = lax.all_gather(hidden, "tensor", axis=0, tiled=True)
    merged = jnp.take(all_hidden, merge_index.reshape(-1), axis=0).reshape(merged_count, 4 * D)
    reduced = jnp.dot(
        merged,
        lax.all_gather(merge_weight, "dp", axis=0, tiled=True),
        preferred_element_type=jnp.float32,
    ).astype(jnp.bfloat16)
    target = owners[:, 0] * slots_cap + slots_of(owners[:, 0], group_count)
    placing = (
        jnp.arange(own_slots, dtype=jnp.int32)[:, None] == target[None, :]
    ).astype(jnp.bfloat16)
    outgoing = jnp.dot(placing, reduced, preferred_element_type=jnp.float32).astype(jnp.bfloat16)
    marks = jnp.sum(placing.astype(jnp.float32), axis=1).astype(jnp.bfloat16)
    incoming, arrived = (
        lax.all_to_all(outgoing, "dp", split_axis=0, concat_axis=0, tiled=True),
        lax.all_to_all(marks, "dp", split_axis=0, concat_axis=0, tiled=True),
    )
    received = incoming.astype(jnp.float32)
    row_total, row_squares = lax.psum(row_stats(received), "tensor")
    routed = (
        finish_norm(received, row_total, row_squares, ln2_gain, ln2_bias)
        * arrived.astype(jnp.float32)[:, None]
    ).astype(jnp.bfloat16)
    return (hidden, routed)


def solution(mesh):
    in_specs = (
        P(("dp", "tensor"), None),
        P(),
        P(),
        P(None, "tensor"),
        P(None, "tensor"),
        P(),
        P("dp"),
        P("dp", None),
        P("dp", None),
        P("dp", "tensor"),
        P("dp", None),
        P("tensor"),
        P("tensor"),
    )
    out_specs = (P(("dp", "tensor"), None), P("dp", "tensor"))
    return jax.shard_map(
        on_device, mesh=mesh, in_specs=in_specs, out_specs=out_specs, check_vma=False
    )
```

```python
import functools
import math

import jax
import jax.numpy as jnp
from jax import lax
from jax.experimental import pallas as pl
from jax.experimental.pallas import tpu as pltpu
from jax.sharding import PartitionSpec as P

D = 4096
HD = 128


def finish_norm(values, row_total, row_squares, gain, bias):
    mean_row = row_total / D
    var_row = row_squares / D - mean_row * mean_row
    return (values - mean_row[:, None]) * lax.rsqrt(var_row[:, None] + 1e-06) * gain + bias


def row_stats(values):
    return (jnp.sum(values, axis=1), jnp.sum(values * values, axis=1))


def swap(block, axis, bit):
    count = lax.axis_size(axis)
    return lax.ppermute(block, axis, [(i, i ^ bit) for i in range(count)])


def gather_blocks(block, axis, early, *beside):
    count = lax.axis_size(axis)
    bit = count // 2
    far = swap(block, axis, bit)
    blocks = {index: swap(block, axis, index) for index in early}
    far, *held = lax.optimization_barrier((far, *blocks.values(), *beside))
    blocks, beside = dict(zip(early, held)), held[len(early) :]
    blocks.update({0: block, bit: far})
    for index in range(1, bit):
        if index not in early:
            blocks[index] = swap(block, axis, index)
    for index in range(1, bit):
        blocks[index ^ bit] = swap(far, axis, index)
    return [blocks[index] for index in range(count)], beside


def contract_blocks(blocks, weight, place):
    depth = blocks[0].shape[1]
    total = None
    for index, block in enumerate(blocks):
        rows = lax.dynamic_slice_in_dim(weight, (place ^ index) * depth, depth, axis=0)
        term = jnp.dot(block, rows, preferred_element_type=jnp.float32)
        total = term if total is None else total + term
    return total


def slots_of(owner_of, group_count):
    one_hot = (owner_of[:, None] == jnp.arange(group_count, dtype=jnp.int32)[None, :]).astype(
        jnp.int32
    )
    before = jnp.cumsum(one_hot, axis=0) - one_hot
    return jnp.sum(before * one_hot, axis=1)


VMEM = pl.BlockSpec(memory_space=pltpu.VMEM)
HBM = pl.BlockSpec(memory_space=pltpu.HBM)
STRIPE = 512
LANES = 128


def column(row, width):
    return jnp.transpose(jnp.broadcast_to(row, (width, row.shape[1])))


def start_stripes(source, held, sems):
    copies = [
        pltpu.make_async_copy(
            source.at[pl.ds(index * STRIPE, STRIPE), :],
            held.at[pl.ds(index * STRIPE, STRIPE), :],
            sems.at[index],
        )
        for index in range(held.shape[0] // STRIPE)
    ]
    for copy in copies:
        copy.start()
    return copies


def fetch_kernel(weight_in, weight, sems):
    copies = start_stripes(weight_in, weight, sems)
    for copy in copies:
        copy.wait()


def fetch(weight):
    return pl.pallas_call(
        fetch_kernel,
        out_shape=jax.ShapeDtypeStruct(weight.shape, weight.dtype),
        in_specs=[HBM],
        out_specs=VMEM,
        scratch_shapes=[pltpu.SemaphoreType.DMA((weight.shape[0] // STRIPE,))],
        compiler_params=pltpu.CompilerParams(vmem_limit_bytes=24 * 2**20),
        cost_estimate=pl.CostEstimate(flops=0, bytes_accessed=weight.size * 4, transcendentals=0),
        name="fetch",
    )(weight)


def prepare_kernel(places, affine, tokens_in, cosine, sine, same, gain, bias, tokens):
    lane = lax.broadcasted_iota(jnp.int32, cosine.shape, 1)
    quarter = HD // 4
    frequency = jnp.exp((lane % quarter).astype(jnp.float32) * (-math.log(100.0) / quarter))
    rows = column(places[0:1, :].astype(jnp.float32), HD)
    columns = column(places[1:2, :].astype(jnp.float32), HD)
    angles = jnp.where(lane < 2 * quarter, rows, columns) * frequency
    cosine[...] = jnp.cos(angles)
    sines = jnp.sin(angles)
    sine[...] = jnp.where((lane & quarter) == 0, -sines, sines)
    ids = places[2:3, :].astype(jnp.float32)
    same[...] = (column(ids, ids.shape[1]) == ids).astype(jnp.float32)
    gain[...] = affine[0:1, :]
    bias[...] = affine[1:2, :]
    tokens[...] = tokens_in[...]


def prepare(positions, segments, gain, bias, tokens):
    seq = segments.shape[0]
    places = jnp.concatenate([positions.T, segments[None]])
    return pl.pallas_call(
        prepare_kernel,
        out_shape=[
            jax.ShapeDtypeStruct((seq, HD), jnp.float32),
            jax.ShapeDtypeStruct((seq, HD), jnp.float32),
            jax.ShapeDtypeStruct((seq, seq), jnp.float32),
            jax.ShapeDtypeStruct((1, D), jnp.float32),
            jax.ShapeDtypeStruct((1, D), jnp.float32),
            jax.ShapeDtypeStruct(tokens.shape, tokens.dtype),
        ],
        in_specs=[VMEM] * 3,
        out_specs=[VMEM] * 6,
        compiler_params=pltpu.CompilerParams(vmem_limit_bytes=24 * 2**20),
        name="prepare",
    )(places, jnp.stack([gain, bias]), tokens)


def attention_kernel(tensor_count, *refs):
    blocks = refs[:tensor_count]
    gain, bias, weight, cosine, sine, same_in, out, residual, normed = refs[tensor_count:]
    place = lax.axis_index("tensor")
    rows, head_count, width = blocks[0].shape[0], out.shape[1] // HD, residual.shape[1]
    lanes = pl.ds(pl.multiple_of(place * width, width), width)
    for index, block in enumerate(blocks):
        values = block[...].astype(jnp.float32)
        center = values - jnp.mean(values, axis=-1, keepdims=True)
        spread = jnp.mean(center * center, axis=-1, keepdims=True)
        value = center * lax.rsqrt(spread + 1e-06) * gain[...] + bias[...]
        at = pl.ds(pl.multiple_of((place ^ index) * rows, rows), rows)
        normed[at, :] = value.astype(jnp.bfloat16)
        residual[at, :] = block[:, lanes]
    same = same_in[...] > 0.5
    low = (lax.broadcasted_iota(jnp.int32, cosine.shape, 1) & (HD // 4)) == 0

    def rotated(part):
        swapped = jnp.where(low, pltpu.roll(part, HD - HD // 4, 1), pltpu.roll(part, HD // 4, 1))
        return (part * cosine[...] + swapped * sine[...]).astype(jnp.bfloat16)

    packed = jnp.dot(normed[...], weight[...], preferred_element_type=jnp.float32)
    parts = [packed[:, at : at + HD] for at in range(0, packed.shape[1], HD)]
    queries, keys = [rotated(part) for part in parts[::3]], [rotated(part) for part in parts[1::3]]
    values = [part.astype(jnp.bfloat16) for part in parts[2::3]]
    scores = [
        lax.dot_general(
            query, key, (((1,), (1,)), ((), ())), preferred_element_type=jnp.float32
        )
        * (1.0 / math.sqrt(HD))
        for query, key in zip(queries, keys)
    ]
    scores = [jnp.where(same, score, -jnp.inf) for score in scores]
    weights = [jnp.exp(score - jnp.max(score, axis=-1, keepdims=True)) for score in scores]
    probs = [
        (part / jnp.sum(part, axis=-1, keepdims=True)).astype(jnp.bfloat16)
        for part in weights
    ]
    for head in range(head_count):
        mixed = jnp.dot(probs[head], values[head], preferred_element_type=jnp.float32)
        out[:, head * HD : (head + 1) * HD] = mixed.astype(jnp.bfloat16)


def attention(blocks, gain, bias, weight, cosine, sine, same, width):
    rows = blocks[0].shape[0]
    seq, columns = rows * len(blocks), weight.shape[1]
    heads = columns // (3 * HD)
    return pl.pallas_call(
        functools.partial(attention_kernel, len(blocks)),
        out_shape=[
            jax.ShapeDtypeStruct((seq, heads * HD), jnp.bfloat16),
            jax.ShapeDtypeStruct((seq, width), jnp.bfloat16),
        ],
        in_specs=[VMEM] * (len(blocks) + 6),
        out_specs=[VMEM] * 2,
        scratch_shapes=[pltpu.VMEM((seq, D), jnp.bfloat16)],
        compiler_params=pltpu.CompilerParams(vmem_limit_bytes=24 * 2**20),
        cost_estimate=pl.CostEstimate(
            flops=2 * seq * D * columns, bytes_accessed=D * columns * 2, transcendentals=0
        ),
        name="attention",
    )(*blocks, gain, bias, weight, cosine, sine, same)


def block_product(blocks, weight, first=0):
    place = lax.axis_index("tensor")
    depth = blocks[0].shape[1]
    total = None
    for index, block in enumerate(blocks, first):
        rows = weight[pl.ds(pl.multiple_of((place ^ index) * depth, depth), depth), :]
        term = jnp.dot(block[...], rows, preferred_element_type=jnp.float32)
        total = term if total is None else total + term
    return total


def hidden_kernel(tensor_count, *refs):
    blocks = refs[:tensor_count]
    near, weight, scale, residual, pick, target, hidden, *picked = refs[tensor_count:]
    place, group = lax.axis_index("tensor"), lax.axis_index("dp")
    width, merged = hidden.shape[1], pick.shape[1]
    own_scale = scale[:, pl.ds(pl.multiple_of(place * width, width), width)]
    projected = near[...] + block_product(blocks, weight, tensor_count)
    projected = projected.astype(jnp.bfloat16).astype(jnp.float32)
    result = (residual[...].astype(jnp.float32) + own_scale * projected).astype(jnp.bfloat16)
    hidden[...] = result
    ids = lax.broadcasted_iota(jnp.int32, (hidden.shape[0], merged), 0)
    lane = lax.broadcasted_iota(jnp.int32, (merged, LANES), 1)
    lines = jnp.broadcast_to(target[...], (merged, LANES))
    for index in range(4):
        chosen = (pick[pl.ds(group ^ index, 1), :] == ids).astype(jnp.bfloat16)
        rows = lax.dot_general(
            chosen, result, (((0,), (0,)), ((), ())), preferred_element_type=jnp.float32
        )
        at = pl.ds(index % 2 * merged, merged)
        picked[index // 2][at, :width] = rows.astype(jnp.bfloat16)
        stands = index % 2 * 2 + index // 2
        line = jnp.where(lane // merged == stands, lines, 0.0)
        picked[index // 2][at, width:] = line.astype(jnp.bfloat16)


def hidden_of(blocks, near, weight, scale, residual, pick, target):
    seq, width = residual.shape
    slots, merged = pick.shape
    return pl.pallas_call(
        functools.partial(hidden_kernel, len(blocks)),
        out_shape=[jax.ShapeDtypeStruct((seq, width), jnp.bfloat16)]
        + [jax.ShapeDtypeStruct((2 * merged, width + LANES), jnp.bfloat16)] * 2,
        in_specs=[VMEM] * (len(blocks) + 6),
        out_specs=[VMEM] * 3,
        compiler_params=pltpu.CompilerParams(vmem_limit_bytes=24 * 2**20),
        cost_estimate=pl.CostEstimate(
            flops=2 * seq * D * width, bytes_accessed=D * width * 2, transcendentals=0
        ),
        name="hidden",
    )(*blocks, near, weight, scale[None], residual, pick, target)


def near_kernel(*refs):
    *blocks, weight_in, weight, total, sems = refs
    copies = start_stripes(weight_in, weight, sems)
    for copy in copies:
        copy.wait()
    total[...] = block_product(blocks, weight)


def near_product(blocks, weight):
    return pl.pallas_call(
        near_kernel,
        out_shape=[
            jax.ShapeDtypeStruct(weight.shape, weight.dtype),
            jax.ShapeDtypeStruct((blocks[0].shape[0], weight.shape[1]), jnp.float32),
        ],
        in_specs=[VMEM] * len(blocks) + [HBM],
        out_specs=[VMEM] * 2,
        scratch_shapes=[pltpu.SemaphoreType.DMA((weight.shape[0] // STRIPE,))],
        compiler_params=pltpu.CompilerParams(vmem_limit_bytes=24 * 2**20),
        cost_estimate=pl.CostEstimate(flops=0, bytes_accessed=weight.size * 4, transcendentals=0),
        name="near",
    )(*blocks, weight)


def targets_kernel(group_count, *refs):
    *blocks, owners, weight_in, target, weight, near, sems = refs
    copies = start_stripes(weight_in, weight, sems)
    total = owners.shape[1]
    merged = total // group_count
    owner = jnp.broadcast_to(owners[...], (8, total))
    before = lax.broadcasted_iota(jnp.int32, (total, total), 0)
    after = lax.broadcasted_iota(jnp.int32, (total, total), 1)
    earlier = ((before < after) & (before // merged == after // merged)).astype(jnp.bfloat16)
    slot = jnp.zeros((8, total), jnp.float32)
    for index in range(group_count):
        named = (owner == index).astype(jnp.float32)
        count = jnp.dot(named.astype(jnp.bfloat16), earlier, preferred_element_type=jnp.float32)
        slot = slot + named * count
    cap = 2 * merged // group_count
    start = (owner * group_count + lax.axis_index("dp")) * cap
    target[...] = (start.astype(jnp.float32) + slot)[0:1]
    for copy in copies:
        copy.wait()
    near[...] = block_product(blocks, weight)


def targets(owners, group_count, weight, blocks):
    total = owners.shape[0] * group_count
    return pl.pallas_call(
        functools.partial(targets_kernel, group_count),
        out_shape=[
            jax.ShapeDtypeStruct((1, total), jnp.float32),
            jax.ShapeDtypeStruct(weight.shape, weight.dtype),
            jax.ShapeDtypeStruct((blocks[0].shape[0], weight.shape[1]), jnp.float32),
        ],
        in_specs=[VMEM] * (len(blocks) + 1) + [HBM],
        out_specs=[VMEM] * 3,
        scratch_shapes=[pltpu.SemaphoreType.DMA((weight.shape[0] // STRIPE,))],
        compiler_params=pltpu.CompilerParams(vmem_limit_bytes=24 * 2**20),
        cost_estimate=pl.CostEstimate(flops=0, bytes_accessed=weight.size * 4, transcendentals=0),
        name="targets",
    )(*blocks, jnp.tile(owners[:, 0], group_count)[None], weight)


def partial_kernel(tensor_count, *refs):
    blocks = refs[:tensor_count]
    near, weight, lines, filled, *outs = refs[tensor_count:]
    group = lax.axis_index("dp")
    partial = (near[...] + block_product(blocks, weight, tensor_count)).astype(jnp.bfloat16)
    cap, merged = outs[0].shape[0], lines.shape[0] // len(outs)
    target = lines[0:1, :].astype(jnp.float32)
    for index in range(1, len(outs)):
        target = target + lines[index * merged : index * merged + 1, :].astype(jnp.float32)
    slot = lax.broadcasted_iota(jnp.int32, (cap, target.shape[1]), 0)
    for index, out in enumerate(outs):
        placing = (slot + (group ^ index) * cap == target.astype(jnp.int32)).astype(jnp.float32)
        if index == 0:
            used = jnp.sum(placing, axis=1, keepdims=True)
            filled[...] = jnp.broadcast_to(used, filled.shape)
        out[...] = jnp.dot(
            placing.astype(jnp.bfloat16), partial, preferred_element_type=jnp.float32
        ).astype(jnp.bfloat16)


def partial_rows(blocks, near, weight, lines, group_count, own_slots):
    seq, width = blocks[0].shape[0], weight.shape[1]
    return pl.pallas_call(
        functools.partial(partial_kernel, len(blocks)),
        out_shape=[jax.ShapeDtypeStruct((own_slots, LANES), jnp.float32)]
        + [jax.ShapeDtypeStruct((own_slots, width), jnp.bfloat16)] * group_count,
        in_specs=[VMEM] * (len(blocks) + 3),
        out_specs=[VMEM] * (1 + group_count),
        compiler_params=pltpu.CompilerParams(vmem_limit_bytes=24 * 2**20),
        cost_estimate=pl.CostEstimate(
            flops=2 * seq * D * width, bytes_accessed=D * width * 2, transcendentals=0
        ),
        name="partial",
    )(*blocks, near, weight, lines)


def summed_kernel(*refs):
    *parts, hidden, received, outgoing = refs
    total = parts[0][...].astype(jnp.float32)
    for part in parts[1:]:
        total = total + part[...].astype(jnp.float32)
    received[...] = total.astype(jnp.bfloat16)
    total = total.astype(jnp.bfloat16).astype(jnp.float32)
    sums = jnp.sum(total, axis=1, keepdims=True)
    squares = jnp.sum(total * total, axis=1, keepdims=True)
    both = jnp.concatenate([sums, squares], axis=0)
    lanes = both.shape[0]
    count, rows, _ = outgoing.shape
    width = hidden.shape[1]
    value = jnp.transpose(jnp.broadcast_to(both, (lanes, lanes)))[:rows]
    high = value.astype(jnp.bfloat16).astype(jnp.float32)
    rest = value - high
    middle = rest.astype(jnp.bfloat16).astype(jnp.float32)
    low = rest - middle
    row = lax.broadcasted_iota(jnp.int32, value.shape, 0)
    stats = jnp.where(row == 0, high, jnp.where(row == 1, middle, jnp.where(row == 2, low, 0.0)))
    stats = stats.astype(jnp.bfloat16)
    for index in range(count):
        outgoing[index, :, :width] = hidden[index * rows : (index + 1) * rows, :]
        outgoing[index, :, width:] = stats


def summed(parts, hidden, tensor_count):
    own_slots, width = parts[0].shape
    rows = hidden.shape[0] // tensor_count
    return pl.pallas_call(
        summed_kernel,
        out_shape=[
            jax.ShapeDtypeStruct((own_slots, width), jnp.bfloat16),
            jax.ShapeDtypeStruct((tensor_count, rows, width + 2 * own_slots), jnp.bfloat16),
        ],
        in_specs=[VMEM] * (len(parts) + 1),
        out_specs=[VMEM] * 2,
        compiler_params=pltpu.CompilerParams(vmem_limit_bytes=8 * 2**20),
        name="summed",
    )(*parts, hidden)


def routed_kernel(received, incoming, gain, bias, filled, hidden, out):
    own_slots, width = received.shape
    stats = jnp.sum(incoming[:, :, width:].astype(jnp.float32), axis=0)
    line = stats[0:1] + stats[1:2] + stats[2:3]
    totals = column(line, line.shape[1])
    mean_row = totals[:own_slots, 0:1] * (1.0 / D)
    var_row = totals[own_slots:, 0:1] * (1.0 / D) - mean_row * mean_row
    value = (received[...].astype(jnp.float32) - mean_row) * lax.rsqrt(var_row + 1e-06)
    value = (value * gain[...] + bias[...]) * filled[:, 0:1]
    out[...] = value.astype(jnp.bfloat16)
    for index in range(incoming.shape[0]):
        hidden[:, index * width : (index + 1) * width] = incoming[index, :, :width]


def routed_rows(received, incoming, gain, bias, filled):
    return pl.pallas_call(
        routed_kernel,
        out_shape=[
            jax.ShapeDtypeStruct((incoming.shape[1], D), jnp.bfloat16),
            jax.ShapeDtypeStruct(received.shape, jnp.bfloat16),
        ],
        in_specs=[VMEM] * 5,
        out_specs=[VMEM] * 2,
        compiler_params=pltpu.CompilerParams(vmem_limit_bytes=8 * 2**20),
        name="routed",
    )(received, incoming, gain[None], bias[None], filled)


def exchange(parts):
    return [parts[0]] + [swap(part, "dp", index) for index, part in enumerate(parts) if index]


def gather_picked(picked, *beside):
    dp, tensor = lax.axis_size("dp"), lax.axis_size("tensor")
    far = tensor // 2
    rows = picked[0].shape[0]
    width = picked[0].shape[1] - LANES
    own, other = picked[0], picked[1]

    def hop(part, group_bit, place_bit):
        pairs = [
            (g * tensor + t, (g ^ group_bit) * tensor + (t ^ place_bit))
            for g in range(dp)
            for t in range(tensor)
        ]
        return lax.ppermute(part, ("dp", "tensor"), pairs)

    half = rows // 2
    block = jnp.concatenate(
        [own[:half], hop(other[:half], 2, 0), hop(own[half:], 1, 0), hop(other[half:], 3, 0)]
    )
    blocks, beside = gather_blocks(block[:, :width], "tensor", (2,), *beside)
    return blocks, block[:, width:], beside


def on_device(
    tokens,
    ln1_gain,
    ln1_bias,
    qkv_weight,
    out_weight,
    layer_scale,
    segment_ids,
    positions,
    merge_index,
    merge_weight,
    owners,
    ln2_gain,
    ln2_bias,
):
    tensor_count = lax.axis_size("tensor")
    group_count = lax.axis_size("dp")
    place = lax.axis_index("tensor")
    width = out_weight.shape[1]
    merged_count = merge_index.shape[0]
    slots_cap = 2 * merged_count // group_count
    own_slots = group_count * slots_cap

    prepared = prepare(positions, segment_ids, ln1_gain, ln1_bias, tokens)
    token_blocks, prepared = gather_blocks(tokens, "tensor", (2,), *prepared)
    cosine, sine, same, gain, bias, own_tokens = prepared
    attended, residual = attention(
        [own_tokens] + token_blocks[1:], gain, bias, fetch(qkv_weight), cosine, sine, same, width
    )

    if group_count == 4 and 2 * own_slots == HD:
        attended_blocks, _ = gather_blocks(attended, "tensor", ())
        half = tensor_count // 2
        target, out_held, near = targets(owners, group_count, out_weight, attended_blocks[:half])
        hidden_columns, *picked = hidden_of(
            attended_blocks[half:], near, out_held, layer_scale, residual, merge_index.T, target
        )
        arrived_blocks, lines, _ = gather_picked(picked)
        merge_held, near = near_product(arrived_blocks[: tensor_count // 2], merge_weight)
        filled, *outgoing = partial_rows(
            arrived_blocks[tensor_count // 2 :], near, merge_held, lines, group_count, own_slots
        )
        received, line = summed(exchange(outgoing), hidden_columns, tensor_count)
        line = lax.all_to_all(line, "tensor", split_axis=0, concat_axis=0, tiled=True)
        hidden, routed = routed_rows(received, line, ln2_gain, ln2_bias, filled)
        return (hidden, routed)

    attended_blocks, _ = gather_blocks(attended, "tensor", ())
    projected = contract_blocks(attended_blocks, out_weight, place).astype(jnp.bfloat16)
    own_scale = lax.dynamic_slice_in_dim(layer_scale, place * width, width, axis=0)
    hidden_columns = (
        residual.astype(jnp.float32) + own_scale * projected.astype(jnp.float32)
    ).astype(jnp.bfloat16)
    hidden = lax.all_to_all(hidden_columns, "tensor", split_axis=0, concat_axis=1, tiled=True)
    all_hidden = lax.all_gather(hidden, "tensor", axis=0, tiled=True)
    merged = jnp.take(all_hidden, merge_index.reshape(-1), axis=0).reshape(merged_count, 4 * D)
    reduced = jnp.dot(
        merged,
        lax.all_gather(merge_weight, "dp", axis=0, tiled=True),
        preferred_element_type=jnp.float32,
    ).astype(jnp.bfloat16)
    target = owners[:, 0] * slots_cap + slots_of(owners[:, 0], group_count)
    placing = (
        jnp.arange(own_slots, dtype=jnp.int32)[:, None] == target[None, :]
    ).astype(jnp.bfloat16)
    outgoing = jnp.dot(placing, reduced, preferred_element_type=jnp.float32).astype(jnp.bfloat16)
    marks = jnp.sum(placing.astype(jnp.float32), axis=1).astype(jnp.bfloat16)
    incoming, arrived = (
        lax.all_to_all(outgoing, "dp", split_axis=0, concat_axis=0, tiled=True),
        lax.all_to_all(marks, "dp", split_axis=0, concat_axis=0, tiled=True),
    )
    received = incoming.astype(jnp.float32)
    row_total, row_squares = lax.psum(row_stats(received), "tensor")
    routed = (
        finish_norm(received, row_total, row_squares, ln2_gain, ln2_bias)
        * arrived.astype(jnp.float32)[:, None]
    ).astype(jnp.bfloat16)
    return (hidden, routed)


def solution(mesh):
    in_specs = (
        P(("dp", "tensor"), None),
        P(),
        P(),
        P(None, "tensor"),
        P(None, "tensor"),
        P(),
        P("dp"),
        P("dp", None),
        P("dp", None),
        P("dp", "tensor"),
        P("dp", None),
        P("tensor"),
        P("tensor"),
    )
    out_specs = (P(("dp", "tensor"), None), P("dp", "tensor"))
    return jax.shard_map(
        on_device, mesh=mesh, in_specs=in_specs, out_specs=out_specs, check_vma=False
    )
```

```python
import functools
import math

import jax
import jax.numpy as jnp
from jax import lax
from jax.experimental import pallas as pl
from jax.experimental.pallas import tpu as pltpu
from jax.sharding import PartitionSpec as P

D = 4096
HD = 128


def finish_norm(values, row_total, row_squares, gain, bias):
    mean_row = row_total / D
    var_row = row_squares / D - mean_row * mean_row
    return (values - mean_row[:, None]) * lax.rsqrt(var_row[:, None] + 1e-06) * gain + bias


def row_stats(values):
    return (jnp.sum(values, axis=1), jnp.sum(values * values, axis=1))


def swap(block, axis, bit):
    count = lax.axis_size(axis)
    return lax.ppermute(block, axis, [(i, i ^ bit) for i in range(count)])


def gather_blocks(block, axis, early, *beside):
    count = lax.axis_size(axis)
    bit = count // 2
    far = swap(block, axis, bit)
    blocks = {index: swap(block, axis, index) for index in early}
    far, *held = lax.optimization_barrier((far, *blocks.values(), *beside))
    blocks, beside = dict(zip(early, held)), held[len(early) :]
    blocks.update({0: block, bit: far})
    for index in range(1, bit):
        if index not in early:
            blocks[index] = swap(block, axis, index)
    for index in range(1, bit):
        blocks[index ^ bit] = swap(far, axis, index)
    return [blocks[index] for index in range(count)], beside


def contract_blocks(blocks, weight, place):
    depth = blocks[0].shape[1]
    total = None
    for index, block in enumerate(blocks):
        rows = lax.dynamic_slice_in_dim(weight, (place ^ index) * depth, depth, axis=0)
        term = jnp.dot(block, rows, preferred_element_type=jnp.float32)
        total = term if total is None else total + term
    return total


def slots_of(owner_of, group_count):
    one_hot = (owner_of[:, None] == jnp.arange(group_count, dtype=jnp.int32)[None, :]).astype(
        jnp.int32
    )
    before = jnp.cumsum(one_hot, axis=0) - one_hot
    return jnp.sum(before * one_hot, axis=1)


VMEM = pl.BlockSpec(memory_space=pltpu.VMEM)
HBM = pl.BlockSpec(memory_space=pltpu.HBM)
STRIPE = 512
LANES = 128


def column(row, width):
    return jnp.transpose(jnp.broadcast_to(row, (width, row.shape[1])))


def start_stripes(source, held, sems):
    copies = [
        pltpu.make_async_copy(
            source.at[pl.ds(index * STRIPE, STRIPE), :],
            held.at[pl.ds(index * STRIPE, STRIPE), :],
            sems.at[index],
        )
        for index in range(held.shape[0] // STRIPE)
    ]
    for copy in copies:
        copy.start()
    return copies


def fetch_kernel(weight_in, weight, sems):
    copies = start_stripes(weight_in, weight, sems)
    for copy in copies:
        copy.wait()


def fetch(weight):
    return pl.pallas_call(
        fetch_kernel,
        out_shape=jax.ShapeDtypeStruct(weight.shape, weight.dtype),
        in_specs=[HBM],
        out_specs=VMEM,
        scratch_shapes=[pltpu.SemaphoreType.DMA((weight.shape[0] // STRIPE,))],
        compiler_params=pltpu.CompilerParams(vmem_limit_bytes=24 * 2**20),
        cost_estimate=pl.CostEstimate(flops=0, bytes_accessed=weight.size * 4, transcendentals=0),
        name="fetch",
    )(weight)


def prepare_kernel(places, affine, tokens_in, cosine, sine, same, gain, bias, tokens):
    lane = lax.broadcasted_iota(jnp.int32, cosine.shape, 1)
    quarter = HD // 4
    frequency = jnp.exp((lane % quarter).astype(jnp.float32) * (-math.log(100.0) / quarter))
    rows = column(places[0:1, :].astype(jnp.float32), HD)
    columns = column(places[1:2, :].astype(jnp.float32), HD)
    angles = jnp.where(lane < 2 * quarter, rows, columns) * frequency
    cosine[...] = jnp.cos(angles)
    sines = jnp.sin(angles)
    sine[...] = jnp.where((lane & quarter) == 0, -sines, sines)
    ids = places[2:3, :].astype(jnp.float32)
    same[...] = (column(ids, ids.shape[1]) == ids).astype(jnp.float32)
    gain[...] = affine[0:1, :]
    bias[...] = affine[1:2, :]
    tokens[...] = tokens_in[...]


def prepare(positions, segments, gain, bias, tokens):
    seq = segments.shape[0]
    places = jnp.concatenate([positions.T, segments[None]])
    return pl.pallas_call(
        prepare_kernel,
        out_shape=[
            jax.ShapeDtypeStruct((seq, HD), jnp.float32),
            jax.ShapeDtypeStruct((seq, HD), jnp.float32),
            jax.ShapeDtypeStruct((seq, seq), jnp.float32),
            jax.ShapeDtypeStruct((1, D), jnp.float32),
            jax.ShapeDtypeStruct((1, D), jnp.float32),
            jax.ShapeDtypeStruct(tokens.shape, tokens.dtype),
        ],
        in_specs=[VMEM] * 3,
        out_specs=[VMEM] * 6,
        compiler_params=pltpu.CompilerParams(vmem_limit_bytes=24 * 2**20),
        name="prepare",
    )(places, jnp.stack([gain, bias]), tokens)


def attention_kernel(tensor_count, *refs):
    blocks = refs[:tensor_count]
    gain, bias, weight, cosine, sine, same_in, out, residual, normed = refs[tensor_count:]
    place = lax.axis_index("tensor")
    rows, head_count, width = blocks[0].shape[0], out.shape[1] // HD, residual.shape[1]
    lanes = pl.ds(pl.multiple_of(place * width, width), width)
    for index, block in enumerate(blocks):
        values = block[...].astype(jnp.float32)
        center = values - jnp.mean(values, axis=-1, keepdims=True)
        spread = jnp.mean(center * center, axis=-1, keepdims=True)
        value = center * lax.rsqrt(spread + 1e-06) * gain[...] + bias[...]
        at = pl.ds(pl.multiple_of((place ^ index) * rows, rows), rows)
        normed[at, :] = value.astype(jnp.bfloat16)
        residual[at, :] = block[:, lanes]
    same = same_in[...] > 0.5
    low = (lax.broadcasted_iota(jnp.int32, cosine.shape, 1) & (HD // 4)) == 0

    def rotated(part):
        swapped = jnp.where(low, pltpu.roll(part, HD - HD // 4, 1), pltpu.roll(part, HD // 4, 1))
        return (part * cosine[...] + swapped * sine[...]).astype(jnp.bfloat16)

    packed = jnp.dot(normed[...], weight[...], preferred_element_type=jnp.float32)
    parts = [packed[:, at : at + HD] for at in range(0, packed.shape[1], HD)]
    queries, keys = [rotated(part) for part in parts[::3]], [rotated(part) for part in parts[1::3]]
    values = [part.astype(jnp.bfloat16) for part in parts[2::3]]
    scores = [
        lax.dot_general(
            query, key, (((1,), (1,)), ((), ())), preferred_element_type=jnp.float32
        )
        * (1.0 / math.sqrt(HD))
        for query, key in zip(queries, keys)
    ]
    scores = [jnp.where(same, score, -jnp.inf) for score in scores]
    weights = [jnp.exp(score - jnp.max(score, axis=-1, keepdims=True)) for score in scores]
    probs = [
        (part / jnp.sum(part, axis=-1, keepdims=True)).astype(jnp.bfloat16)
        for part in weights
    ]
    for head in range(head_count):
        mixed = jnp.dot(probs[head], values[head], preferred_element_type=jnp.float32)
        out[:, head * HD : (head + 1) * HD] = mixed.astype(jnp.bfloat16)


def attention(blocks, gain, bias, weight, cosine, sine, same, width):
    rows = blocks[0].shape[0]
    seq, columns = rows * len(blocks), weight.shape[1]
    heads = columns // (3 * HD)
    return pl.pallas_call(
        functools.partial(attention_kernel, len(blocks)),
        out_shape=[
            jax.ShapeDtypeStruct((seq, heads * HD), jnp.bfloat16),
            jax.ShapeDtypeStruct((seq, width), jnp.bfloat16),
        ],
        in_specs=[VMEM] * (len(blocks) + 6),
        out_specs=[VMEM] * 2,
        scratch_shapes=[pltpu.VMEM((seq, D), jnp.bfloat16)],
        compiler_params=pltpu.CompilerParams(vmem_limit_bytes=24 * 2**20),
        cost_estimate=pl.CostEstimate(
            flops=2 * seq * D * columns, bytes_accessed=D * columns * 2, transcendentals=0
        ),
        name="attention",
    )(*blocks, gain, bias, weight, cosine, sine, same)


def block_product(blocks, weight, first=0):
    place = lax.axis_index("tensor")
    depth = blocks[0].shape[1]
    total = None
    for index, block in enumerate(blocks, first):
        rows = weight[pl.ds(pl.multiple_of((place ^ index) * depth, depth), depth), :]
        term = jnp.dot(block[...], rows, preferred_element_type=jnp.float32)
        total = term if total is None else total + term
    return total


def hidden_kernel(tensor_count, *refs):
    blocks = refs[:tensor_count]
    near, weight, scale, residual, pick, target, hidden, *picked = refs[tensor_count:]
    place, group = lax.axis_index("tensor"), lax.axis_index("dp")
    width, merged = hidden.shape[1], pick.shape[1]
    own_scale = scale[:, pl.ds(pl.multiple_of(place * width, width), width)]
    projected = near[...] + block_product(blocks, weight, tensor_count)
    projected = projected.astype(jnp.bfloat16).astype(jnp.float32)
    result = (residual[...].astype(jnp.float32) + own_scale * projected).astype(jnp.bfloat16)
    hidden[...] = result
    ids = lax.broadcasted_iota(jnp.int32, (hidden.shape[0], merged), 0)
    lane = lax.broadcasted_iota(jnp.int32, (merged, LANES), 1)
    lines = jnp.broadcast_to(target[...], (merged, LANES))
    for index in range(4):
        chosen = (pick[pl.ds(group ^ index, 1), :] == ids).astype(jnp.bfloat16)
        rows = lax.dot_general(
            chosen, result, (((0,), (0,)), ((), ())), preferred_element_type=jnp.float32
        )
        at = pl.ds(index % 2 * merged, merged)
        picked[index // 2][at, :width] = rows.astype(jnp.bfloat16)
        stands = index % 2 * 2 + index // 2
        line = jnp.where(lane // merged == stands, lines, 0.0)
        picked[index // 2][at, width:] = line.astype(jnp.bfloat16)


def hidden_of(blocks, near, weight, scale, residual, pick, target):
    seq, width = residual.shape
    slots, merged = pick.shape
    return pl.pallas_call(
        functools.partial(hidden_kernel, len(blocks)),
        out_shape=[jax.ShapeDtypeStruct((seq, width), jnp.bfloat16)]
        + [jax.ShapeDtypeStruct((2 * merged, width + LANES), jnp.bfloat16)] * 2,
        in_specs=[VMEM] * (len(blocks) + 6),
        out_specs=[VMEM] * 3,
        compiler_params=pltpu.CompilerParams(vmem_limit_bytes=24 * 2**20),
        cost_estimate=pl.CostEstimate(
            flops=2 * seq * D * width, bytes_accessed=D * width * 2, transcendentals=0
        ),
        name="hidden",
    )(*blocks, near, weight, scale[None], residual, pick, target)


def near_kernel(*refs):
    *blocks, weight_in, weight, total, sems = refs
    copies = start_stripes(weight_in, weight, sems)
    for copy in copies:
        copy.wait()
    total[...] = block_product(blocks, weight)


def near_product(blocks, weight):
    return pl.pallas_call(
        near_kernel,
        out_shape=[
            jax.ShapeDtypeStruct(weight.shape, weight.dtype),
            jax.ShapeDtypeStruct((blocks[0].shape[0], weight.shape[1]), jnp.float32),
        ],
        in_specs=[VMEM] * len(blocks) + [HBM],
        out_specs=[VMEM] * 2,
        scratch_shapes=[pltpu.SemaphoreType.DMA((weight.shape[0] // STRIPE,))],
        compiler_params=pltpu.CompilerParams(vmem_limit_bytes=24 * 2**20),
        cost_estimate=pl.CostEstimate(flops=0, bytes_accessed=weight.size * 4, transcendentals=0),
        name="near",
    )(*blocks, weight)


def targets_kernel(group_count, *refs):
    *blocks, owners, weight_in, target, weight, near, sems = refs
    copies = start_stripes(weight_in, weight, sems)
    total = owners.shape[1]
    merged = total // group_count
    owner = jnp.broadcast_to(owners[...], (8, total))
    before = lax.broadcasted_iota(jnp.int32, (total, total), 0)
    after = lax.broadcasted_iota(jnp.int32, (total, total), 1)
    earlier = ((before < after) & (before // merged == after // merged)).astype(jnp.bfloat16)
    slot = jnp.zeros((8, total), jnp.float32)
    for index in range(group_count):
        named = (owner == index).astype(jnp.float32)
        count = jnp.dot(named.astype(jnp.bfloat16), earlier, preferred_element_type=jnp.float32)
        slot = slot + named * count
    cap = 2 * merged // group_count
    start = (owner * group_count + lax.axis_index("dp")) * cap
    target[...] = (start.astype(jnp.float32) + slot)[0:1]
    for copy in copies:
        copy.wait()
    near[...] = block_product(blocks, weight)


def targets(owners, group_count, weight, blocks):
    total = owners.shape[0] * group_count
    return pl.pallas_call(
        functools.partial(targets_kernel, group_count),
        out_shape=[
            jax.ShapeDtypeStruct((1, total), jnp.float32),
            jax.ShapeDtypeStruct(weight.shape, weight.dtype),
            jax.ShapeDtypeStruct((blocks[0].shape[0], weight.shape[1]), jnp.float32),
        ],
        in_specs=[VMEM] * (len(blocks) + 1) + [HBM],
        out_specs=[VMEM] * 3,
        scratch_shapes=[pltpu.SemaphoreType.DMA((weight.shape[0] // STRIPE,))],
        compiler_params=pltpu.CompilerParams(vmem_limit_bytes=24 * 2**20),
        cost_estimate=pl.CostEstimate(flops=0, bytes_accessed=weight.size * 4, transcendentals=0),
        name="targets",
    )(*blocks, jnp.tile(owners[:, 0], group_count)[None], weight)


def partial_kernel(tensor_count, *refs):
    blocks = refs[:tensor_count]
    near, weight, lines, filled, *outs = refs[tensor_count:]
    group = lax.axis_index("dp")
    partial = (near[...] + block_product(blocks, weight, tensor_count)).astype(jnp.bfloat16)
    cap, merged = outs[0].shape[0], lines.shape[0] // len(outs)
    target = lines[0:16, :].astype(jnp.float32)
    for index in range(1, len(outs)):
        target = target + lines[index * merged : index * merged + 16, :].astype(jnp.float32)
    target = target[0:1]
    slot = lax.broadcasted_iota(jnp.int32, (cap, target.shape[1]), 0)
    for index, out in enumerate(outs):
        placing = (slot + (group ^ index) * cap == target.astype(jnp.int32)).astype(jnp.float32)
        if index == 0:
            used = jnp.sum(placing, axis=1, keepdims=True)
            filled[...] = jnp.broadcast_to(used, filled.shape)
        out[...] = jnp.dot(
            placing.astype(jnp.bfloat16), partial, preferred_element_type=jnp.float32
        ).astype(jnp.bfloat16)


def partial_rows(blocks, near, weight, lines, group_count, own_slots):
    seq, width = blocks[0].shape[0], weight.shape[1]
    return pl.pallas_call(
        functools.partial(partial_kernel, len(blocks)),
        out_shape=[jax.ShapeDtypeStruct((own_slots, LANES), jnp.float32)]
        + [jax.ShapeDtypeStruct((own_slots, width), jnp.bfloat16)] * group_count,
        in_specs=[VMEM] * (len(blocks) + 3),
        out_specs=[VMEM] * (1 + group_count),
        compiler_params=pltpu.CompilerParams(vmem_limit_bytes=24 * 2**20),
        cost_estimate=pl.CostEstimate(
            flops=2 * seq * D * width, bytes_accessed=D * width * 2, transcendentals=0
        ),
        name="partial",
    )(*blocks, near, weight, lines)


def summed_kernel(*refs):
    *parts, hidden, received, outgoing = refs
    total = parts[0][...].astype(jnp.float32)
    for part in parts[1:]:
        total = total + part[...].astype(jnp.float32)
    received[...] = total.astype(jnp.bfloat16)
    total = total.astype(jnp.bfloat16).astype(jnp.float32)
    sums = jnp.sum(total, axis=1, keepdims=True)
    squares = jnp.sum(total * total, axis=1, keepdims=True)
    both = jnp.concatenate([sums, squares], axis=0)
    lanes = both.shape[0]
    count, rows, _ = outgoing.shape
    width = hidden.shape[1]
    value = jnp.transpose(jnp.broadcast_to(both, (lanes, lanes)))[:rows]
    high = value.astype(jnp.bfloat16).astype(jnp.float32)
    rest = value - high
    middle = rest.astype(jnp.bfloat16).astype(jnp.float32)
    low = rest - middle
    row = lax.broadcasted_iota(jnp.int32, value.shape, 0)
    stats = jnp.where(row == 0, high, jnp.where(row == 1, middle, jnp.where(row == 2, low, 0.0)))
    stats = stats.astype(jnp.bfloat16)
    for index in range(count):
        outgoing[index, :, :width] = hidden[index * rows : (index + 1) * rows, :]
        outgoing[index, :, width:] = stats


def summed(parts, hidden, tensor_count):
    own_slots, width = parts[0].shape
    rows = hidden.shape[0] // tensor_count
    return pl.pallas_call(
        summed_kernel,
        out_shape=[
            jax.ShapeDtypeStruct((own_slots, width), jnp.bfloat16),
            jax.ShapeDtypeStruct((tensor_count, rows, width + 2 * own_slots), jnp.bfloat16),
        ],
        in_specs=[VMEM] * (len(parts) + 1),
        out_specs=[VMEM] * 2,
        compiler_params=pltpu.CompilerParams(vmem_limit_bytes=8 * 2**20),
        name="summed",
    )(*parts, hidden)


def routed_kernel(received, incoming, gain, bias, filled, hidden, out):
    own_slots, width = received.shape
    stats = jnp.sum(incoming[:, :, width:].astype(jnp.float32), axis=0)
    line = stats[0:1] + stats[1:2] + stats[2:3]
    totals = column(line, line.shape[1])
    mean_row = totals[:own_slots, 0:1] * (1.0 / D)
    var_row = totals[own_slots:, 0:1] * (1.0 / D) - mean_row * mean_row
    value = (received[...].astype(jnp.float32) - mean_row) * lax.rsqrt(var_row + 1e-06)
    value = (value * gain[...] + bias[...]) * filled[:, 0:1]
    out[...] = value.astype(jnp.bfloat16)
    for index in range(incoming.shape[0]):
        hidden[:, index * width : (index + 1) * width] = incoming[index, :, :width]


def routed_rows(received, incoming, gain, bias, filled):
    return pl.pallas_call(
        routed_kernel,
        out_shape=[
            jax.ShapeDtypeStruct((incoming.shape[1], D), jnp.bfloat16),
            jax.ShapeDtypeStruct(received.shape, jnp.bfloat16),
        ],
        in_specs=[VMEM] * 5,
        out_specs=[VMEM] * 2,
        compiler_params=pltpu.CompilerParams(vmem_limit_bytes=8 * 2**20),
        name="routed",
    )(received, incoming, gain[None], bias[None], filled)


def exchange(parts):
    moved = {index: swap(parts[index], "dp", index) for index in (3, 2, 1)}
    return [parts[0]] + [moved[index] for index in (1, 2, 3)]


def gather_picked(picked, *beside):
    dp, tensor = lax.axis_size("dp"), lax.axis_size("tensor")
    far = tensor // 2
    rows = picked[0].shape[0]
    width = picked[0].shape[1] - LANES
    own, other = picked[0], picked[1]

    def hop(part, group_bit, place_bit):
        pairs = [
            (g * tensor + t, (g ^ group_bit) * tensor + (t ^ place_bit))
            for g in range(dp)
            for t in range(tensor)
        ]
        return lax.ppermute(part, ("dp", "tensor"), pairs)

    half = rows // 2
    block = jnp.concatenate(
        [own[:half], hop(other[:half], 2, 0), hop(own[half:], 1, 0), hop(other[half:], 3, 0)]
    )
    blocks, beside = gather_blocks(block[:, :width], "tensor", (2,), *beside)
    return blocks, block[:, width:], beside


def on_device(
    tokens,
    ln1_gain,
    ln1_bias,
    qkv_weight,
    out_weight,
    layer_scale,
    segment_ids,
    positions,
    merge_index,
    merge_weight,
    owners,
    ln2_gain,
    ln2_bias,
):
    tensor_count = lax.axis_size("tensor")
    group_count = lax.axis_size("dp")
    place = lax.axis_index("tensor")
    width = out_weight.shape[1]
    merged_count = merge_index.shape[0]
    slots_cap = 2 * merged_count // group_count
    own_slots = group_count * slots_cap

    prepared = prepare(positions, segment_ids, ln1_gain, ln1_bias, tokens)
    token_blocks, prepared = gather_blocks(tokens, "tensor", (2,), *prepared)
    cosine, sine, same, gain, bias, own_tokens = prepared
    attended, residual = attention(
        [own_tokens] + token_blocks[1:], gain, bias, fetch(qkv_weight), cosine, sine, same, width
    )

    if group_count == 4 and 2 * own_slots == HD:
        attended_blocks, _ = gather_blocks(attended, "tensor", ())
        half = tensor_count // 2
        target, out_held, near = targets(owners, group_count, out_weight, attended_blocks[:half])
        hidden_columns, *picked = hidden_of(
            attended_blocks[half:], near, out_held, layer_scale, residual, merge_index.T, target
        )
        arrived_blocks, lines, _ = gather_picked(picked)
        merge_held, near = near_product(arrived_blocks[: tensor_count // 2], merge_weight)
        filled, *outgoing = partial_rows(
            arrived_blocks[tensor_count // 2 :], near, merge_held, lines, group_count, own_slots
        )
        received, line = summed(exchange(outgoing), hidden_columns, tensor_count)
        line = lax.all_to_all(line, "tensor", split_axis=0, concat_axis=0, tiled=True)
        hidden, routed = routed_rows(received, line, ln2_gain, ln2_bias, filled)
        return (hidden, routed)

    attended_blocks, _ = gather_blocks(attended, "tensor", ())
    projected = contract_blocks(attended_blocks, out_weight, place).astype(jnp.bfloat16)
    own_scale = lax.dynamic_slice_in_dim(layer_scale, place * width, width, axis=0)
    hidden_columns = (
        residual.astype(jnp.float32) + own_scale * projected.astype(jnp.float32)
    ).astype(jnp.bfloat16)
    hidden = lax.all_to_all(hidden_columns, "tensor", split_axis=0, concat_axis=1, tiled=True)
    all_hidden = lax.all_gather(hidden, "tensor", axis=0, tiled=True)
    merged = jnp.take(all_hidden, merge_index.reshape(-1), axis=0).reshape(merged_count, 4 * D)
    reduced = jnp.dot(
        merged,
        lax.all_gather(merge_weight, "dp", axis=0, tiled=True),
        preferred_element_type=jnp.float32,
    ).astype(jnp.bfloat16)
    target = owners[:, 0] * slots_cap + slots_of(owners[:, 0], group_count)
    placing = (
        jnp.arange(own_slots, dtype=jnp.int32)[:, None] == target[None, :]
    ).astype(jnp.bfloat16)
    outgoing = jnp.dot(placing, reduced, preferred_element_type=jnp.float32).astype(jnp.bfloat16)
    marks = jnp.sum(placing.astype(jnp.float32), axis=1).astype(jnp.bfloat16)
    incoming, arrived = (
        lax.all_to_all(outgoing, "dp", split_axis=0, concat_axis=0, tiled=True),
        lax.all_to_all(marks, "dp", split_axis=0, concat_axis=0, tiled=True),
    )
    received = incoming.astype(jnp.float32)
    row_total, row_squares = lax.psum(row_stats(received), "tensor")
    routed = (
        finish_norm(received, row_total, row_squares, ln2_gain, ln2_bias)
        * arrived.astype(jnp.float32)[:, None]
    ).astype(jnp.bfloat16)
    return (hidden, routed)


def solution(mesh):
    in_specs = (
        P(("dp", "tensor"), None),
        P(),
        P(),
        P(None, "tensor"),
        P(None, "tensor"),
        P(),
        P("dp"),
        P("dp", None),
        P("dp", None),
        P("dp", "tensor"),
        P("dp", None),
        P("tensor"),
        P("tensor"),
    )
    out_specs = (P(("dp", "tensor"), None), P("dp", "tensor"))
    return jax.shard_map(
        on_device, mesh=mesh, in_specs=in_specs, out_specs=out_specs, check_vma=False
    )
```

```python
import functools
import math

import jax
import jax.numpy as jnp
from jax import lax
from jax.experimental import pallas as pl
from jax.experimental.pallas import tpu as pltpu
from jax.sharding import PartitionSpec as P

D = 4096
HD = 128


def finish_norm(values, row_total, row_squares, gain, bias):
    mean_row = row_total / D
    var_row = row_squares / D - mean_row * mean_row
    return (values - mean_row[:, None]) * lax.rsqrt(var_row[:, None] + 1e-06) * gain + bias


def row_stats(values):
    return (jnp.sum(values, axis=1), jnp.sum(values * values, axis=1))


def swap(block, axis, bit):
    count = lax.axis_size(axis)
    return lax.ppermute(block, axis, [(i, i ^ bit) for i in range(count)])


def gather_blocks(block, axis, early, *beside):
    count = lax.axis_size(axis)
    bit = count // 2
    far = swap(block, axis, bit)
    blocks = {index: swap(block, axis, index) for index in early}
    far, *held = lax.optimization_barrier((far, *blocks.values(), *beside))
    blocks, beside = dict(zip(early, held)), held[len(early) :]
    blocks.update({0: block, bit: far})
    for index in range(1, bit):
        if index not in early:
            blocks[index] = swap(block, axis, index)
    for index in range(1, bit):
        blocks[index ^ bit] = swap(far, axis, index)
    return [blocks[index] for index in range(count)], beside


def contract_blocks(blocks, weight, place):
    depth = blocks[0].shape[1]
    total = None
    for index, block in enumerate(blocks):
        rows = lax.dynamic_slice_in_dim(weight, (place ^ index) * depth, depth, axis=0)
        term = jnp.dot(block, rows, preferred_element_type=jnp.float32)
        total = term if total is None else total + term
    return total


def slots_of(owner_of, group_count):
    one_hot = (owner_of[:, None] == jnp.arange(group_count, dtype=jnp.int32)[None, :]).astype(
        jnp.int32
    )
    before = jnp.cumsum(one_hot, axis=0) - one_hot
    return jnp.sum(before * one_hot, axis=1)


VMEM = pl.BlockSpec(memory_space=pltpu.VMEM)
HBM = pl.BlockSpec(memory_space=pltpu.HBM)
STRIPE = 512
LANES = 128


def column(row, width):
    return jnp.transpose(jnp.broadcast_to(row, (width, row.shape[1])))


def start_stripes(source, held, sems):
    copies = [
        pltpu.make_async_copy(
            source.at[pl.ds(index * STRIPE, STRIPE), :],
            held.at[pl.ds(index * STRIPE, STRIPE), :],
            sems.at[index],
        )
        for index in range(held.shape[0] // STRIPE)
    ]
    for copy in copies:
        copy.start()
    return copies


def fetch_kernel(weight_in, weight, sems):
    copies = start_stripes(weight_in, weight, sems)
    for copy in copies:
        copy.wait()


def fetch(weight):
    return pl.pallas_call(
        fetch_kernel,
        out_shape=jax.ShapeDtypeStruct(weight.shape, weight.dtype),
        in_specs=[HBM],
        out_specs=VMEM,
        scratch_shapes=[pltpu.SemaphoreType.DMA((weight.shape[0] // STRIPE,))],
        compiler_params=pltpu.CompilerParams(vmem_limit_bytes=24 * 2**20),
        cost_estimate=pl.CostEstimate(flops=0, bytes_accessed=weight.size * 4, transcendentals=0),
        name="fetch",
    )(weight)


def prepare_kernel(places, affine, tokens_in, cosine, sine, same, gain, bias, tokens):
    lane = lax.broadcasted_iota(jnp.int32, cosine.shape, 1)
    quarter = HD // 4
    frequency = jnp.exp((lane % quarter).astype(jnp.float32) * (-math.log(100.0) / quarter))
    rows = column(places[0:1, :].astype(jnp.float32), HD)
    columns = column(places[1:2, :].astype(jnp.float32), HD)
    angles = jnp.where(lane < 2 * quarter, rows, columns) * frequency
    cosine[...] = jnp.cos(angles)
    sines = jnp.sin(angles)
    sine[...] = jnp.where((lane & quarter) == 0, -sines, sines)
    ids = places[2:3, :].astype(jnp.float32)
    same[...] = (column(ids, ids.shape[1]) == ids).astype(jnp.float32)
    gain[...] = affine[0:1, :]
    bias[...] = affine[1:2, :]
    tokens[...] = tokens_in[...]


def prepare(positions, segments, gain, bias, tokens):
    seq = segments.shape[0]
    places = jnp.concatenate([positions.T, segments[None]])
    return pl.pallas_call(
        prepare_kernel,
        out_shape=[
            jax.ShapeDtypeStruct((seq, HD), jnp.float32),
            jax.ShapeDtypeStruct((seq, HD), jnp.float32),
            jax.ShapeDtypeStruct((seq, seq), jnp.float32),
            jax.ShapeDtypeStruct((1, D), jnp.float32),
            jax.ShapeDtypeStruct((1, D), jnp.float32),
            jax.ShapeDtypeStruct(tokens.shape, tokens.dtype),
        ],
        in_specs=[VMEM] * 3,
        out_specs=[VMEM] * 6,
        compiler_params=pltpu.CompilerParams(vmem_limit_bytes=24 * 2**20),
        name="prepare",
    )(places, jnp.stack([gain, bias]), tokens)


def normalized(block, gain, bias):
    values = block[...].astype(jnp.float32)
    center = values - jnp.mean(values, axis=-1, keepdims=True)
    spread = jnp.mean(center * center, axis=-1, keepdims=True)
    value = center * lax.rsqrt(spread + 1e-06) * gain[...] + bias[...]
    return value.astype(jnp.bfloat16)


def normalize_kernel(*refs):
    *blocks, gain, bias, out = refs
    rows = blocks[0].shape[0]
    for index, block in enumerate(blocks):
        out[index * rows : (index + 1) * rows, :] = normalized(block, gain, bias)


def normalize(blocks, gain, bias):
    return pl.pallas_call(
        normalize_kernel,
        out_shape=jax.ShapeDtypeStruct((len(blocks) * blocks[0].shape[0], D), jnp.bfloat16),
        in_specs=[VMEM] * (len(blocks) + 2),
        out_specs=VMEM,
        compiler_params=pltpu.CompilerParams(vmem_limit_bytes=24 * 2**20),
        name="normalize",
    )(*blocks, gain, bias)


def attention_kernel(tensor_count, *refs):
    blocks = refs[:tensor_count]
    near, gain, bias, weight, cosine, sine, same_in, out, residual, normed = refs[tensor_count:]
    place = lax.axis_index("tensor")
    rows, head_count, width = blocks[0].shape[0], out.shape[1] // HD, residual.shape[1]
    lanes = pl.ds(pl.multiple_of(place * width, width), width)
    for index, block in enumerate(blocks):
        at = pl.ds(pl.multiple_of((place ^ index) * rows, rows), rows)
        if index < tensor_count // 2:
            normed[at, :] = near[index * rows : (index + 1) * rows, :]
        else:
            normed[at, :] = normalized(block, gain, bias)
        residual[at, :] = block[:, lanes]
    same = same_in[...] > 0.5
    low = (lax.broadcasted_iota(jnp.int32, cosine.shape, 1) & (HD // 4)) == 0

    def rotated(part):
        swapped = jnp.where(low, pltpu.roll(part, HD - HD // 4, 1), pltpu.roll(part, HD // 4, 1))
        return (part * cosine[...] + swapped * sine[...]).astype(jnp.bfloat16)

    packed = jnp.dot(normed[...], weight[...], preferred_element_type=jnp.float32)
    parts = [packed[:, at : at + HD] for at in range(0, packed.shape[1], HD)]
    queries, keys = [rotated(part) for part in parts[::3]], [rotated(part) for part in parts[1::3]]
    values = [part.astype(jnp.bfloat16) for part in parts[2::3]]
    scores = [
        lax.dot_general(
            query, key, (((1,), (1,)), ((), ())), preferred_element_type=jnp.float32
        )
        * (1.0 / math.sqrt(HD))
        for query, key in zip(queries, keys)
    ]
    scores = [jnp.where(same, score, -jnp.inf) for score in scores]
    weights = [jnp.exp(score - jnp.max(score, axis=-1, keepdims=True)) for score in scores]
    probs = [
        (part / jnp.sum(part, axis=-1, keepdims=True)).astype(jnp.bfloat16)
        for part in weights
    ]
    for head in range(head_count):
        mixed = jnp.dot(probs[head], values[head], preferred_element_type=jnp.float32)
        out[:, head * HD : (head + 1) * HD] = mixed.astype(jnp.bfloat16)


def attention(blocks, near, gain, bias, weight, cosine, sine, same, width):
    rows = blocks[0].shape[0]
    seq, columns = rows * len(blocks), weight.shape[1]
    heads = columns // (3 * HD)
    return pl.pallas_call(
        functools.partial(attention_kernel, len(blocks)),
        out_shape=[
            jax.ShapeDtypeStruct((seq, heads * HD), jnp.bfloat16),
            jax.ShapeDtypeStruct((seq, width), jnp.bfloat16),
        ],
        in_specs=[VMEM] * (len(blocks) + 7),
        out_specs=[VMEM] * 2,
        scratch_shapes=[pltpu.VMEM((seq, D), jnp.bfloat16)],
        compiler_params=pltpu.CompilerParams(vmem_limit_bytes=24 * 2**20),
        cost_estimate=pl.CostEstimate(
            flops=2 * seq * D * columns, bytes_accessed=D * columns * 2, transcendentals=0
        ),
        name="attention",
    )(*blocks, near, gain, bias, weight, cosine, sine, same)


def block_product(blocks, weight, first=0):
    place = lax.axis_index("tensor")
    depth = blocks[0].shape[1]
    total = None
    for index, block in enumerate(blocks, first):
        rows = weight[pl.ds(pl.multiple_of((place ^ index) * depth, depth), depth), :]
        term = jnp.dot(block[...], rows, preferred_element_type=jnp.float32)
        total = term if total is None else total + term
    return total


def hidden_kernel(tensor_count, *refs):
    blocks = refs[:tensor_count]
    near, weight, scale, residual, pick, target, hidden, *picked = refs[tensor_count:]
    place, group = lax.axis_index("tensor"), lax.axis_index("dp")
    width, merged = hidden.shape[1], pick.shape[1]
    own_scale = scale[:, pl.ds(pl.multiple_of(place * width, width), width)]
    projected = near[...] + block_product(blocks, weight, tensor_count)
    projected = projected.astype(jnp.bfloat16).astype(jnp.float32)
    result = (residual[...].astype(jnp.float32) + own_scale * projected).astype(jnp.bfloat16)
    hidden[...] = result
    ids = lax.broadcasted_iota(jnp.int32, (hidden.shape[0], merged), 0)
    lane = lax.broadcasted_iota(jnp.int32, (merged, LANES), 1)
    lines = jnp.broadcast_to(target[...], (merged, LANES))
    for index in range(4):
        chosen = (pick[pl.ds(group ^ index, 1), :] == ids).astype(jnp.bfloat16)
        rows = lax.dot_general(
            chosen, result, (((0,), (0,)), ((), ())), preferred_element_type=jnp.float32
        )
        at = pl.ds(index % 2 * merged, merged)
        picked[index // 2][at, :width] = rows.astype(jnp.bfloat16)
        stands = index % 2 * 2 + index // 2
        line = jnp.where(lane // merged == stands, lines, 0.0)
        picked[index // 2][at, width:] = line.astype(jnp.bfloat16)


def hidden_of(blocks, near, weight, scale, residual, pick, target):
    seq, width = residual.shape
    slots, merged = pick.shape
    return pl.pallas_call(
        functools.partial(hidden_kernel, len(blocks)),
        out_shape=[jax.ShapeDtypeStruct((seq, width), jnp.bfloat16)]
        + [jax.ShapeDtypeStruct((2 * merged, width + LANES), jnp.bfloat16)] * 2,
        in_specs=[VMEM] * (len(blocks) + 6),
        out_specs=[VMEM] * 3,
        compiler_params=pltpu.CompilerParams(vmem_limit_bytes=24 * 2**20),
        cost_estimate=pl.CostEstimate(
            flops=2 * seq * D * width, bytes_accessed=D * width * 2, transcendentals=0
        ),
        name="hidden",
    )(*blocks, near, weight, scale[None], residual, pick, target)


def near_kernel(*refs):
    *blocks, weight_in, weight, total, sems = refs
    copies = start_stripes(weight_in, weight, sems)
    for copy in copies:
        copy.wait()
    total[...] = block_product(blocks, weight)


def near_product(blocks, weight):
    return pl.pallas_call(
        near_kernel,
        out_shape=[
            jax.ShapeDtypeStruct(weight.shape, weight.dtype),
            jax.ShapeDtypeStruct((blocks[0].shape[0], weight.shape[1]), jnp.float32),
        ],
        in_specs=[VMEM] * len(blocks) + [HBM],
        out_specs=[VMEM] * 2,
        scratch_shapes=[pltpu.SemaphoreType.DMA((weight.shape[0] // STRIPE,))],
        compiler_params=pltpu.CompilerParams(vmem_limit_bytes=24 * 2**20),
        cost_estimate=pl.CostEstimate(flops=0, bytes_accessed=weight.size * 4, transcendentals=0),
        name="near",
    )(*blocks, weight)


def targets_kernel(group_count, *refs):
    *blocks, owners, weight_in, target, weight, near, sems = refs
    copies = start_stripes(weight_in, weight, sems)
    total = owners.shape[1]
    merged = total // group_count
    owner = jnp.broadcast_to(owners[...], (8, total))
    before = lax.broadcasted_iota(jnp.int32, (total, total), 0)
    after = lax.broadcasted_iota(jnp.int32, (total, total), 1)
    earlier = ((before < after) & (before // merged == after // merged)).astype(jnp.bfloat16)
    slot = jnp.zeros((8, total), jnp.float32)
    for index in range(group_count):
        named = (owner == index).astype(jnp.float32)
        count = jnp.dot(named.astype(jnp.bfloat16), earlier, preferred_element_type=jnp.float32)
        slot = slot + named * count
    cap = 2 * merged // group_count
    start = (owner * group_count + lax.axis_index("dp")) * cap
    target[...] = (start.astype(jnp.float32) + slot)[0:1]
    for copy in copies:
        copy.wait()
    near[...] = block_product(blocks, weight)


def targets(owners, group_count, weight, blocks):
    total = owners.shape[0] * group_count
    return pl.pallas_call(
        functools.partial(targets_kernel, group_count),
        out_shape=[
            jax.ShapeDtypeStruct((1, total), jnp.float32),
            jax.ShapeDtypeStruct(weight.shape, weight.dtype),
            jax.ShapeDtypeStruct((blocks[0].shape[0], weight.shape[1]), jnp.float32),
        ],
        in_specs=[VMEM] * (len(blocks) + 1) + [HBM],
        out_specs=[VMEM] * 3,
        scratch_shapes=[pltpu.SemaphoreType.DMA((weight.shape[0] // STRIPE,))],
        compiler_params=pltpu.CompilerParams(vmem_limit_bytes=24 * 2**20),
        cost_estimate=pl.CostEstimate(flops=0, bytes_accessed=weight.size * 4, transcendentals=0),
        name="targets",
    )(*blocks, jnp.tile(owners[:, 0], group_count)[None], weight)


def partial_kernel(tensor_count, *refs):
    blocks = refs[:tensor_count]
    near, weight, lines, filled, *outs = refs[tensor_count:]
    group = lax.axis_index("dp")
    partial = (near[...] + block_product(blocks, weight, tensor_count)).astype(jnp.bfloat16)
    cap, merged = outs[0].shape[0], lines.shape[0] // len(outs)
    target = lines[0:16, :].astype(jnp.float32)
    for index in range(1, len(outs)):
        target = target + lines[index * merged : index * merged + 16, :].astype(jnp.float32)
    target = target[0:1]
    slot = lax.broadcasted_iota(jnp.int32, (cap, target.shape[1]), 0)
    for index, out in enumerate(outs):
        placing = (slot + (group ^ index) * cap == target.astype(jnp.int32)).astype(jnp.float32)
        if index == 0:
            used = jnp.sum(placing, axis=1, keepdims=True)
            filled[...] = jnp.broadcast_to(used, filled.shape)
        out[...] = jnp.dot(
            placing.astype(jnp.bfloat16), partial, preferred_element_type=jnp.float32
        ).astype(jnp.bfloat16)


def partial_rows(blocks, near, weight, lines, group_count, own_slots):
    seq, width = blocks[0].shape[0], weight.shape[1]
    return pl.pallas_call(
        functools.partial(partial_kernel, len(blocks)),
        out_shape=[jax.ShapeDtypeStruct((own_slots, LANES), jnp.float32)]
        + [jax.ShapeDtypeStruct((own_slots, width), jnp.bfloat16)] * group_count,
        in_specs=[VMEM] * (len(blocks) + 3),
        out_specs=[VMEM] * (1 + group_count),
        compiler_params=pltpu.CompilerParams(vmem_limit_bytes=24 * 2**20),
        cost_estimate=pl.CostEstimate(
            flops=2 * seq * D * width, bytes_accessed=D * width * 2, transcendentals=0
        ),
        name="partial",
    )(*blocks, near, weight, lines)


def summed_kernel(*refs):
    *parts, hidden, received, outgoing = refs
    total = parts[0][...].astype(jnp.float32)
    for part in parts[1:]:
        total = total + part[...].astype(jnp.float32)
    received[...] = total.astype(jnp.bfloat16)
    total = total.astype(jnp.bfloat16).astype(jnp.float32)
    sums = jnp.sum(total, axis=1, keepdims=True)
    squares = jnp.sum(total * total, axis=1, keepdims=True)
    both = jnp.concatenate([sums, squares], axis=0)
    lanes = both.shape[0]
    count, rows, _ = outgoing.shape
    width = hidden.shape[1]
    value = jnp.transpose(jnp.broadcast_to(both, (lanes, lanes)))[:rows]
    high = value.astype(jnp.bfloat16).astype(jnp.float32)
    rest = value - high
    middle = rest.astype(jnp.bfloat16).astype(jnp.float32)
    low = rest - middle
    row = lax.broadcasted_iota(jnp.int32, value.shape, 0)
    stats = jnp.where(row == 0, high, jnp.where(row == 1, middle, jnp.where(row == 2, low, 0.0)))
    stats = stats.astype(jnp.bfloat16)
    for index in range(count):
        outgoing[index, :, :width] = hidden[index * rows : (index + 1) * rows, :]
        outgoing[index, :, width:] = stats


def summed(parts, hidden, tensor_count):
    own_slots, width = parts[0].shape
    rows = hidden.shape[0] // tensor_count
    return pl.pallas_call(
        summed_kernel,
        out_shape=[
            jax.ShapeDtypeStruct((own_slots, width), jnp.bfloat16),
            jax.ShapeDtypeStruct((tensor_count, rows, width + 2 * own_slots), jnp.bfloat16),
        ],
        in_specs=[VMEM] * (len(parts) + 1),
        out_specs=[VMEM] * 2,
        compiler_params=pltpu.CompilerParams(vmem_limit_bytes=8 * 2**20),
        name="summed",
    )(*parts, hidden)


def routed_kernel(received, incoming, gain, bias, filled, hidden, out):
    own_slots, width = received.shape
    stats = jnp.sum(incoming[:, :, width:].astype(jnp.float32), axis=0)
    line = stats[0:1] + stats[1:2] + stats[2:3]
    totals = column(line, line.shape[1])
    mean_row = totals[:own_slots, 0:1] * (1.0 / D)
    var_row = totals[own_slots:, 0:1] * (1.0 / D) - mean_row * mean_row
    value = (received[...].astype(jnp.float32) - mean_row) * lax.rsqrt(var_row + 1e-06)
    value = (value * gain[...] + bias[...]) * filled[:, 0:1]
    out[...] = value.astype(jnp.bfloat16)
    for index in range(incoming.shape[0]):
        hidden[:, index * width : (index + 1) * width] = incoming[index, :, :width]


def routed_rows(received, incoming, gain, bias, filled):
    return pl.pallas_call(
        routed_kernel,
        out_shape=[
            jax.ShapeDtypeStruct((incoming.shape[1], D), jnp.bfloat16),
            jax.ShapeDtypeStruct(received.shape, jnp.bfloat16),
        ],
        in_specs=[VMEM] * 5,
        out_specs=[VMEM] * 2,
        compiler_params=pltpu.CompilerParams(vmem_limit_bytes=8 * 2**20),
        name="routed",
    )(received, incoming, gain[None], bias[None], filled)


def exchange(parts):
    moved = {index: swap(parts[index], "dp", index) for index in (3, 2, 1)}
    return [parts[0]] + [moved[index] for index in (1, 2, 3)]


def gather_picked(picked, *beside):
    dp, tensor = lax.axis_size("dp"), lax.axis_size("tensor")
    far = tensor // 2
    rows = picked[0].shape[0]
    width = picked[0].shape[1] - LANES
    own, other = picked[0], picked[1]

    def hop(part, group_bit, place_bit):
        pairs = [
            (g * tensor + t, (g ^ group_bit) * tensor + (t ^ place_bit))
            for g in range(dp)
            for t in range(tensor)
        ]
        return lax.ppermute(part, ("dp", "tensor"), pairs)

    half = rows // 2
    block = jnp.concatenate(
        [own[:half], hop(other[:half], 2, 0), hop(own[half:], 1, 0), hop(other[half:], 3, 0)]
    )
    blocks, beside = gather_blocks(block[:, :width], "tensor", (2,), *beside)
    return blocks, block[:, width:], beside


def on_device(
    tokens,
    ln1_gain,
    ln1_bias,
    qkv_weight,
    out_weight,
    layer_scale,
    segment_ids,
    positions,
    merge_index,
    merge_weight,
    owners,
    ln2_gain,
    ln2_bias,
):
    tensor_count = lax.axis_size("tensor")
    group_count = lax.axis_size("dp")
    place = lax.axis_index("tensor")
    width = out_weight.shape[1]
    merged_count = merge_index.shape[0]
    slots_cap = 2 * merged_count // group_count
    own_slots = group_count * slots_cap

    prepared = prepare(positions, segment_ids, ln1_gain, ln1_bias, tokens)
    token_blocks, prepared = gather_blocks(tokens, "tensor", (2,), *prepared)
    cosine, sine, same, gain, bias, own_tokens = prepared
    token_blocks[0] = own_tokens
    near = normalize(token_blocks[: tensor_count // 2], gain, bias)
    attended, residual = attention(
        token_blocks, near, gain, bias, fetch(qkv_weight), cosine, sine, same, width
    )

    if group_count == 4 and 2 * own_slots == HD:
        attended_blocks, _ = gather_blocks(attended, "tensor", ())
        half = tensor_count // 2
        target, out_held, near = targets(owners, group_count, out_weight, attended_blocks[:half])
        hidden_columns, *picked = hidden_of(
            attended_blocks[half:], near, out_held, layer_scale, residual, merge_index.T, target
        )
        arrived_blocks, lines, _ = gather_picked(picked)
        merge_held, near = near_product(arrived_blocks[: tensor_count // 2], merge_weight)
        filled, *outgoing = partial_rows(
            arrived_blocks[tensor_count // 2 :], near, merge_held, lines, group_count, own_slots
        )
        received, line = summed(exchange(outgoing), hidden_columns, tensor_count)
        line = lax.all_to_all(line, "tensor", split_axis=0, concat_axis=0, tiled=True)
        hidden, routed = routed_rows(received, line, ln2_gain, ln2_bias, filled)
        return (hidden, routed)

    attended_blocks, _ = gather_blocks(attended, "tensor", ())
    projected = contract_blocks(attended_blocks, out_weight, place).astype(jnp.bfloat16)
    own_scale = lax.dynamic_slice_in_dim(layer_scale, place * width, width, axis=0)
    hidden_columns = (
        residual.astype(jnp.float32) + own_scale * projected.astype(jnp.float32)
    ).astype(jnp.bfloat16)
    hidden = lax.all_to_all(hidden_columns, "tensor", split_axis=0, concat_axis=1, tiled=True)
    all_hidden = lax.all_gather(hidden, "tensor", axis=0, tiled=True)
    merged = jnp.take(all_hidden, merge_index.reshape(-1), axis=0).reshape(merged_count, 4 * D)
    reduced = jnp.dot(
        merged,
        lax.all_gather(merge_weight, "dp", axis=0, tiled=True),
        preferred_element_type=jnp.float32,
    ).astype(jnp.bfloat16)
    target = owners[:, 0] * slots_cap + slots_of(owners[:, 0], group_count)
    placing = (
        jnp.arange(own_slots, dtype=jnp.int32)[:, None] == target[None, :]
    ).astype(jnp.bfloat16)
    outgoing = jnp.dot(placing, reduced, preferred_element_type=jnp.float32).astype(jnp.bfloat16)
    marks = jnp.sum(placing.astype(jnp.float32), axis=1).astype(jnp.bfloat16)
    incoming, arrived = (
        lax.all_to_all(outgoing, "dp", split_axis=0, concat_axis=0, tiled=True),
        lax.all_to_all(marks, "dp", split_axis=0, concat_axis=0, tiled=True),
    )
    received = incoming.astype(jnp.float32)
    row_total, row_squares = lax.psum(row_stats(received), "tensor")
    routed = (
        finish_norm(received, row_total, row_squares, ln2_gain, ln2_bias)
        * arrived.astype(jnp.float32)[:, None]
    ).astype(jnp.bfloat16)
    return (hidden, routed)


def solution(mesh):
    in_specs = (
        P(("dp", "tensor"), None),
        P(),
        P(),
        P(None, "tensor"),
        P(None, "tensor"),
        P(),
        P("dp"),
        P("dp", None),
        P("dp", None),
        P("dp", "tensor"),
        P("dp", None),
        P("tensor"),
        P("tensor"),
    )
    out_specs = (P(("dp", "tensor"), None), P("dp", "tensor"))
    return jax.shard_map(
        on_device, mesh=mesh, in_specs=in_specs, out_specs=out_specs, check_vma=False
    )
```
